128 devices in a mesh: ctx: 64 (over z, x, y), head: 2 (over core).
Axes of the slice: x: 4, y: 4, z: 4, core: 2. Of those that a mesh axis runs over, the one named last changes fastest.
Arguments:
- teacher_query: bfloat16 [14336, 5120], P('ctx', 'head'), may hold values from -25 to 25
- teacher_key: bfloat16 [14336, 5120], P('ctx', 'head'), may hold values from -25 to 25
- student_hidden: bfloat16 [14336, 2048], P('ctx'), may hold values from -25 to 25
- w_query: bfloat16 [2048, 2048], P(None, 'head'), may hold values from -0.125 to 0.125
- w_key: bfloat16 [2048, 2048], P(None, 'head'), may hold values from -0.125 to 0.125
- segment_ids: int32 [14336], replicated, may hold values from 0 to 3, never falling along the last dimension, each value on 1 to 7168 neighbouring positions
- block_mask: int32 [64, 7], P('ctx'), may hold values 0 or 1
Outputs:
- grad_hidden: bfloat16 [14336, 2048], P('ctx', 'head')
The draws below stay inside these ranges and needn't reach their ends.
Inputs may be any that keep to these rules, and one draw needn't show every extreme that they name: `segment_ids`: document numbers never fall along the row; no document is longer than 7168 tokens and one is exactly that long.
All inputs are finite; a program needn't handle non-finite values. No bound on the sum of `block_mask` on one device may be relied on, other than what follows from the above.
Results may differ from the reference program's by a relative error of at most 0.0085.
Values may be sent and summed in bfloat16 or wider, within the bound.
No kernel may reach another device: no remote copies, remote signals or barrier semaphores. Data moves between devices by JAX's collectives and lax.ppermute only.
A program may use at most 256 MiB of HBM per device.

```python
import math
import jax
import jax.numpy as jnp
import numpy as np
from jax import lax

DT = 5120
DS = 2048
HEADS = 64
TOK_DEV = 224
DOCS = 4
REACH = 8
NBLOCKS = 64
TOKENS = 14336


def draw_teacher_query(key, part):
    key = jax.random.fold_in(key, 11)
    first_key = jax.random.fold_in(key, 0)
    values = jnp.clip(0.8 * jax.random.normal(first_key, (TOKENS, DT), jnp.float32), -4.0, 4.0)
    return values.astype(jnp.bfloat16)


def draw_teacher_key(key, part):
    key = jax.random.fold_in(key, 23)
    first_key = jax.random.fold_in(key, 0)
    values = jnp.clip(0.8 * jax.random.normal(first_key, (TOKENS, DT), jnp.float32), -4.0, 4.0)
    return values.astype(jnp.bfloat16)


def draw_student_hidden(key, part):
    key = jax.random.fold_in(key, 37)
    first_key = jax.random.fold_in(key, 0)
    values = jnp.clip(jax.random.normal(first_key, (TOKENS, DS), jnp.float32), -5.0, 5.0)
    return values.astype(jnp.bfloat16)


def touch_ends(array, stream_key, low, high):
    index_at = [jax.random.randint(jax.random.fold_in(stream_key, axis), (), 0, length) for axis, length in enumerate(array.shape)]
    longest = array.shape.index(max(array.shape))
    next_to = index_at[:longest] + [(index_at[longest] + 1) % array.shape[longest]] + index_at[longest + 1:]
    return array.at[tuple(index_at)].set(low).at[tuple(next_to)].set(high)


def level_of(rng, shape, pieces, least, high):
    level = 1.0
    for dim, shards_of in pieces:
        steps = jax.random.uniform(jax.random.fold_in(jax.random.fold_in(rng, 6), dim), (shards_of,), jnp.float32, least / len(pieces), high / len(pieces))
        level = level * jnp.repeat(jnp.exp(steps), shape[dim] // shards_of).reshape((-1,) + (1,) * (len(shape) - 1 - dim))
    return level


def length_profile(number_of, total, bound, lean):
    weights = [(1 << 20) // math.isqrt(rank ** lean) + 1 for rank in range(2, number_of + 1)]
    rest, given = total - bound - (number_of - 1), [1] * (number_of - 1)
    while rest > 0:
        free = [i for i in range(number_of - 1) if given[i] < bound]
        pool, budget = sum([weights[i] for i in free]), rest
        for i in free:
            addition = min(bound - given[i], max(1, budget * weights[i] // pool), rest)
            given[i] = given[i] + addition
            rest = rest - addition
    return np.array([bound] + given)


def ragged(stream_key, count, total, bound, lean):
    if count == 2:
        one = jax.random.randint(stream_key, (), max(1, total - bound), min(bound, total - 1) + 1)
        return jnp.stack([one, total - one])
    sizes = jnp.asarray(length_profile(count, total, bound, lean), jnp.int32)
    twos = (count - 1) // 2
    donor, taker = sizes[1:1 + 2 * twos:2], sizes[2:2 + 2 * twos:2]
    room = jnp.minimum(donor - 1, bound - taker)
    shifted = jax.random.randint(jax.random.fold_in(stream_key, 1), (twos,), 0, 1 << 20) % (room + 1)
    sizes = sizes.at[1:1 + 2 * twos:2].set(donor - shifted).at[2:2 + 2 * twos:2].set(taker + shifted)
    return sizes[jax.random.permutation(jax.random.fold_in(stream_key, 2), count)]


def centred(stream_key, shape, scale, limit, pieces=(), held_as=jnp.bfloat16):
    level = level_of(stream_key, shape, pieces, -0.22, 0.18) if pieces else 1.0
    array = jax.random.normal(stream_key, shape, jnp.float32) * scale * level
    return jnp.minimum(jnp.maximum(array, -limit), limit).astype(held_as)


def setup_inputs(seed: int = 0) -> dict:
    keys = jax.random.split(jax.random.key(seed), 8)
    return {
        "teacher_query": draw_teacher_query(jax.random.fold_in(keys[7], 71), 0),
        "teacher_key": draw_teacher_key(jax.random.fold_in(keys[7], 71), 0),
        "student_hidden": draw_student_hidden(jax.random.fold_in(keys[7], 71), 0),
        "w_query": centred(keys[3], (DS, DS), DS ** -0.5, 0.125, ((1, 2),)),
        "w_key": centred(keys[4], (DS, DS), DS ** -0.5, 0.125, ((1, 2),)),
        "segment_ids": jnp.searchsorted(jnp.cumsum(ragged(keys[5], DOCS, TOKENS, TOKENS // 2, 0)), jnp.arange(TOKENS), side="right").astype(jnp.int32),
        "block_mask": touch_ends((jax.random.randint(keys[6], (NBLOCKS, REACH - 1), 0, 3) < 2).astype(jnp.int32), jax.random.fold_in(keys[6], 1), 0, 1),
    }


def relation_probs(scores, visible):
    masked = jnp.where(visible, scores, -jnp.inf)
    highest = lax.optimization_barrier(jnp.max(masked, axis=-1, keepdims=True))
    weights = jnp.exp(masked - highest)
    return weights / lax.optimization_barrier(jnp.sum(weights, axis=-1, keepdims=True))

def visibility(block_id, row_count, reach, segment_ids, mask_row):
    margin = (reach - 1) * row_count
    window_rows = reach * row_count
    first_row = block_id * row_count
    key_places = first_row - margin + jnp.arange(window_rows, dtype=jnp.int32)
    query_places = first_row + jnp.arange(row_count, dtype=jnp.int32)
    padded_segments = jnp.concatenate([jnp.full((margin,), -1, jnp.int32), segment_ids.astype(jnp.int32)])
    key_segments = lax.dynamic_slice_in_dim(padded_segments, first_row, window_rows)
    query_segments = lax.dynamic_slice_in_dim(padded_segments, first_row + margin, row_count)
    opened = jnp.concatenate([jnp.ones((1,), jnp.int32), mask_row.astype(jnp.int32)])
    block_open = jnp.repeat(opened[::-1], row_count)
    return (key_places[None, :] >= 0) & (key_places[None, :] <= query_places[:, None]) & (key_segments[None, :] == query_segments[:, None]) & (block_open[None, :] == 1)

def relation_terms(teacher_rows, teacher_window, student_rows, student_window, visible):
    width_t = DT // HEADS
    width_s = DS // HEADS
    query_count = teacher_rows.shape[0]
    key_count = teacher_window.shape[0]
    teacher_a = teacher_rows.astype(jnp.float32).reshape(query_count, -1, width_t)
    teacher_b = teacher_window.astype(jnp.float32).reshape(key_count, -1, width_t)
    student_a = student_rows.astype(jnp.float32).reshape(query_count, -1, width_s)
    student_b = student_window.astype(jnp.float32).reshape(key_count, -1, width_s)
    teacher_scores = jnp.einsum('qhd,khd->hqk', teacher_a, teacher_b) * (1.0 / math.sqrt(width_t))
    student_scores = jnp.einsum('qhd,khd->hqk', student_a, student_b) * (1.0 / math.sqrt(width_s))
    shown = visible[None]
    difference = relation_probs(student_scores, shown) - relation_probs(teacher_scores, shown)
    coupling = jnp.where(shown, difference * (1.0 / math.sqrt(width_s)), 0.0).astype(jnp.bfloat16)
    coupling = coupling.astype(jnp.float32)
    query_term = jnp.einsum('hqk,khd->qhd', coupling, student_b).reshape(query_count, -1)
    key_term = jnp.einsum('hqk,qhd->khd', coupling, student_a).reshape(key_count, -1)
    return (query_term, key_term)

def reference(teacher_query, teacher_key, student_hidden, w_query, w_key, segment_ids, block_mask):
    student_query = jnp.dot(student_hidden, w_query, preferred_element_type=jnp.float32).astype(jnp.bfloat16)
    student_key = jnp.dot(student_hidden, w_key, preferred_element_type=jnp.float32).astype(jnp.bfloat16)
    margin = (REACH - 1) * TOK_DEV
    window_rows = REACH * TOK_DEV

    def front(values):
        return jnp.concatenate([jnp.zeros((margin, values.shape[1]), values.dtype), values], axis=0)
    padded = [front(values) for values in (teacher_query, teacher_key, student_query, student_key)]

    def block_step(totals, block_id):
        first_row = block_id * TOK_DEV
        windows = [lax.dynamic_slice_in_dim(values, first_row, window_rows, 0) for values in padded]
        current = [lax.dynamic_slice_in_dim(values, first_row + margin, TOK_DEV, 0) for values in padded]
        mask_row = lax.dynamic_index_in_dim(block_mask, block_id, 0, keepdims=False)
        visible = visibility(block_id, TOK_DEV, REACH, segment_ids, mask_row)
        updated = []
        for member in range(2):
            query_term, key_term = relation_terms(current[member], windows[member], current[member + 2], windows[member + 2], visible)
            running = totals[member]
            running = lax.dynamic_update_slice_in_dim(running, lax.dynamic_slice_in_dim(running, first_row, window_rows, 0) + key_term, first_row, 0)
            running = lax.dynamic_update_slice_in_dim(running, lax.dynamic_slice_in_dim(running, first_row + margin, TOK_DEV, 0) + query_term, first_row + margin, 0)
            updated.append(running)
        return ((updated[0], updated[1]), None)
    zeros_start = jnp.zeros((margin + TOKENS, DS), jnp.float32)
    totals, _ = lax.scan(block_step, (zeros_start, zeros_start), jnp.arange(NBLOCKS, dtype=jnp.int32))
    grad_query = totals[0][margin:].astype(jnp.bfloat16)
    grad_key = totals[1][margin:].astype(jnp.bfloat16)
    combined = jnp.dot(grad_query, w_query.T, preferred_element_type=jnp.float32) + jnp.dot(grad_key, w_key.T, preferred_element_type=jnp.float32)
    return combined.astype(jnp.bfloat16)
```

```python
import functools
import math

import jax
import jax.numpy as jnp
from jax import lax
from jax.experimental import pallas as pl
from jax.experimental.pallas import tpu as pltpu
from jax.sharding import PartitionSpec as P

DT = 5120
DS = 2048
HEADS = 64
REACH = 8
WT = DT // HEADS
WS = DS // HEADS
SEG0 = WT + WS
ONE0 = SEG0 + 4
MASK0 = ONE0 + 3
SLAB = 128
PACK = 8
LAG = 14
UNROLL = 4
SLOTS = 8
LIST = 640
HIDDEN = 1e30
LOG2E = math.log2(math.e)
SCALE_T = LOG2E / math.sqrt(WT)
SCALE_S = LOG2E / math.sqrt(WS)
SAFE = 90.0


def pack_kernel(hidden, wq, wk, tq, tk, extra, out, pick, place):
    @pl.when(pl.program_id(0) == 0)
    def _():
        row = lax.broadcasted_iota(jnp.int32, (256, 2 * SLAB), 0)
        lane = lax.broadcasted_iota(jnp.int32, (256, 2 * SLAB), 1)
        second = jnp.where(lane >= SLAB, 1, 0)
        column = lane - second * SLAB
        for pair in range(PACK // 2):
            source = column + second * WT + pair * 2 * WT % 128
            pick[pair] = jnp.where((row == source) & (column < WT), 1.0, 0.0).astype(jnp.bfloat16)
        for half in range(2):
            source = column - WT + second * WS + half * 2 * WS
            inside = (row == source) & (column >= WT) & (column < SEG0)
            place[half] = jnp.where(inside, 1.0, 0.0)[:128].astype(jnp.bfloat16)

    for rel, (weight, teacher) in enumerate(((wq, tq), (wk, tk))):
        student = jnp.dot(hidden[...], weight[...], preferred_element_type=jnp.float32).astype(
            jnp.bfloat16
        )
        for pair in range(PACK // 2):
            low = pair * 2 * WT // 128 * 128
            slab = jnp.dot(
                teacher[:, low : low + 256], pick[pair], preferred_element_type=jnp.float32
            )
            low = pair * 2 * WS // 128 * 128
            slab += jnp.dot(
                student[:, low : low + 128], place[pair % 2], preferred_element_type=jnp.float32
            )
            for second in range(2):
                part = slab[:, second * SLAB : (second + 1) * SLAB] + extra[...]
                out[rel, 2 * pair + second] = part.astype(jnp.bfloat16)


def pack(hidden, wq, wk, tq, tk, extra):
    rows = hidden.shape[0]
    heads = wq.shape[1] // WS
    return pl.pallas_call(
        pack_kernel,
        grid=(heads // PACK,),
        out_shape=jax.ShapeDtypeStruct((2, heads, rows, SLAB), jnp.bfloat16),
        in_specs=[
            pl.BlockSpec((rows, DS), lambda i: (0, 0)),
            pl.BlockSpec((DS, PACK * WS), lambda i: (0, i)),
            pl.BlockSpec((DS, PACK * WS), lambda i: (0, i)),
            pl.BlockSpec((rows, PACK * WT), lambda i: (0, i)),
            pl.BlockSpec((rows, PACK * WT), lambda i: (0, i)),
            pl.BlockSpec((rows, SLAB), lambda i: (0, 0)),
        ],
        out_specs=pl.BlockSpec((2, PACK, rows, SLAB), lambda i: (0, i, 0, 0)),
        scratch_shapes=[
            pltpu.VMEM((PACK // 2, 256, 2 * SLAB), jnp.bfloat16),
            pltpu.VMEM((2, 128, 2 * SLAB), jnp.bfloat16),
        ],
        compiler_params=pltpu.CompilerParams(vmem_limit_bytes=56 * 1024 * 1024),
        cost_estimate=pl.CostEstimate(
            flops=8 * rows * DS * heads * WS, bytes_accessed=16_000_000, transcendentals=0
        ),
        name="project_and_pack",
    )(hidden, wq, wk, tq, tk, extra)


def relation_kernel(
    blocks, ends, x, out, xt, wt, ws, t_rings, s_rings, causal, sums, grad, seen, opened, pairs, sem
):
    rows = x.shape[1]
    wide = xt.shape[2]
    f32 = jnp.float32

    def entry(place):
        code = pairs[place]
        query = code & 255
        key = (code >> 8) & 255
        return query, key, code >> 16

    def readable(block):
        return jnp.minimum(block, blocks - 1)

    key_at = lax.broadcasted_iota(jnp.int32, (rows, wide), 0)
    query_at = lax.broadcasted_iota(jnp.int32, (rows, wide), 1)
    causal[0] = jnp.zeros((rows, wide), f32)
    causal[1] = jnp.where(key_at <= query_at, 0.0, -HIDDEN)

    feature = lax.broadcasted_iota(jnp.int32, (SLAB, wide), 0)
    lane = lax.broadcasted_iota(jnp.int32, (SLAB, wide), 1)

    def look(block, carry):
        seen[pl.ds(block, 1)] = x[block, :16].astype(f32)[:1].astype(jnp.int32)
        return carry

    lax.fori_loop(0, blocks, look, 0)
    fetch = pltpu.make_async_copy(seen, opened, sem)
    fetch.start()
    fetch.wait()

    def list_pairs(block, total):
        for back in range(REACH):
            key = jnp.maximum(block - back, 0)
            code = block | (key << 8)
            if back == 0:
                pairs[total + LAG] = code | (1 << 16)
                total = total + 1
            else:
                pairs[total + LAG] = code
                is_open = (block >= back) & (opened[block, MASK0 + back - 1] == 1)
                is_open = is_open & (ends[0, block] == ends[1, key])
                total = total + is_open.astype(jnp.int32)
        return total

    def prepare(block, carry):
        peak_t, peak_s, total = carry
        total = list_pairs(block, total)
        tall = jnp.concatenate([x[block], jnp.zeros((wide - rows, SLAB), jnp.bfloat16)], axis=0)
        turned = tall.T
        xt[block] = turned
        values = turned.astype(f32)
        is_seg = (feature >= SEG0) & (feature < ONE0) & (lane < rows)
        bias = jnp.where(is_seg, (values - 1.0) * HIDDEN, 0.0)
        teacher = jnp.where(feature < WT, values, 0.0)
        student = jnp.where((feature >= WT) & (feature < SEG0), values, 0.0)
        wt[block] = (teacher + bias).astype(jnp.bfloat16)
        ws[block] = (student + bias).astype(jnp.bfloat16)
        grad[block] = jnp.zeros((WS, wide), f32)
        return (
            jnp.maximum(peak_t, jnp.sum(teacher * teacher, axis=0, keepdims=True)),
            jnp.maximum(peak_s, jnp.sum(student * student, axis=0, keepdims=True)),
            total,
        )

    none = jnp.zeros((1, wide), f32)
    peak_t, peak_s, count = lax.fori_loop(0, blocks, prepare, (none, none, 0))
    for place in range(LAG):
        pairs[place] = blocks | (blocks << 8)
    for place in range(LAG + UNROLL):
        pairs[count + LAG + place] = blocks | (blocks << 8)
    bound = jnp.maximum(jnp.max(peak_t) * SCALE_T, jnp.max(peak_s) * SCALE_S)

    @pl.when(jnp.logical_not(bound <= SAFE))
    def _():
        def raise_maxima(place, carry):
            query, key, diagonal = entry(place + LAG)
            for member, weights in enumerate((wt, ws)):
                scores = jnp.dot(x[key], weights[query], preferred_element_type=f32)
                scores = scores + causal[diagonal]
                top = jnp.max(scores.reshape(rows // 8, 8, wide), axis=0)
                sums[query, member] = jnp.where(
                    diagonal == 1, top, jnp.maximum(top, sums[query, member])
                )
            return carry

        lax.fori_loop(0, count, raise_maxima, 0)
        slab_row = lax.broadcasted_iota(jnp.int32, (SLAB - SEG0, wide), 0) + SEG0

        def set_maxima(block, carry):
            for member, weights in enumerate((wt, ws)):
                top = jnp.max(sums[block, member], axis=0, keepdims=True)
                slab = weights[block, SEG0:].astype(f32)
                rest = top
                for part in range(3):
                    piece = rest.astype(jnp.bfloat16).astype(f32)
                    rest = rest - piece
                    slab = jnp.where(slab_row == ONE0 + part, -piece, slab)
                weights[block, SEG0:] = slab.astype(jnp.bfloat16)
            return carry

        lax.fori_loop(0, blocks, set_maxima, 0)

    def inverse(place):
        query, _, _ = entry(place)
        total_t = jnp.sum(sums[query, 0], axis=0, keepdims=True)
        total_s = jnp.sum(sums[query, 1], axis=0, keepdims=True)
        return 1.0 / (total_t * math.sqrt(WS)), 1.0 / (total_s * math.sqrt(WS))

    def weigh(place, slot, t_ring, s_ring):
        query, key, diagonal = entry(place + LAG)
        keys = x[readable(key)]
        hide = causal[diagonal]
        for member, (weights, ring, scale) in enumerate(((wt, t_ring, SCALE_T), (ws, s_ring, SCALE_S))):
            scores = jnp.dot(keys, weights[readable(query)], preferred_element_type=f32)
            made = jnp.exp2(scores * scale + hide)
            ring[slot] = made
            part = jnp.sum(made.reshape(rows // 8, 8, wide), axis=0)
            sums[query, member] = jnp.where(diagonal == 1, part, part + sums[query, member])

    def couple(place, slot, t_ring, s_ring, scales):
        query, key, _ = entry(place)
        coupling = (s_ring[slot] * scales[1] - t_ring[slot] * scales[0]).astype(jnp.bfloat16)
        query_side = xt[readable(query), WT:SEG0]
        key_side = xt[readable(key), WT:SEG0, :rows]
        to_keys = lax.dot_general(
            query_side, coupling, (((1,), (1,)), ((), ())), preferred_element_type=f32
        )
        to_queries = jnp.dot(key_side, coupling, preferred_element_type=f32)
        grad[key, :, :rows] += to_keys
        grad[query] += to_queries

    def steps(turn, carry):
        place = UNROLL * turn
        scales = [inverse(place + step) for step in range(UNROLL)]
        for step in range(UNROLL):
            ring = (step - LAG) % UNROLL
            slot = (turn + (step - LAG) // UNROLL) & (SLOTS - 1)
            couple(place + step, slot, t_rings[ring], s_rings[ring], scales[step])
            weigh(place + step, turn & (SLOTS - 1), t_rings[step], s_rings[step])
        return carry

    lax.fori_loop(0, (count + LAG + UNROLL - 1) // UNROLL, steps, 0)

    def finish(block, carry):
        out[block] = grad[block, :, :rows].astype(jnp.bfloat16)
        return carry

    lax.fori_loop(0, blocks, finish, 0)


def relation(x, ends):
    blocks, rows, _ = x.shape
    wide = (rows + 127) // 128 * 128
    ring = pltpu.VMEM((SLOTS, rows, wide), jnp.float32)
    turned = pltpu.VMEM((blocks, SLAB, wide), jnp.bfloat16)
    return pl.pallas_call(
        functools.partial(relation_kernel, blocks),
        out_shape=jax.ShapeDtypeStruct((blocks, WS, rows), jnp.bfloat16),
        in_specs=[
            pl.BlockSpec(memory_space=pltpu.SMEM),
            pl.BlockSpec(memory_space=pltpu.VMEM),
        ],
        out_specs=pl.BlockSpec(memory_space=pltpu.VMEM),
        scratch_shapes=[
            turned,
            turned,
            turned,
            [ring] * UNROLL,
            [ring] * UNROLL,
            pltpu.VMEM((2, rows, wide), jnp.float32),
            pltpu.VMEM((blocks + 1, 2, 8, wide), jnp.float32),
            pltpu.VMEM((blocks + 1, WS, wide), jnp.float32),
            pltpu.VMEM((blocks, SLAB), jnp.int32),
            pltpu.SMEM((blocks, SLAB), jnp.int32),
            pltpu.SMEM((LIST,), jnp.int32),
            pltpu.SemaphoreType.DMA,
        ],
        compiler_params=pltpu.CompilerParams(vmem_limit_bytes=48 * 1024 * 1024),
        cost_estimate=pl.CostEstimate(
            flops=20_000_000_000, bytes_accessed=5_000_000, transcendentals=40_000_000
        ),
        name="relation_gradient",
    )(ends, x)


def shards(teacher_query, teacher_key, student_hidden, w_query, w_key, segment_ids, block_mask):
    rows = student_hidden.shape[0]
    block = lax.axis_index("ctx")
    ends = jnp.stack([segment_ids[::rows], segment_ids[rows - 1 :: rows]])

    own_seg = lax.dynamic_slice_in_dim(segment_ids, block * rows, rows)
    column = jnp.arange(SLAB, dtype=jnp.int32)[None, :]
    extra = (column == own_seg[:, None] + SEG0) | ((column >= ONE0) & (column < MASK0))
    extra = extra.astype(jnp.float32)
    extra += jnp.pad(block_mask.astype(jnp.float32), ((0, 0), (MASK0, SLAB - MASK0 - REACH + 1)))
    slabs = pack(
        student_hidden, w_query, w_key, teacher_query, teacher_key, extra
    )
    units = slabs.reshape(-1, rows, SLAB)
    row = lax.all_to_all(units, "ctx", 0, 0, tiled=True)
    turned = relation(row, ends)
    back = lax.all_to_all(turned, "ctx", 0, 0, tiled=True)
    half = back.shape[0] // 2
    grads = [back[:half].reshape(-1, rows), back[half:].reshape(-1, rows)]

    side = lax.axis_index("head")
    width = w_query.shape[0] // 2

    def project(part):
        return sum(
            lax.dot_general(
                grad,
                lax.dynamic_slice_in_dim(weight, part * width, width, 0),
                (((0,), (1,)), ((), ())),
                preferred_element_type=jnp.float32,
            )
            for grad, weight in zip(grads, (w_query, w_key))
        )

    away = lax.ppermute(project(1 - side), "head", [(0, 1), (1, 0)])
    return (project(side) + away).astype(jnp.bfloat16)


def solution(mesh):
    placed = (
        P("ctx", "head"),
        P("ctx", "head"),
        P("ctx", None),
        P(None, "head"),
        P(None, "head"),
        P(),
        P("ctx", None),
    )
    return jax.shard_map(
        shards, mesh=mesh, in_specs=placed, out_specs=P("ctx", "head"), check_vma=False
    )
```

```python
import functools
import math

import jax
import jax.numpy as jnp
from jax import lax
from jax.experimental import pallas as pl
from jax.experimental.pallas import tpu as pltpu
from jax.sharding import PartitionSpec as P

DT = 5120
DS = 2048
HEADS = 64
REACH = 8
WT = DT // HEADS
WS = DS // HEADS
DEPTH = 128
EXTRA = 16
DOCS = 4
PACK = 8
LISTED = 8
UNROLL = 4
LAG = 3 * UNROLL
SLOTS = 4
AHEAD = 2
LIST = 640
HIDDEN = 1e30
LOG2E = math.log2(math.e)
SCALE_T = LOG2E / math.sqrt(WT)
SCALE_S = LOG2E / math.sqrt(WS)
SAFE = 90.0
MIB = 1024 * 1024
f32 = jnp.float32
bf16 = jnp.bfloat16


def round_up(value, unit):
    return (value + unit - 1) // unit * unit


def project_kernel(hidden, wq, wk, extra, out):
    for rel, weight in enumerate((wq, wk)):
        student = jnp.dot(hidden[...], weight[...], preferred_element_type=f32).astype(bf16)
        turned = jnp.concatenate([student, extra[...]], axis=0).T
        out[rel] = turned.reshape(out.shape[1:])


def project(hidden, wq, wk, mask):
    rows = hidden.shape[0]
    wide = round_up(rows, 128)
    heads = wq.shape[1] // WS
    extra = jnp.pad(mask.astype(bf16).T, ((0, wide - rows - REACH + 1), (0, 0)))
    extra = jnp.broadcast_to(extra, (wide - rows, PACK * WS))
    return pl.pallas_call(
        project_kernel,
        grid=(heads // PACK,),
        out_shape=jax.ShapeDtypeStruct((2, heads, WS, wide), bf16),
        in_specs=[
            pl.BlockSpec((rows, DS), lambda i: (0, 0)),
            pl.BlockSpec((DS, PACK * WS), lambda i: (0, i)),
            pl.BlockSpec((DS, PACK * WS), lambda i: (0, i)),
            pl.BlockSpec((wide - rows, PACK * WS), lambda i: (0, 0)),
        ],
        out_specs=pl.BlockSpec((2, PACK, WS, wide), lambda i: (0, i, 0, 0)),
        compiler_params=pltpu.CompilerParams(vmem_limit_bytes=56 * MIB),
        cost_estimate=pl.CostEstimate(
            flops=4 * rows * DS * heads * WS, bytes_accessed=10_000_000, transcendentals=0
        ),
        name="project_student",
    )(hidden, wq, wk, extra)


def turn_kernel(tq, tk, out):
    rows = tq.shape[0]
    wide = out.shape[-1]
    for rel, teacher in enumerate((tq, tk)):
        zeros = jnp.zeros((wide - rows, teacher.shape[1]), bf16)
        turned = jnp.concatenate([teacher[...], zeros], axis=0).T
        out[rel] = turned.reshape(out.shape[1:])


def turn(tq, tk):
    rows, columns = tq.shape
    wide = round_up(rows, 128)
    heads = columns // WT
    return pl.pallas_call(
        turn_kernel,
        grid=(heads // PACK,),
        out_shape=jax.ShapeDtypeStruct((2, heads, WT, wide), bf16),
        in_specs=[pl.BlockSpec((rows, PACK * WT), lambda i: (0, i))] * 2,
        out_specs=pl.BlockSpec((2, PACK, WT, wide), lambda i: (0, i, 0, 0)),
        compiler_params=pltpu.CompilerParams(vmem_limit_bytes=56 * MIB),
        cost_estimate=pl.CostEstimate(flops=0, bytes_accessed=5_000_000, transcendentals=0),
        name="turn_teacher",
    )(tq, tk)


def read_pair(pairs, place):
    code = pairs[place]
    return code & 255, code >> 8


def fill(block, slab, segments, keys, weights):
    width, wide = slab.shape
    rows = keys.shape[1]
    row = lax.broadcasted_iota(jnp.int32, (EXTRA, wide), 0)
    lane = lax.broadcasted_iota(jnp.int32, (EXTRA, wide), 1)
    hot = jnp.where(row == segments[pl.ds(block, 1)], 1.0, 0.0)
    key_extra = jnp.where((row >= DOCS) & (row < DOCS + 3), 1.0, hot)
    query_extra = jnp.where((row < DOCS) & (lane < rows), (hot - 1.0) * HIDDEN, 0.0)
    zeros = jnp.zeros((DEPTH - EXTRA - width, wide), bf16)
    weights[block] = jnp.concatenate([slab, query_extra.astype(bf16), zeros], axis=0)
    keys[block] = jnp.concatenate([slab, key_extra.astype(bf16), zeros], axis=0).T[:rows]
    values = slab.astype(f32)
    return jnp.sum(values * values, axis=0, keepdims=True)


def subtract_maxima(width, blocks, count, pairs, keys, weights, causal, sums):
    rows, wide = causal.shape

    def highest(query, key):
        return jnp.dot(keys[key], weights[query], preferred_element_type=f32)

    def fold(scores):
        return jnp.max(scores.reshape(rows // 8, 8, wide), axis=0)

    def own_maxima(block, carry):
        sums[block] = fold(highest(block, block) + causal[...])
        return carry

    def raise_maxima(place, carry):
        query, key = read_pair(pairs, place + LAG)
        sums[query] = jnp.maximum(fold(highest(query, key)), sums[query])
        return carry

    lax.fori_loop(0, blocks, own_maxima, 0)
    lax.fori_loop(0, count, raise_maxima, 0)
    row = lax.broadcasted_iota(jnp.int32, (EXTRA, wide), 0)

    def set_maxima(block, carry):
        rest = jnp.max(sums[block], axis=0, keepdims=True)
        extra = weights[block, width : width + EXTRA].astype(f32)
        for part in range(3):
            piece = rest.astype(bf16).astype(f32)
            rest = rest - piece
            extra = jnp.where(row == DOCS + part, -piece, extra)
        weights[block, width : width + EXTRA] = extra.astype(bf16)
        return carry

    lax.fori_loop(0, blocks, set_maxima, 0)


def fill_causal(causal):
    key_at = lax.broadcasted_iota(jnp.int32, causal.shape, 0)
    query_at = lax.broadcasted_iota(jnp.int32, causal.shape, 1)
    causal[...] = jnp.where(key_at <= query_at, 0.0, -HIDDEN)


def weigh(query, key, keys, weights, scale, hide=None):
    last = keys.shape[0] - 1
    scores = jnp.dot(
        keys[jnp.minimum(key, last)],
        weights[jnp.minimum(query, last)],
        preferred_element_type=f32,
    )
    scores = scores * scale
    made = jnp.exp2(scores if hide is None else scores + hide)
    rows, wide = made.shape
    return made, jnp.sum(made.reshape(rows // 8, 8, wide), axis=0)


def student_kernel(
    blocks, ends, segments, slabs, made, scales, features, pairs, count_out, keys, weights, ring, causal, sums, seen, opened, sem, sems
):
    rows, wide = causal.shape
    fill_causal(causal)

    def look(block, carry):
        seen[pl.ds(block, 1)] = slabs[block, :16, wide - 128 :].astype(f32)[:1].astype(jnp.int32)
        return carry

    lax.fori_loop(0, blocks, look, 0)
    fetch = pltpu.make_async_copy(seen, opened, sem)
    fetch.start()
    fetch.wait()
    mask_lane = rows % 128

    def list_pairs(block, total):
        for back in range(1, REACH):
            key = jnp.maximum(block - back, 0)
            pairs[total + LAG] = block | (key << 8)
            is_open = (block >= back) & (opened[block, mask_lane + back - 1] == 1)
            is_open = is_open & (ends[0, block] == ends[1, key])
            total = total + is_open.astype(jnp.int32)
        return total

    lane = lax.broadcasted_iota(jnp.int32, (WS, wide), 1)

    def prepare(block, carry):
        peak, total = carry
        total = list_pairs(block, total)
        slab = jnp.where(lane < rows, slabs[block].astype(f32), 0.0).astype(bf16)
        features[block] = slab
        return jnp.maximum(peak, fill(block, slab, segments, keys, weights)), total

    peak, count = lax.fori_loop(0, blocks, prepare, (jnp.zeros((1, wide), f32), 0))
    count_out[0] = count
    for place in range(LAG):
        pairs[place] = blocks | (blocks << 8)
    for place in range(LAG + LISTED):
        pairs[count + LAG + place] = blocks | (blocks << 8)

    @pl.when(jnp.logical_not(jnp.max(peak) * SCALE_S <= SAFE))
    def _():
        subtract_maxima(WS, blocks, count, pairs, keys, weights, causal, sums)

    def send(turn):
        slot = turn & (SLOTS - 1)
        group = made.at[pl.ds(turn * LISTED, LISTED)]
        return pltpu.make_async_copy(ring.at[slot], group, sems.at[slot])

    def free(turn):
        @pl.when(turn >= SLOTS)
        def _():
            send(turn - SLOTS).wait()

    own_turns = blocks // LISTED

    def own(turn, carry):
        free(turn)
        for step in range(LISTED):
            block = turn * LISTED + step
            ring[turn & (SLOTS - 1), step], sums[block] = weigh(
                block, block, keys, weights, SCALE_S, causal[...]
            )
        send(turn).start()
        return carry

    def others(turn, carry):
        free(turn)
        for step in range(LISTED):
            query, key = read_pair(pairs, (turn - own_turns) * LISTED + step + LAG)
            ring[turn & (SLOTS - 1), step], part = weigh(query, key, keys, weights, SCALE_S)
            sums[query] += part
        send(turn).start()
        return carry

    def drain(turn, carry):
        send(turn).wait()
        return carry

    turns = own_turns + (count + LISTED - 1) // LISTED
    lax.fori_loop(0, own_turns, own, 0)
    lax.fori_loop(own_turns, turns, others, 0)
    lax.fori_loop(turns - SLOTS, turns, drain, 0)

    def finish(block, carry):
        total = jnp.sum(sums[block], axis=0, keepdims=True) * math.sqrt(WS)
        scales[block] = jnp.broadcast_to(1.0 / total, (8, wide))
        return carry

    lax.fori_loop(0, blocks, finish, 0)


def student_weights(slabs, ends, segments, rows):
    blocks, _, wide = slabs.shape
    vmem = pl.BlockSpec(memory_space=pltpu.VMEM)
    smem = pl.BlockSpec(memory_space=pltpu.SMEM)
    return pl.pallas_call(
        functools.partial(student_kernel, blocks),
        out_shape=(
            jax.ShapeDtypeStruct((blocks * REACH, rows, wide), f32),
            jax.ShapeDtypeStruct((blocks, 8, wide), f32),
            jax.ShapeDtypeStruct((blocks, WS, wide), bf16),
            jax.ShapeDtypeStruct((LIST,), jnp.int32),
            jax.ShapeDtypeStruct((1,), jnp.int32),
        ),
        in_specs=[smem, vmem, vmem],
        out_specs=(pl.BlockSpec(memory_space=pl.ANY), vmem, vmem, smem, smem),
        scratch_shapes=[
            pltpu.VMEM((blocks, rows, DEPTH), bf16),
            pltpu.VMEM((blocks, DEPTH, wide), bf16),
            pltpu.VMEM((SLOTS, LISTED, rows, wide), f32),
            pltpu.VMEM((rows, wide), f32),
            pltpu.VMEM((blocks + 1, 8, wide), f32),
            pltpu.VMEM((blocks, 128), jnp.int32),
            pltpu.SMEM((blocks, 128), jnp.int32),
            pltpu.SemaphoreType.DMA,
            pltpu.SemaphoreType.DMA((SLOTS,)),
        ],
        compiler_params=pltpu.CompilerParams(vmem_limit_bytes=48 * MIB),
        cost_estimate=pl.CostEstimate(
            flops=10_000_000_000, bytes_accessed=80_000_000, transcendentals=20_000_000
        ),
        name="student_weights",
    )(ends, segments, slabs)


def gradient_kernel(
    blocks, count_in, pairs, segments, slabs, made, scales, features, out, keys, weights, rings, own_ring, fetched, causal, sums, grad, sems
):
    rows, wide = causal.shape
    count = count_in[0]
    fill_causal(causal)
    turns = (count + LAG + UNROLL - 1) // UNROLL

    def fetch(turn):
        group = jnp.clip(turn - LAG // UNROLL, 0, (made.shape[0] - blocks) // UNROLL - 1)
        first = jnp.where(turn < turns, blocks + group * UNROLL, (turn - turns) * UNROLL)
        slot = turn & (SLOTS - 1)
        group = made.at[pl.ds(first, UNROLL)]
        return pltpu.make_async_copy(group, fetched.at[slot], sems.at[slot])

    for turn in range(AHEAD):
        fetch(turn).start()

    def prepare(block, peak):
        grad[block] = jnp.zeros((WS, wide), f32)
        return jnp.maximum(peak, fill(block, slabs[block], segments, keys, weights))

    peak = lax.fori_loop(0, blocks, prepare, jnp.zeros((1, wide), f32))

    @pl.when(jnp.logical_not(jnp.max(peak) * SCALE_T <= SAFE))
    def _():
        subtract_maxima(WT, blocks, count, pairs, keys, weights, causal, sums)

    def readable(block):
        return jnp.minimum(block, blocks - 1)

    def inverses(query):
        total = jnp.sum(sums[query], axis=0, keepdims=True) * math.sqrt(WS)
        return 1.0 / total, scales[readable(query), :1]

    def couple(query, key, teacher, student, scale):
        coupling = (student * scale[1] - teacher * scale[0]).astype(bf16)
        query_side = features[readable(query)]
        key_side = features[readable(key), :, :rows]
        grad[key, :, :rows] += lax.dot_general(
            query_side, coupling, (((1,), (1,)), ((), ())), preferred_element_type=f32
        )
        grad[query] += jnp.dot(key_side, coupling, preferred_element_type=f32)

    def own_weights(turn, carry):
        for step in range(UNROLL):
            block = turn * UNROLL + step
            own_ring[block], sums[block] = weigh(
                block, block, keys, weights, SCALE_T, causal[...]
            )
        return carry

    def half(turn, parity):
        slot = turn & (SLOTS - 1)
        fetch(turn).wait()
        fetch(turn + AHEAD).start()
        place = UNROLL * turn
        old = [read_pair(pairs, place + step) for step in range(UNROLL)]
        new = [read_pair(pairs, place + step + LAG) for step in range(UNROLL)]
        scale = [inverses(query) for query, _ in old]
        now = turn >> 1 & 1
        before = (turn - LAG // UNROLL) >> 1 & 1
        for step in range(UNROLL):
            teacher = rings[1 - parity][before, step]
            couple(*old[step], teacher, fetched[slot, step], scale[step])
            rings[parity][now, step], part = weigh(*new[step], keys, weights, SCALE_T)
            sums[new[step][0]] += part

    def others(turn, carry):
        for parity in range(2):
            pl.when(turn & 1 == parity)(functools.partial(half, turn, parity))
        return carry

    own_turns = blocks // UNROLL

    def own_terms(turn, carry):
        slot = turn & (SLOTS - 1)
        fetch(turn).wait()

        @pl.when(turn + AHEAD < turns + own_turns)
        def _():
            fetch(turn + AHEAD).start()

        scale = [inverses((turn - turns) * UNROLL + step) for step in range(UNROLL)]
        for step in range(UNROLL):
            block = (turn - turns) * UNROLL + step
            couple(block, block, own_ring[block], fetched[slot, step], scale[step])
        return carry

    lax.fori_loop(0, own_turns, own_weights, 0)
    lax.fori_loop(0, turns, others, 0)
    lax.fori_loop(turns, turns + own_turns, own_terms, 0)

    def finish(block, carry):
        out[block] = grad[block, :, :rows].astype(bf16)
        return carry

    lax.fori_loop(0, blocks, finish, 0)


def relation_gradient(slabs, segments, made, scales, features, pairs, count):
    blocks, _, wide = slabs.shape
    rows = made.shape[1]
    vmem = pl.BlockSpec(memory_space=pltpu.VMEM)
    smem = pl.BlockSpec(memory_space=pltpu.SMEM)
    return pl.pallas_call(
        functools.partial(gradient_kernel, blocks),
        out_shape=jax.ShapeDtypeStruct((blocks, WS, rows), bf16),
        in_specs=[smem, smem, vmem, vmem, pl.BlockSpec(memory_space=pl.ANY), vmem, vmem],
        out_specs=vmem,
        scratch_shapes=[
            pltpu.VMEM((blocks, rows, DEPTH), bf16),
            pltpu.VMEM((blocks, DEPTH, wide), bf16),
            [pltpu.VMEM((2, UNROLL, rows, wide), f32)] * 2,
            pltpu.VMEM((blocks, rows, wide), f32),
            pltpu.VMEM((SLOTS, UNROLL, rows, wide), f32),
            pltpu.VMEM((rows, wide), f32),
            pltpu.VMEM((blocks + 1, 8, wide), f32),
            pltpu.VMEM((blocks + 1, WS, wide), f32),
            pltpu.SemaphoreType.DMA((SLOTS,)),
        ],
        compiler_params=pltpu.CompilerParams(vmem_limit_bytes=56 * MIB),
        cost_estimate=pl.CostEstimate(
            flops=20_000_000_000, bytes_accessed=80_000_000, transcendentals=20_000_000
        ),
        name="relation_gradient",
    )(count, pairs, segments, slabs, made, scales, features)


def head_gradient(student, teacher, segment_ids, rows):
    blocks, _, wide = student.shape
    ends = jnp.stack([segment_ids[::rows], segment_ids[rows - 1 :: rows]])
    segments = jnp.pad(
        segment_ids.reshape(blocks, rows), ((0, 0), (0, wide - rows)), constant_values=-1
    )
    made, scales, features, pairs, count = student_weights(student, ends, segments, rows)
    return relation_gradient(teacher, segments, made, scales, features, pairs, count)


def shards(teacher_query, teacher_key, student_hidden, w_query, w_key, segment_ids, block_mask):
    rows = student_hidden.shape[0]
    student = project(student_hidden, w_query, w_key, block_mask)
    teacher = turn(teacher_query, teacher_key)
    student = lax.all_to_all(student.reshape(-1, *student.shape[2:]), "ctx", 0, 0, tiled=True)
    teacher = lax.all_to_all(teacher.reshape(-1, *teacher.shape[2:]), "ctx", 0, 0, tiled=True)
    turned = head_gradient(student, teacher, segment_ids, rows)
    back = lax.all_to_all(turned, "ctx", 0, 0, tiled=True)
    half = back.shape[0] // 2
    grads = [back[:half].reshape(-1, rows), back[half:].reshape(-1, rows)]

    side = lax.axis_index("head")
    width = w_query.shape[0] // 2

    def unproject(part):
        return sum(
            lax.dot_general(
                grad,
                lax.dynamic_slice_in_dim(weight, part * width, width, 0),
                (((0,), (1,)), ((), ())),
                preferred_element_type=f32,
            )
            for grad, weight in zip(grads, (w_query, w_key))
        )

    away = lax.ppermute(unproject(1 - side), "head", [(0, 1), (1, 0)])
    return (unproject(side) + away).astype(bf16)


def solution(mesh):
    placed = (
        P("ctx", "head"),
        P("ctx", "head"),
        P("ctx", None),
        P(None, "head"),
        P(None, "head"),
        P(),
        P("ctx", None),
    )
    return jax.shard_map(
        shards, mesh=mesh, in_specs=placed, out_specs=P("ctx", "head"), check_vma=False
    )
```

```python
import functools
import math

import jax
import jax.numpy as jnp
from jax import lax
from jax.experimental import pallas as pl
from jax.experimental.pallas import tpu as pltpu
from jax.sharding import PartitionSpec as P

DT = 5120
DS = 2048
HEADS = 64
REACH = 8
WT = DT // HEADS
WS = DS // HEADS
SEG0 = WT + WS
ONE0 = SEG0 + 4
MASK0 = ONE0 + 3
SLAB = 128
PACK = 8
LAG = 14
UNROLL = 4
SLOTS = 8
LIST = 640
HIDDEN = 1e30
LOG2E = math.log2(math.e)
SCALE_T = LOG2E / math.sqrt(WT)
SCALE_S = LOG2E / math.sqrt(WS)
SAFE = 90.0


def pack_kernel(hidden, wq, wk, tq, tk, extra, out, pick, place):
    @pl.when(pl.program_id(0) == 0)
    def _():
        row = lax.broadcasted_iota(jnp.int32, (256, 2 * SLAB), 0)
        lane = lax.broadcasted_iota(jnp.int32, (256, 2 * SLAB), 1)
        second = jnp.where(lane >= SLAB, 1, 0)
        column = lane - second * SLAB
        for pair in range(PACK // 2):
            source = column + second * WT + pair * 2 * WT % 128
            pick[pair] = jnp.where((row == source) & (column < WT), 1.0, 0.0).astype(jnp.bfloat16)
        for half in range(2):
            source = column - WT + second * WS + half * 2 * WS
            inside = (row == source) & (column >= WT) & (column < SEG0)
            place[half] = jnp.where(inside, 1.0, 0.0)[:128].astype(jnp.bfloat16)

    for rel, (weight, teacher) in enumerate(((wq, tq), (wk, tk))):
        student = jnp.dot(hidden[...], weight[...], preferred_element_type=jnp.float32).astype(
            jnp.bfloat16
        )
        for pair in range(PACK // 2):
            low = pair * 2 * WT // 128 * 128
            slab = jnp.dot(
                teacher[:, low : low + 256], pick[pair], preferred_element_type=jnp.float32
            )
            low = pair * 2 * WS // 128 * 128
            slab += jnp.dot(
                student[:, low : low + 128], place[pair % 2], preferred_element_type=jnp.float32
            )
            for second in range(2):
                part = slab[:, second * SLAB : (second + 1) * SLAB] + extra[...]
                out[rel, 2 * pair + second] = part.astype(jnp.bfloat16)


def pack(hidden, wq, wk, tq, tk, extra):
    rows = hidden.shape[0]
    heads = wq.shape[1] // WS
    return pl.pallas_call(
        pack_kernel,
        grid=(heads // PACK,),
        out_shape=jax.ShapeDtypeStruct((2, heads, rows, SLAB), jnp.bfloat16),
        in_specs=[
            pl.BlockSpec((rows, DS), lambda i: (0, 0)),
            pl.BlockSpec((DS, PACK * WS), lambda i: (0, i)),
            pl.BlockSpec((DS, PACK * WS), lambda i: (0, i)),
            pl.BlockSpec((rows, PACK * WT), lambda i: (0, i)),
            pl.BlockSpec((rows, PACK * WT), lambda i: (0, i)),
            pl.BlockSpec((rows, SLAB), lambda i: (0, 0)),
        ],
        out_specs=pl.BlockSpec((2, PACK, rows, SLAB), lambda i: (0, i, 0, 0)),
        scratch_shapes=[
            pltpu.VMEM((PACK // 2, 256, 2 * SLAB), jnp.bfloat16),
            pltpu.VMEM((2, 128, 2 * SLAB), jnp.bfloat16),
        ],
        compiler_params=pltpu.CompilerParams(vmem_limit_bytes=56 * 1024 * 1024),
        cost_estimate=pl.CostEstimate(
            flops=8 * rows * DS * heads * WS, bytes_accessed=16_000_000, transcendentals=0
        ),
        name="project_and_pack",
    )(hidden, wq, wk, tq, tk, extra)


def relation_kernel(
    blocks, ends, x, out, xt, both, t_rings, s_rings, causal, sums, grad, seen, opened, pairs, sem
):
    rows = x.shape[1]
    wide = xt.shape[2]
    f32 = jnp.float32

    def entry(place):
        code = pairs[place]
        query = code & 255
        key = (code >> 8) & 255
        return query, key, code >> 16

    def readable(block):
        return jnp.minimum(block, blocks - 1)

    key_at = lax.broadcasted_iota(jnp.int32, (rows, wide), 0)
    query_at = lax.broadcasted_iota(jnp.int32, (rows, wide), 1)
    causal[0] = jnp.zeros((rows, wide), f32)
    causal[1] = jnp.where(key_at <= query_at, 0.0, -HIDDEN)

    feature = lax.broadcasted_iota(jnp.int32, (SLAB, wide), 0)
    lane = lax.broadcasted_iota(jnp.int32, (SLAB, wide), 1)

    def look(block, carry):
        seen[pl.ds(block, 1)] = x[block, :16].astype(f32)[:1].astype(jnp.int32)
        return carry

    lax.fori_loop(0, blocks, look, 0)
    fetch = pltpu.make_async_copy(seen, opened, sem)
    fetch.start()
    fetch.wait()

    def list_pairs(block, total):
        for back in range(REACH):
            key = jnp.maximum(block - back, 0)
            code = block | (key << 8)
            if back == 0:
                pairs[total + LAG] = code | (1 << 16)
                total = total + 1
            else:
                pairs[total + LAG] = code
                is_open = (block >= back) & (opened[block, MASK0 + back - 1] == 1)
                is_open = is_open & (ends[0, block] == ends[1, key])
                total = total + is_open.astype(jnp.int32)
        return total

    def prepare(block, carry):
        peak_t, peak_s, total = carry
        total = list_pairs(block, total)
        tall = jnp.concatenate([x[block], jnp.zeros((wide - rows, SLAB), jnp.bfloat16)], axis=0)
        turned = tall.T
        xt[block] = turned
        values = turned.astype(f32)
        is_seg = (feature >= SEG0) & (feature < ONE0) & (lane < rows)
        bias = jnp.where(is_seg, (values - 1.0) * HIDDEN, 0.0)
        teacher = jnp.where(feature < WT, values, 0.0)
        student = jnp.where((feature >= WT) & (feature < SEG0), values, 0.0)
        both[block, :, :wide] = (teacher + bias).astype(jnp.bfloat16)
        both[block, :, wide:] = (student + bias).astype(jnp.bfloat16)
        grad[block] = jnp.zeros((WS, wide), f32)
        return (
            jnp.maximum(peak_t, jnp.sum(teacher * teacher, axis=0, keepdims=True)),
            jnp.maximum(peak_s, jnp.sum(student * student, axis=0, keepdims=True)),
            total,
        )

    none = jnp.zeros((1, wide), f32)
    peak_t, peak_s, count = lax.fori_loop(0, blocks, prepare, (none, none, 0))
    for place in range(LAG):
        pairs[place] = blocks | (blocks << 8)
    for place in range(LAG + UNROLL):
        pairs[count + LAG + place] = blocks | (blocks << 8)
    bound = jnp.maximum(jnp.max(peak_t) * SCALE_T, jnp.max(peak_s) * SCALE_S)

    @pl.when(jnp.logical_not(bound <= SAFE))
    def _():
        def raise_maxima(place, carry):
            query, key, diagonal = entry(place + LAG)
            for member in range(2):
                columns = slice(member * wide, (member + 1) * wide)
                scores = jnp.dot(x[key], both[query, :, columns], preferred_element_type=f32)
                scores = scores + causal[diagonal]
                top = jnp.max(scores.reshape(rows // 8, 8, wide), axis=0)
                sums[query, member] = jnp.where(
                    diagonal == 1, top, jnp.maximum(top, sums[query, member])
                )
            return carry

        lax.fori_loop(0, count, raise_maxima, 0)
        slab_row = lax.broadcasted_iota(jnp.int32, (SLAB - SEG0, wide), 0) + SEG0

        def set_maxima(block, carry):
            for member in range(2):
                columns = slice(member * wide, (member + 1) * wide)
                top = jnp.max(sums[block, member], axis=0, keepdims=True)
                slab = both[block, SEG0:, columns].astype(f32)
                rest = top
                for part in range(3):
                    piece = rest.astype(jnp.bfloat16).astype(f32)
                    rest = rest - piece
                    slab = jnp.where(slab_row == ONE0 + part, -piece, slab)
                both[block, SEG0:, columns] = slab.astype(jnp.bfloat16)
            return carry

        lax.fori_loop(0, blocks, set_maxima, 0)

    def inverse(place):
        query, _, _ = entry(place)
        total_t = jnp.sum(sums[query, 0], axis=0, keepdims=True)
        total_s = jnp.sum(sums[query, 1], axis=0, keepdims=True)
        return 1.0 / (total_t * math.sqrt(WS)), 1.0 / (total_s * math.sqrt(WS))

    def weigh(place, slot, t_ring, s_ring):
        query, key, diagonal = entry(place + LAG)
        keys = x[readable(key)]
        hide = causal[diagonal]
        products = jnp.dot(keys, both[readable(query)], preferred_element_type=f32)
        for member, (ring, scale) in enumerate(((t_ring, SCALE_T), (s_ring, SCALE_S))):
            scores = products[:, member * wide : (member + 1) * wide]
            made = jnp.exp2(scores * scale + hide)
            ring[slot] = made
            part = jnp.sum(made.reshape(rows // 8, 8, wide), axis=0)
            sums[query, member] = jnp.where(diagonal == 1, part, part + sums[query, member])

    def couple(place, slot, t_ring, s_ring, scales):
        query, key, _ = entry(place)
        coupling = (s_ring[slot] * scales[1] - t_ring[slot] * scales[0]).astype(jnp.bfloat16)
        query_side = xt[readable(query), WT:SEG0]
        key_side = xt[readable(key), WT:SEG0, :rows]
        to_keys = lax.dot_general(
            query_side, coupling, (((1,), (1,)), ((), ())), preferred_element_type=f32
        )
        to_queries = jnp.dot(key_side, coupling, preferred_element_type=f32)
        grad[key, :, :rows] += to_keys
        grad[query] += to_queries

    def steps(turn, carry):
        place = UNROLL * turn
        scales = [inverse(place + step) for step in range(UNROLL)]
        for step in range(UNROLL):
            ring = (step - LAG) % UNROLL
            slot = (turn + (step - LAG) // UNROLL) & (SLOTS - 1)
            couple(place + step, slot, t_rings[ring], s_rings[ring], scales[step])
            weigh(place + step, turn & (SLOTS - 1), t_rings[step], s_rings[step])
        return carry

    lax.fori_loop(0, (count + LAG + UNROLL - 1) // UNROLL, steps, 0)

    def finish(block, carry):
        out[block] = grad[block, :, :rows].astype(jnp.bfloat16)
        return carry

    lax.fori_loop(0, blocks, finish, 0)


def relation(x, ends):
    blocks, rows, _ = x.shape
    wide = (rows + 127) // 128 * 128
    ring = pltpu.VMEM((SLOTS, rows, wide), jnp.float32)
    turned = pltpu.VMEM((blocks, SLAB, wide), jnp.bfloat16)
    return pl.pallas_call(
        functools.partial(relation_kernel, blocks),
        out_shape=jax.ShapeDtypeStruct((blocks, WS, rows), jnp.bfloat16),
        in_specs=[
            pl.BlockSpec(memory_space=pltpu.SMEM),
            pl.BlockSpec(memory_space=pltpu.VMEM),
        ],
        out_specs=pl.BlockSpec(memory_space=pltpu.VMEM),
        scratch_shapes=[
            turned,
            pltpu.VMEM((blocks, SLAB, 2 * wide), jnp.bfloat16),
            [ring] * UNROLL,
            [ring] * UNROLL,
            pltpu.VMEM((2, rows, wide), jnp.float32),
            pltpu.VMEM((blocks + 1, 2, 8, wide), jnp.float32),
            pltpu.VMEM((blocks + 1, WS, wide), jnp.float32),
            pltpu.VMEM((blocks, SLAB), jnp.int32),
            pltpu.SMEM((blocks, SLAB), jnp.int32),
            pltpu.SMEM((LIST,), jnp.int32),
            pltpu.SemaphoreType.DMA,
        ],
        compiler_params=pltpu.CompilerParams(vmem_limit_bytes=48 * 1024 * 1024),
        cost_estimate=pl.CostEstimate(
            flops=20_000_000_000, bytes_accessed=5_000_000, transcendentals=40_000_000
        ),
        name="relation_gradient",
    )(ends, x)


def shards(teacher_query, teacher_key, student_hidden, w_query, w_key, segment_ids, block_mask):
    rows = student_hidden.shape[0]
    block = lax.axis_index("ctx")
    ends = jnp.stack([segment_ids[::rows], segment_ids[rows - 1 :: rows]])

    own_seg = lax.dynamic_slice_in_dim(segment_ids, block * rows, rows)
    column = jnp.arange(SLAB, dtype=jnp.int32)[None, :]
    extra = (column == own_seg[:, None] + SEG0) | ((column >= ONE0) & (column < MASK0))
    extra = extra.astype(jnp.float32)
    extra += jnp.pad(block_mask.astype(jnp.float32), ((0, 0), (MASK0, SLAB - MASK0 - REACH + 1)))
    slabs = pack(
        student_hidden, w_query, w_key, teacher_query, teacher_key, extra
    )
    units = slabs.reshape(-1, rows, SLAB)
    row = lax.all_to_all(units, "ctx", 0, 0, tiled=True)
    turned = relation(row, ends)
    back = lax.all_to_all(turned, "ctx", 0, 0, tiled=True)
    half = back.shape[0] // 2
    grads = [back[:half].reshape(-1, rows), back[half:].reshape(-1, rows)]

    side = lax.axis_index("head")
    width = w_query.shape[0] // 2

    def project(part):
        return sum(
            lax.dot_general(
                grad,
                lax.dynamic_slice_in_dim(weight, part * width, width, 0),
                (((0,), (1,)), ((), ())),
                preferred_element_type=jnp.float32,
            )
            for grad, weight in zip(grads, (w_query, w_key))
        )

    away = lax.ppermute(project(1 - side), "head", [(0, 1), (1, 0)])
    return (project(side) + away).astype(jnp.bfloat16)


def solution(mesh):
    placed = (
        P("ctx", "head"),
        P("ctx", "head"),
        P("ctx", None),
        P(None, "head"),
        P(None, "head"),
        P(),
        P("ctx", None),
    )
    return jax.shard_map(
        shards, mesh=mesh, in_specs=placed, out_specs=P("ctx", "head"), check_vma=False
    )
```

```python
import functools
import math

import jax
import jax.numpy as jnp
from jax import lax
from jax.experimental import pallas as pl
from jax.experimental.pallas import tpu as pltpu
from jax.sharding import PartitionSpec as P

DT = 5120
DS = 2048
HEADS = 64
REACH = 8
WT = DT // HEADS
WS = DS // HEADS
DEPTH = 128
EXTRA = 16
DOCS = 4
PACK = 8
LISTED = 8
UNROLL = 4
LAG = 3 * UNROLL
SLOTS = 4
AHEAD = 2
LIST = 640
HIDDEN = 1e30
LOG2E = math.log2(math.e)
SCALE_T = LOG2E / math.sqrt(WT)
SCALE_S = LOG2E / math.sqrt(WS)
SAFE = 90.0
MIB = 1024 * 1024
f32 = jnp.float32
bf16 = jnp.bfloat16


def round_up(value, unit):
    return (value + unit - 1) // unit * unit


def project_kernel(mask, hidden, wq, wk, out):
    rows, wide = hidden.shape[0], out.shape[-1]
    row = lax.broadcasted_iota(jnp.int32, (wide - rows, PACK * WS), 0)
    extra = jnp.zeros(row.shape, f32)
    for back in range(REACH - 1):
        extra = jnp.where(row == back, mask[0, back].astype(f32), extra)
    extra = extra.astype(bf16)
    for rel, weight in enumerate((wq, wk)):
        student = jnp.dot(hidden[...], weight[...], preferred_element_type=f32).astype(bf16)
        turned = jnp.concatenate([student, extra], axis=0).T
        out[rel] = turned.reshape(out.shape[1:])


def project(hidden, wq, wk, mask):
    rows = hidden.shape[0]
    wide = round_up(rows, 128)
    heads = wq.shape[1] // WS
    return pl.pallas_call(
        project_kernel,
        grid=(heads // PACK,),
        out_shape=jax.ShapeDtypeStruct((2, heads, WS, wide), bf16),
        in_specs=[
            pl.BlockSpec(memory_space=pltpu.SMEM),
            pl.BlockSpec((rows, DS), lambda i: (0, 0)),
            pl.BlockSpec((DS, PACK * WS), lambda i: (0, i)),
            pl.BlockSpec((DS, PACK * WS), lambda i: (0, i)),
        ],
        out_specs=pl.BlockSpec((2, PACK, WS, wide), lambda i: (0, i, 0, 0)),
        compiler_params=pltpu.CompilerParams(vmem_limit_bytes=56 * MIB),
        cost_estimate=pl.CostEstimate(
            flops=4 * rows * DS * heads * WS, bytes_accessed=10_000_000, transcendentals=0
        ),
        name="project_student",
    )(mask, hidden, wq, wk)


def turn_kernel(tq, tk, out):
    rows = tq.shape[0]
    wide = out.shape[-1]
    for rel, teacher in enumerate((tq, tk)):
        zeros = jnp.zeros((wide - rows, teacher.shape[1]), bf16)
        turned = jnp.concatenate([teacher[...], zeros], axis=0).T
        out[rel] = turned.reshape(out.shape[1:])


def turn(tq, tk):
    rows, columns = tq.shape
    wide = round_up(rows, 128)
    heads = columns // WT
    return pl.pallas_call(
        turn_kernel,
        grid=(heads // PACK,),
        out_shape=jax.ShapeDtypeStruct((2, heads, WT, wide), bf16),
        in_specs=[pl.BlockSpec((rows, PACK * WT), lambda i: (0, i))] * 2,
        out_specs=pl.BlockSpec((2, PACK, WT, wide), lambda i: (0, i, 0, 0)),
        compiler_params=pltpu.CompilerParams(vmem_limit_bytes=56 * MIB),
        cost_estimate=pl.CostEstimate(flops=0, bytes_accessed=5_000_000, transcendentals=0),
        name="turn_teacher",
    )(tq, tk)


def read_pair(pairs, place):
    code = pairs[place]
    return code & 255, (code >> 8) & 255, code >> 16


def fill(block, slab, segments, keys, weights):
    width, wide = slab.shape
    rows = keys.shape[1]
    row = lax.broadcasted_iota(jnp.int32, (EXTRA, wide), 0)
    lane = lax.broadcasted_iota(jnp.int32, (EXTRA, wide), 1)
    hot = jnp.where(row == segments[pl.ds(block, 1)], 1.0, 0.0)
    key_extra = jnp.where((row >= DOCS) & (row < DOCS + 3), 1.0, hot)
    query_extra = jnp.where((row < DOCS) & (lane < rows), (hot - 1.0) * HIDDEN, 0.0)
    zeros = jnp.zeros((DEPTH - EXTRA - width, wide), bf16)
    weights[block] = jnp.concatenate([slab, query_extra.astype(bf16), zeros], axis=0)
    keys[block] = jnp.concatenate([slab, key_extra.astype(bf16), zeros], axis=0).T[:rows]
    values = slab.astype(f32)
    return jnp.sum(values * values, axis=0, keepdims=True)


def subtract_maxima(width, blocks, count, pairs, keys, weights, causal, sums):
    rows, wide = causal.shape[1:]

    def raise_maxima(place, carry):
        query, key, diagonal = read_pair(pairs, place + LAG)
        scores = jnp.dot(keys[key], weights[query], preferred_element_type=f32)
        scores = scores + causal[diagonal]
        top = jnp.max(scores.reshape(rows // 8, 8, wide), axis=0)
        sums[query] = jnp.where(diagonal == 1, top, jnp.maximum(top, sums[query]))
        return carry

    lax.fori_loop(0, count, raise_maxima, 0)
    row = lax.broadcasted_iota(jnp.int32, (EXTRA, wide), 0)

    def set_maxima(block, carry):
        rest = jnp.max(sums[block], axis=0, keepdims=True)
        extra = weights[block, width : width + EXTRA].astype(f32)
        for part in range(3):
            piece = rest.astype(bf16).astype(f32)
            rest = rest - piece
            extra = jnp.where(row == DOCS + part, -piece, extra)
        weights[block, width : width + EXTRA] = extra.astype(bf16)
        return carry

    lax.fori_loop(0, blocks, set_maxima, 0)


def fill_causal(causal):
    shape = causal.shape[1:]
    key_at = lax.broadcasted_iota(jnp.int32, shape, 0)
    query_at = lax.broadcasted_iota(jnp.int32, shape, 1)
    causal[0] = jnp.zeros(shape, f32)
    causal[1] = jnp.where(key_at <= query_at, 0.0, -HIDDEN)


def weigh(place, blocks, pairs, keys, weights, scale, causal, ring, slot, sums):
    query, key, diagonal = read_pair(pairs, place + LAG)
    rows, wide = causal.shape[1:]
    scores = jnp.dot(
        keys[jnp.minimum(key, blocks - 1)],
        weights[jnp.minimum(query, blocks - 1)],
        preferred_element_type=f32,
    )
    made = jnp.exp2(scores * scale + causal[diagonal])
    ring[slot] = made
    part = jnp.sum(made.reshape(rows // 8, 8, wide), axis=0)
    sums[query] = jnp.where(diagonal == 1, part, part + sums[query])


def student_kernel(
    blocks, ends, segments, slabs, made, scales, features, pairs, count_out, keys, weights, rings, causal, sums, seen, opened, sem, sems
):
    rows, wide = causal.shape[1:]
    fill_causal(causal)

    def look(block, carry):
        seen[pl.ds(block, 1)] = slabs[block, :16, wide - 128 :].astype(f32)[:1].astype(jnp.int32)
        return carry

    lax.fori_loop(0, blocks, look, 0, unroll=8)
    fetch = pltpu.make_async_copy(seen, opened, sem)
    fetch.start()
    fetch.wait()
    mask_lane = rows % 128

    def list_pairs(block, total):
        for back in range(REACH):
            key = jnp.maximum(block - back, 0)
            code = block | (key << 8)
            if back == 0:
                pairs[total + LAG] = code | (1 << 16)
                total = total + 1
            else:
                pairs[total + LAG] = code
                is_open = (block >= back) & (opened[block, mask_lane + back - 1] == 1)
                is_open = is_open & (ends[0, block] == ends[1, key])
                total = total + is_open.astype(jnp.int32)
        return total

    lane = lax.broadcasted_iota(jnp.int32, (WS, wide), 1)

    def prepare(block, carry):
        peak, total = carry
        total = list_pairs(block, total)
        slab = jnp.where(lane < rows, slabs[block].astype(f32), 0.0).astype(bf16)
        features[block] = slab
        return jnp.maximum(peak, fill(block, slab, segments, keys, weights)), total

    peak, count = lax.fori_loop(0, blocks, prepare, (jnp.zeros((1, wide), f32), 0), unroll=4)
    count_out[0] = count
    for place in range(LAG):
        pairs[place] = blocks | (blocks << 8)
    for place in range(LAG + LISTED):
        pairs[count + LAG + place] = blocks | (blocks << 8)

    @pl.when(jnp.logical_not(jnp.max(peak) * SCALE_S <= SAFE))
    def _():
        subtract_maxima(WS, blocks, count, pairs, keys, weights, causal, sums)

    def send(place, step, slot):
        return pltpu.make_async_copy(rings[step].at[slot], made.at[place], sems.at[step, slot])

    def steps(turn, carry):
        slot = turn & (SLOTS - 1)

        @pl.when(turn >= SLOTS)
        def _():
            for step in range(LISTED):
                send(LISTED * turn + step, step, slot).wait()

        for step in range(LISTED):
            place = LISTED * turn + step
            weigh(place, blocks, pairs, keys, weights, SCALE_S, causal, rings[step], slot, sums)
        for step in range(LISTED):
            send(LISTED * turn + step, step, slot).start()
        return carry

    turns = (count + LISTED - 1) // LISTED
    lax.fori_loop(0, turns, steps, 0)

    def drain(turn, carry):
        for step in range(LISTED):
            send(LISTED * turn + step, step, turn & (SLOTS - 1)).wait()
        return carry

    lax.fori_loop(jnp.maximum(turns - SLOTS, 0), turns, drain, 0)

    def finish(block, carry):
        total = jnp.sum(sums[block], axis=0, keepdims=True) * math.sqrt(WS)
        scales[block] = jnp.broadcast_to(1.0 / total, (8, wide))
        return carry

    lax.fori_loop(0, blocks, finish, 0, unroll=8)


def student_weights(slabs, ends, segments, rows):
    blocks, _, wide = slabs.shape
    vmem = pl.BlockSpec(memory_space=pltpu.VMEM)
    smem = pl.BlockSpec(memory_space=pltpu.SMEM)
    ring = pltpu.VMEM((SLOTS, rows, wide), f32)
    return pl.pallas_call(
        functools.partial(student_kernel, blocks),
        out_shape=(
            jax.ShapeDtypeStruct((blocks * REACH, rows, wide), f32),
            jax.ShapeDtypeStruct((blocks, 8, wide), f32),
            jax.ShapeDtypeStruct((blocks, WS, wide), bf16),
            jax.ShapeDtypeStruct((LIST,), jnp.int32),
            jax.ShapeDtypeStruct((1,), jnp.int32),
        ),
        in_specs=[smem, vmem, vmem],
        out_specs=(pl.BlockSpec(memory_space=pl.ANY), vmem, vmem, smem, smem),
        scratch_shapes=[
            pltpu.VMEM((blocks, rows, DEPTH), bf16),
            pltpu.VMEM((blocks, DEPTH, wide), bf16),
            [ring] * LISTED,
            pltpu.VMEM((2, rows, wide), f32),
            pltpu.VMEM((blocks + 1, 8, wide), f32),
            pltpu.VMEM((blocks, 128), jnp.int32),
            pltpu.SMEM((blocks, 128), jnp.int32),
            pltpu.SemaphoreType.DMA,
            pltpu.SemaphoreType.DMA((LISTED, SLOTS)),
        ],
        compiler_params=pltpu.CompilerParams(vmem_limit_bytes=48 * MIB),
        cost_estimate=pl.CostEstimate(
            flops=10_000_000_000, bytes_accessed=80_000_000, transcendentals=20_000_000
        ),
        name="student_weights",
    )(ends, segments, slabs)


def gradient_kernel(
    blocks, count_in, pairs, segments, slabs, made, scales, features, out, keys, weights, rings, fetched, causal, sums, grad, sems
):
    rows, wide = causal.shape[1:]
    count = count_in[0]
    fill_causal(causal)

    def fetch(turn, step):
        pair = jnp.clip(UNROLL * turn + step - LAG, 0, made.shape[0] - 1)
        slot = turn & (SLOTS - 1)
        return pltpu.make_async_copy(made.at[pair], fetched[step].at[slot], sems.at[step, slot])

    for turn in range(AHEAD):
        for step in range(UNROLL):
            fetch(turn, step).start()

    def prepare(block, peak):
        grad[block] = jnp.zeros((WS, wide), f32)
        return jnp.maximum(peak, fill(block, slabs[block], segments, keys, weights))

    peak = lax.fori_loop(0, blocks, prepare, jnp.zeros((1, wide), f32), unroll=4)

    @pl.when(jnp.logical_not(jnp.max(peak) * SCALE_T <= SAFE))
    def _():
        subtract_maxima(WT, blocks, count, pairs, keys, weights, causal, sums)

    def readable(block):
        return jnp.minimum(block, blocks - 1)

    def inverses(place):
        query, _, _ = read_pair(pairs, place)
        total = jnp.sum(sums[query], axis=0, keepdims=True) * math.sqrt(WS)
        return 1.0 / total, scales[readable(query), :1]

    def couple(place, teacher, student, scale):
        query, key, _ = read_pair(pairs, place)
        coupling = (student * scale[1] - teacher * scale[0]).astype(bf16)
        query_side = features[readable(query)]
        key_side = features[readable(key), :, :rows]
        grad[key, :, :rows] += lax.dot_general(
            query_side, coupling, (((1,), (1,)), ((), ())), preferred_element_type=f32
        )
        grad[query] += jnp.dot(key_side, coupling, preferred_element_type=f32)

    def half(turn, parity):
        slot = turn & (SLOTS - 1)
        for step in range(UNROLL):
            fetch(turn, step).wait()
        for step in range(UNROLL):
            fetch(turn + AHEAD, step).start()
        scale = [inverses(UNROLL * turn + step) for step in range(UNROLL)]
        now = turn // 2 & 1
        before = (turn - LAG // UNROLL) // 2 & 1
        for step in range(UNROLL):
            place = UNROLL * turn + step
            old = rings[1 - parity][step][before]
            couple(place, old, fetched[step][slot], scale[step])
            ring = rings[parity][step]
            weigh(place, blocks, pairs, keys, weights, SCALE_T, causal, ring, now, sums)

    def steps(turn, carry):
        for parity in range(2):
            pl.when(turn & 1 == parity)(functools.partial(half, turn, parity))
        return carry

    turns = (count + LAG + UNROLL - 1) // UNROLL
    lax.fori_loop(0, turns, steps, 0)
    for turn in range(AHEAD):
        for step in range(UNROLL):
            fetch(turns + turn, step).wait()

    def finish(block, carry):
        out[block] = grad[block, :, :rows].astype(bf16)
        return carry

    lax.fori_loop(0, blocks, finish, 0, unroll=8)


def relation_gradient(slabs, segments, made, scales, features, pairs, count):
    blocks, _, wide = slabs.shape
    rows = made.shape[1]
    vmem = pl.BlockSpec(memory_space=pltpu.VMEM)
    smem = pl.BlockSpec(memory_space=pltpu.SMEM)
    ring = pltpu.VMEM((SLOTS, rows, wide), f32)
    return pl.pallas_call(
        functools.partial(gradient_kernel, blocks),
        out_shape=jax.ShapeDtypeStruct((blocks, WS, rows), bf16),
        in_specs=[smem, smem, vmem, vmem, pl.BlockSpec(memory_space=pl.ANY), vmem, vmem],
        out_specs=vmem,
        scratch_shapes=[
            pltpu.VMEM((blocks, rows, DEPTH), bf16),
            pltpu.VMEM((blocks, DEPTH, wide), bf16),
            [[pltpu.VMEM((2, rows, wide), f32)] * UNROLL] * 2,
            [ring] * UNROLL,
            pltpu.VMEM((2, rows, wide), f32),
            pltpu.VMEM((blocks + 1, 8, wide), f32),
            pltpu.VMEM((blocks + 1, WS, wide), f32),
            pltpu.SemaphoreType.DMA((UNROLL, SLOTS)),
        ],
        compiler_params=pltpu.CompilerParams(vmem_limit_bytes=48 * MIB),
        cost_estimate=pl.CostEstimate(
            flops=20_000_000_000, bytes_accessed=80_000_000, transcendentals=20_000_000
        ),
        name="relation_gradient",
    )(count, pairs, segments, slabs, made, scales, features)


def head_gradient(student, teacher, segment_ids, rows):
    blocks, _, wide = student.shape
    ends = jnp.stack([segment_ids[::rows], segment_ids[rows - 1 :: rows]])
    segments = jnp.pad(
        segment_ids.reshape(blocks, rows), ((0, 0), (0, wide - rows)), constant_values=-1
    )
    made, scales, features, pairs, count = student_weights(student, ends, segments, rows)
    return relation_gradient(teacher, segments, made, scales, features, pairs, count)


def unproject_kernel(part, grads, wq, wk, out):
    half = grads.shape[0] // 2
    rows, wide = grads.shape[2], round_up(grads.shape[2], 128)
    total = jnp.zeros((wq.shape[0], wide), f32)
    for rel, weight in enumerate((wq, wk)):
        turned = grads[rel * half : (rel + 1) * half].reshape(half * WS, rows)
        turned = jnp.concatenate([turned, jnp.zeros((half * WS, wide - rows), bf16)], axis=1)
        total += jnp.dot(weight[...], turned, preferred_element_type=f32)
    out[...] = total.T[:rows].astype(out.dtype)


def unproject(part, grads, wq, wk, dtype):
    rows = grads.shape[2]
    width = wq.shape[0] // 2
    tile = 256
    steps = width // tile

    def weight_block(i, part):
        return part[0] * steps + i, 0

    weight = pl.BlockSpec((tile, wq.shape[1]), weight_block)
    return pl.pallas_call(
        unproject_kernel,
        grid_spec=pltpu.PrefetchScalarGridSpec(
            num_scalar_prefetch=1,
            grid=(steps,),
            in_specs=[pl.BlockSpec(grads.shape, lambda i, part: (0, 0, 0)), weight, weight],
            out_specs=pl.BlockSpec((rows, tile), lambda i, part: (0, i)),
        ),
        out_shape=jax.ShapeDtypeStruct((rows, width), dtype),
        compiler_params=pltpu.CompilerParams(vmem_limit_bytes=56 * MIB),
        cost_estimate=pl.CostEstimate(
            flops=4 * rows * width * wq.shape[1], bytes_accessed=6_000_000, transcendentals=0
        ),
        name="unproject",
    )(part[None], grads, wq, wk)


def shards(teacher_query, teacher_key, student_hidden, w_query, w_key, segment_ids, block_mask):
    rows = student_hidden.shape[0]
    student = project(student_hidden, w_query, w_key, block_mask)
    teacher = turn(teacher_query, teacher_key)
    student = lax.all_to_all(student.reshape(-1, *student.shape[2:]), "ctx", 0, 0, tiled=True)
    teacher = lax.all_to_all(teacher.reshape(-1, *teacher.shape[2:]), "ctx", 0, 0, tiled=True)
    turned = head_gradient(student, teacher, segment_ids, rows)
    back = lax.all_to_all(turned, "ctx", 0, 0, tiled=True)
    side = lax.axis_index("head")
    away = unproject(1 - side, back, w_query, w_key, bf16)
    away = lax.ppermute(away, "head", [(0, 1), (1, 0)])
    own = unproject(side, back, w_query, w_key, f32)
    return (own + away).astype(bf16)


def solution(mesh):
    placed = (
        P("ctx", "head"),
        P("ctx", "head"),
        P("ctx", None),
        P(None, "head"),
        P(None, "head"),
        P(),
        P("ctx", None),
    )
    return jax.shard_map(
        shards, mesh=mesh, in_specs=placed, out_specs=P("ctx", "head"), check_vma=False
    )
```

```python
import functools
import math

import jax
import jax.numpy as jnp
from jax import lax
from jax.experimental import pallas as pl
from jax.experimental.pallas import tpu as pltpu
from jax.sharding import PartitionSpec as P

DT = 5120
DS = 2048
HEADS = 64
REACH = 8
WT = DT // HEADS
WS = DS // HEADS
DEPTH = 128
EXTRA = 16
DOCS = 4
PACK = 8
LISTED = 8
UNROLL = 4
LAG = 3 * UNROLL
SLOTS = 4
AHEAD = 2
LIST = 640
HIDDEN = 1e30
LOG2E = math.log2(math.e)
SCALE_T = LOG2E / math.sqrt(WT)
SCALE_S = LOG2E / math.sqrt(WS)
SAFE = 90.0
MIB = 1024 * 1024
f32 = jnp.float32
bf16 = jnp.bfloat16


def round_up(value, unit):
    return (value + unit - 1) // unit * unit


def project_kernel(mask, hidden, wq, wk, out):
    rows, wide = hidden.shape[0], out.shape[-1]
    row = lax.broadcasted_iota(jnp.int32, (wide - rows, PACK * WS), 0)
    extra = jnp.zeros(row.shape, f32)
    for back in range(REACH - 1):
        extra = jnp.where(row == back, mask[0, back].astype(f32), extra)
    extra = extra.astype(bf16)
    for rel, weight in enumerate((wq, wk)):
        student = jnp.dot(hidden[...], weight[...], preferred_element_type=f32).astype(bf16)
        turned = jnp.concatenate([student, extra], axis=0).T
        out[rel] = turned.reshape(out.shape[1:])


def project(hidden, wq, wk, mask):
    rows = hidden.shape[0]
    wide = round_up(rows, 128)
    heads = wq.shape[1] // WS
    return pl.pallas_call(
        project_kernel,
        grid=(heads // PACK,),
        out_shape=jax.ShapeDtypeStruct((2, heads, WS, wide), bf16),
        in_specs=[
            pl.BlockSpec(memory_space=pltpu.SMEM),
            pl.BlockSpec((rows, DS), lambda i: (0, 0)),
            pl.BlockSpec((DS, PACK * WS), lambda i: (0, i)),
            pl.BlockSpec((DS, PACK * WS), lambda i: (0, i)),
        ],
        out_specs=pl.BlockSpec((2, PACK, WS, wide), lambda i: (0, i, 0, 0)),
        compiler_params=pltpu.CompilerParams(vmem_limit_bytes=56 * MIB),
        cost_estimate=pl.CostEstimate(
            flops=4 * rows * DS * heads * WS, bytes_accessed=10_000_000, transcendentals=0
        ),
        name="project_student",
    )(mask, hidden, wq, wk)


def turn_kernel(tq, tk, out):
    rows = tq.shape[0]
    wide = out.shape[-1]
    for rel, teacher in enumerate((tq, tk)):
        zeros = jnp.zeros((wide - rows, teacher.shape[1]), bf16)
        turned = jnp.concatenate([teacher[...], zeros], axis=0).T
        out[rel] = turned.reshape(out.shape[1:])


def turn(tq, tk):
    rows, columns = tq.shape
    wide = round_up(rows, 128)
    heads = columns // WT
    return pl.pallas_call(
        turn_kernel,
        grid=(heads // PACK,),
        out_shape=jax.ShapeDtypeStruct((2, heads, WT, wide), bf16),
        in_specs=[pl.BlockSpec((rows, PACK * WT), lambda i: (0, i))] * 2,
        out_specs=pl.BlockSpec((2, PACK, WT, wide), lambda i: (0, i, 0, 0)),
        compiler_params=pltpu.CompilerParams(vmem_limit_bytes=56 * MIB),
        cost_estimate=pl.CostEstimate(flops=0, bytes_accessed=5_000_000, transcendentals=0),
        name="turn_teacher",
    )(tq, tk)


def read_pair(pairs, place):
    code = pairs[place]
    return code & 255, (code >> 8) & 255, code >> 16


def fill(block, slab, segments, keys, weights):
    width, wide = slab.shape
    rows = keys.shape[1]
    row = lax.broadcasted_iota(jnp.int32, (EXTRA, wide), 0)
    lane = lax.broadcasted_iota(jnp.int32, (EXTRA, wide), 1)
    hot = jnp.where(row == segments[pl.ds(block, 1)], 1.0, 0.0)
    key_extra = jnp.where((row >= DOCS) & (row < DOCS + 3), 1.0, hot)
    query_extra = jnp.where((row < DOCS) & (lane < rows), (hot - 1.0) * HIDDEN, 0.0)
    zeros = jnp.zeros((DEPTH - EXTRA - width, wide), bf16)
    weights[block] = jnp.concatenate([slab, query_extra.astype(bf16), zeros], axis=0)
    keys[block] = jnp.concatenate([slab, key_extra.astype(bf16), zeros], axis=0).T[:rows]
    values = slab.astype(f32)
    return jnp.sum(values * values, axis=0, keepdims=True)


def subtract_maxima(width, blocks, count, pairs, keys, weights, causal, sums):
    rows, wide = causal.shape[1:]

    def raise_maxima(place, carry):
        query, key, diagonal = read_pair(pairs, place + LAG)
        scores = jnp.dot(keys[key], weights[query], preferred_element_type=f32)
        scores = scores + causal[diagonal]
        top = jnp.max(scores.reshape(rows // 8, 8, wide), axis=0)
        sums[query] = jnp.where(diagonal == 1, top, jnp.maximum(top, sums[query]))
        return carry

    lax.fori_loop(0, count, raise_maxima, 0)
    row = lax.broadcasted_iota(jnp.int32, (EXTRA, wide), 0)

    def set_maxima(block, carry):
        rest = jnp.max(sums[block], axis=0, keepdims=True)
        extra = weights[block, width : width + EXTRA].astype(f32)
        for part in range(3):
            piece = rest.astype(bf16).astype(f32)
            rest = rest - piece
            extra = jnp.where(row == DOCS + part, -piece, extra)
        weights[block, width : width + EXTRA] = extra.astype(bf16)
        return carry

    lax.fori_loop(0, blocks, set_maxima, 0)


def fill_causal(causal):
    shape = causal.shape[1:]
    key_at = lax.broadcasted_iota(jnp.int32, shape, 0)
    query_at = lax.broadcasted_iota(jnp.int32, shape, 1)
    causal[0] = jnp.zeros(shape, f32)
    causal[1] = jnp.where(key_at <= query_at, 0.0, -HIDDEN)


def halves(rows):
    return (0, 128), (128, rows)


def weigh(place, blocks, pairs, keys, weights, scale, causal, ring, slot, sums):
    query, key, diagonal = read_pair(pairs, place + LAG)
    rows, wide = causal.shape[1:]
    key_block = jnp.minimum(key, blocks - 1)
    operand = weights[jnp.minimum(query, blocks - 1)]
    part = jnp.where(diagonal == 1, 0.0, sums[query])
    for low, high in halves(rows):
        scores = jnp.dot(keys[key_block, low:high], operand, preferred_element_type=f32)
        made = jnp.exp2(scores * scale + causal[diagonal, low:high])
        ring[slot, low:high] = made
        part += jnp.sum(made.reshape((high - low) // 8, 8, wide), axis=0)
    sums[query] = part


def student_kernel(
    blocks, ends, segments, slabs, made, scales, features, pairs, count_out, keys, weights, rings, causal, sums, seen, opened, sem, sems
):
    rows, wide = causal.shape[1:]
    fill_causal(causal)

    def look(block, carry):
        seen[pl.ds(block, 1)] = slabs[block, :16, wide - 128 :].astype(f32)[:1].astype(jnp.int32)
        return carry

    lax.fori_loop(0, blocks, look, 0, unroll=8)
    fetch = pltpu.make_async_copy(seen, opened, sem)
    fetch.start()
    fetch.wait()
    mask_lane = rows % 128

    def list_pairs(block, total):
        for back in range(REACH):
            key = jnp.maximum(block - back, 0)
            code = block | (key << 8)
            if back == 0:
                pairs[total + LAG] = code | (1 << 16)
                total = total + 1
            else:
                pairs[total + LAG] = code
                is_open = (block >= back) & (opened[block, mask_lane + back - 1] == 1)
                is_open = is_open & (ends[0, block] == ends[1, key])
                total = total + is_open.astype(jnp.int32)
        return total

    lane = lax.broadcasted_iota(jnp.int32, (WS, wide), 1)

    def prepare(block, carry):
        peak, total = carry
        total = list_pairs(block, total)
        slab = jnp.where(lane < rows, slabs[block].astype(f32), 0.0).astype(bf16)
        features[block] = slab
        return jnp.maximum(peak, fill(block, slab, segments, keys, weights)), total

    peak, count = lax.fori_loop(0, blocks, prepare, (jnp.zeros((1, wide), f32), 0), unroll=4)
    count_out[0] = count
    for place in range(LAG):
        pairs[place] = blocks | (blocks << 8)
    for place in range(LAG + LISTED):
        pairs[count + LAG + place] = blocks | (blocks << 8)

    @pl.when(jnp.logical_not(jnp.max(peak) * SCALE_S <= SAFE))
    def _():
        subtract_maxima(WS, blocks, count, pairs, keys, weights, causal, sums)

    def send(place, step, slot):
        return pltpu.make_async_copy(rings[step].at[slot], made.at[place], sems.at[step, slot])

    def steps(turn, carry):
        slot = turn & (SLOTS - 1)

        @pl.when(turn >= SLOTS)
        def _():
            for step in range(LISTED):
                send(LISTED * turn + step, step, slot).wait()

        for step in range(LISTED):
            place = LISTED * turn + step
            weigh(place, blocks, pairs, keys, weights, SCALE_S, causal, rings[step], slot, sums)
        for step in range(LISTED):
            send(LISTED * turn + step, step, slot).start()
        return carry

    turns = (count + LISTED - 1) // LISTED
    lax.fori_loop(0, turns, steps, 0)

    def drain(turn, carry):
        for step in range(LISTED):
            send(LISTED * turn + step, step, turn & (SLOTS - 1)).wait()
        return carry

    lax.fori_loop(jnp.maximum(turns - SLOTS, 0), turns, drain, 0)

    def finish(block, carry):
        total = jnp.sum(sums[block], axis=0, keepdims=True) * math.sqrt(WS)
        scales[block] = jnp.broadcast_to(1.0 / total, (8, wide))
        return carry

    lax.fori_loop(0, blocks, finish, 0, unroll=8)


def student_weights(slabs, ends, segments, rows):
    blocks, _, wide = slabs.shape
    vmem = pl.BlockSpec(memory_space=pltpu.VMEM)
    smem = pl.BlockSpec(memory_space=pltpu.SMEM)
    ring = pltpu.VMEM((SLOTS, rows, wide), f32)
    return pl.pallas_call(
        functools.partial(student_kernel, blocks),
        out_shape=(
            jax.ShapeDtypeStruct((blocks * REACH, rows, wide), f32),
            jax.ShapeDtypeStruct((blocks, 8, wide), f32),
            jax.ShapeDtypeStruct((blocks, WS, wide), bf16),
            jax.ShapeDtypeStruct((LIST,), jnp.int32),
            jax.ShapeDtypeStruct((1,), jnp.int32),
        ),
        in_specs=[smem, vmem, vmem],
        out_specs=(pl.BlockSpec(memory_space=pl.ANY), vmem, vmem, smem, smem),
        scratch_shapes=[
            pltpu.VMEM((blocks, rows, DEPTH), bf16),
            pltpu.VMEM((blocks, DEPTH, wide), bf16),
            [ring] * LISTED,
            pltpu.VMEM((2, rows, wide), f32),
            pltpu.VMEM((blocks + 1, 8, wide), f32),
            pltpu.VMEM((blocks, 128), jnp.int32),
            pltpu.SMEM((blocks, 128), jnp.int32),
            pltpu.SemaphoreType.DMA,
            pltpu.SemaphoreType.DMA((LISTED, SLOTS)),
        ],
        compiler_params=pltpu.CompilerParams(vmem_limit_bytes=48 * MIB),
        cost_estimate=pl.CostEstimate(
            flops=10_000_000_000, bytes_accessed=80_000_000, transcendentals=20_000_000
        ),
        name="student_weights",
    )(ends, segments, slabs)


def gradient_kernel(
    blocks, count_in, pairs, segments, slabs, made, scales, features, out, keys, weights, rings, fetched, causal, sums, grad, sems
):
    rows, wide = causal.shape[1:]
    count = count_in[0]
    fill_causal(causal)

    def fetch(turn, step):
        pair = jnp.clip(UNROLL * turn + step - LAG, 0, made.shape[0] - 1)
        slot = turn & (SLOTS - 1)
        return pltpu.make_async_copy(made.at[pair], fetched[step].at[slot], sems.at[step, slot])

    for turn in range(AHEAD):
        for step in range(UNROLL):
            fetch(turn, step).start()

    def prepare(block, peak):
        grad[block] = jnp.zeros((WS, wide), f32)
        return jnp.maximum(peak, fill(block, slabs[block], segments, keys, weights))

    peak = lax.fori_loop(0, blocks, prepare, jnp.zeros((1, wide), f32), unroll=4)

    @pl.when(jnp.logical_not(jnp.max(peak) * SCALE_T <= SAFE))
    def _():
        subtract_maxima(WT, blocks, count, pairs, keys, weights, causal, sums)

    def readable(block):
        return jnp.minimum(block, blocks - 1)

    def inverses(place):
        query, _, _ = read_pair(pairs, place)
        total = jnp.sum(sums[query], axis=0, keepdims=True) * math.sqrt(WS)
        return 1.0 / total, scales[readable(query), :1]

    def couple(place, teacher, student, scale):
        query, key, _ = read_pair(pairs, place)
        query_side = features[readable(query)]
        to_queries = jnp.zeros((WS, wide), f32)
        for low, high in halves(rows):
            coupling = student[low:high] * scale[1] - teacher[low:high] * scale[0]
            coupling = coupling.astype(bf16)
            key_side = features[readable(key), :, low:high]
            grad[key, :, low:high] += lax.dot_general(
                query_side, coupling, (((1,), (1,)), ((), ())), preferred_element_type=f32
            )
            to_queries += jnp.dot(key_side, coupling, preferred_element_type=f32)
        grad[query] += to_queries

    def half(turn, parity):
        slot = turn & (SLOTS - 1)
        for step in range(UNROLL):
            fetch(turn, step).wait()
        for step in range(UNROLL):
            fetch(turn + AHEAD, step).start()
        scale = [inverses(UNROLL * turn + step) for step in range(UNROLL)]
        now = turn // 2 & 1
        before = (turn - LAG // UNROLL) // 2 & 1
        for step in range(UNROLL):
            place = UNROLL * turn + step
            old = rings[1 - parity][step].at[before]
            couple(place, old, fetched[step].at[slot], scale[step])
            ring = rings[parity][step]
            weigh(place, blocks, pairs, keys, weights, SCALE_T, causal, ring, now, sums)

    def steps(turn, carry):
        for parity in range(2):
            pl.when(turn & 1 == parity)(functools.partial(half, turn, parity))
        return carry

    turns = (count + LAG + UNROLL - 1) // UNROLL
    lax.fori_loop(0, turns, steps, 0)
    for turn in range(AHEAD):
        for step in range(UNROLL):
            fetch(turns + turn, step).wait()

    def finish(block, carry):
        out[block] = grad[block].astype(bf16)
        return carry

    lax.fori_loop(0, blocks, finish, 0, unroll=8)


def relation_gradient(slabs, segments, made, scales, features, pairs, count):
    blocks, _, wide = slabs.shape
    rows = made.shape[1]
    vmem = pl.BlockSpec(memory_space=pltpu.VMEM)
    smem = pl.BlockSpec(memory_space=pltpu.SMEM)
    ring = pltpu.VMEM((SLOTS, rows, wide), f32)
    return pl.pallas_call(
        functools.partial(gradient_kernel, blocks),
        out_shape=jax.ShapeDtypeStruct((blocks, WS, wide), bf16),
        in_specs=[smem, smem, vmem, vmem, pl.BlockSpec(memory_space=pl.ANY), vmem, vmem],
        out_specs=vmem,
        scratch_shapes=[
            pltpu.VMEM((blocks, rows, DEPTH), bf16),
            pltpu.VMEM((blocks, DEPTH, wide), bf16),
            [[pltpu.VMEM((2, rows, wide), f32)] * UNROLL] * 2,
            [ring] * UNROLL,
            pltpu.VMEM((2, rows, wide), f32),
            pltpu.VMEM((blocks + 1, 8, wide), f32),
            pltpu.VMEM((blocks + 1, WS, wide), f32),
            pltpu.SemaphoreType.DMA((UNROLL, SLOTS)),
        ],
        compiler_params=pltpu.CompilerParams(vmem_limit_bytes=48 * MIB),
        cost_estimate=pl.CostEstimate(
            flops=20_000_000_000, bytes_accessed=80_000_000, transcendentals=20_000_000
        ),
        name="relation_gradient",
    )(count, pairs, segments, slabs, made, scales, features)


def head_gradient(student, teacher, segment_ids, rows):
    blocks, _, wide = student.shape
    ends = jnp.stack([segment_ids[::rows], segment_ids[rows - 1 :: rows]])
    segments = jnp.pad(
        segment_ids.reshape(blocks, rows), ((0, 0), (0, wide - rows)), constant_values=-1
    )
    made, scales, features, pairs, count = student_weights(student, ends, segments, rows)
    return relation_gradient(teacher, segments, made, scales, features, pairs, count)


def unproject_kernel(part, grads, wq, wk, out, held, sems):
    half = grads.shape[0] // 2
    rows, width = out.shape
    pieces = held.shape[1]
    size = width // pieces
    copies = []
    for rel, weight in enumerate((wq, wk)):
        for piece in range(pieces):
            first = pl.multiple_of(part[0] * width + piece * size, size)
            copies.append(
                pltpu.make_async_copy(
                    weight.at[pl.ds(first, size)], held.at[rel, piece], sems.at[rel, piece]
                )
            )
            copies[-1].start()
    total = jnp.zeros((width, grads.shape[2]), f32)
    for rel in range(2):
        turned = grads[rel * half : (rel + 1) * half].reshape(half * WS, grads.shape[2])
        for piece in range(pieces):
            copies[rel * pieces + piece].wait()
        weight = held[rel].reshape(width, half * WS)
        total += jnp.dot(weight, turned, preferred_element_type=f32)
    out[...] = total.T[:rows].astype(out.dtype)


def unproject(part, grads, wq, wk, rows, dtype):
    width = wq.shape[0] // 2
    vmem = pl.BlockSpec(memory_space=pltpu.VMEM)
    hbm = pl.BlockSpec(memory_space=pl.ANY)
    return pl.pallas_call(
        unproject_kernel,
        in_specs=[pl.BlockSpec(memory_space=pltpu.SMEM), vmem, hbm, hbm],
        out_specs=vmem,
        scratch_shapes=[
            pltpu.VMEM((2, 4, width // 4, wq.shape[1]), bf16),
            pltpu.SemaphoreType.DMA((2, 4)),
        ],
        out_shape=jax.ShapeDtypeStruct((rows, width), dtype),
        compiler_params=pltpu.CompilerParams(vmem_limit_bytes=56 * MIB),
        cost_estimate=pl.CostEstimate(
            flops=4 * rows * width * wq.shape[1], bytes_accessed=6_000_000, transcendentals=0
        ),
        name="unproject",
    )(part[None], grads, wq, wk)


def shards(teacher_query, teacher_key, student_hidden, w_query, w_key, segment_ids, block_mask):
    rows = student_hidden.shape[0]
    student = project(student_hidden, w_query, w_key, block_mask)
    teacher = turn(teacher_query, teacher_key)
    student = lax.all_to_all(student.reshape(-1, *student.shape[2:]), "ctx", 0, 0, tiled=True)
    teacher = lax.all_to_all(teacher.reshape(-1, *teacher.shape[2:]), "ctx", 0, 0, tiled=True)
    turned = head_gradient(student, teacher, segment_ids, rows)
    back = lax.all_to_all(turned, "ctx", 0, 0, tiled=True)
    side = lax.axis_index("head")
    away = unproject(1 - side, back, w_query, w_key, rows, bf16)
    away = lax.ppermute(away, "head", [(0, 1), (1, 0)])
    own = unproject(side, back, w_query, w_key, rows, f32)
    return (own + away).astype(bf16)


def solution(mesh):
    placed = (
        P("ctx", "head"),
        P("ctx", "head"),
        P("ctx", None),
        P(None, "head"),
        P(None, "head"),
        P(),
        P("ctx", None),
    )
    return jax.shard_map(
        shards, mesh=mesh, in_specs=placed, out_specs=P("ctx", "head"), check_vma=False
    )
```

```python
import functools
import math

import jax
import jax.numpy as jnp
from jax import lax
from jax.experimental import pallas as pl
from jax.experimental.pallas import tpu as pltpu
from jax.sharding import PartitionSpec as P

DT = 5120
DS = 2048
HEADS = 64
REACH = 8
WT = DT // HEADS
WS = DS // HEADS
DEPTH = 128
EXTRA = 16
DOCS = 4
PACK = 8
LISTED = 8
UNROLL = 4
LAG = 3 * UNROLL
SLOTS = 4
AHEAD = 2
LIST = 640
HIDDEN = 1e30
SCALE_T = 1.0 / math.sqrt(WT)
SCALE_S = 1.0 / math.sqrt(WS)
SAFE = 60.0
MIB = 1024 * 1024
f32 = jnp.float32
bf16 = jnp.bfloat16


def round_up(value, unit):
    return (value + unit - 1) // unit * unit


def project_kernel(mask, hidden, wq, wk, out):
    rows, wide = hidden.shape[0], out.shape[-1]
    row = lax.broadcasted_iota(jnp.int32, (wide - rows, PACK * WS), 0)
    extra = jnp.zeros(row.shape, f32)
    for back in range(REACH - 1):
        extra = jnp.where(row == back, mask[0, back].astype(f32), extra)
    extra = extra.astype(bf16)
    for rel, weight in enumerate((wq, wk)):
        student = jnp.dot(hidden[...], weight[...], preferred_element_type=f32).astype(bf16)
        turned = jnp.concatenate([student, extra], axis=0).T
        out[rel] = turned.reshape(out.shape[1:])


def project(hidden, wq, wk, mask):
    rows = hidden.shape[0]
    wide = round_up(rows, 128)
    heads = wq.shape[1] // WS
    return pl.pallas_call(
        project_kernel,
        grid=(heads // PACK,),
        out_shape=jax.ShapeDtypeStruct((2, heads, WS, wide), bf16),
        in_specs=[
            pl.BlockSpec(memory_space=pltpu.SMEM),
            pl.BlockSpec((rows, DS), lambda i: (0, 0)),
            pl.BlockSpec((DS, PACK * WS), lambda i: (0, i)),
            pl.BlockSpec((DS, PACK * WS), lambda i: (0, i)),
        ],
        out_specs=pl.BlockSpec((2, PACK, WS, wide), lambda i: (0, i, 0, 0)),
        compiler_params=pltpu.CompilerParams(vmem_limit_bytes=56 * MIB),
        cost_estimate=pl.CostEstimate(
            flops=4 * rows * DS * heads * WS, bytes_accessed=10_000_000, transcendentals=0
        ),
        name="project_student",
    )(mask, hidden, wq, wk)


def turn_kernel(tq, tk, out):
    rows = tq.shape[0]
    wide = out.shape[-1]
    for rel, teacher in enumerate((tq, tk)):
        zeros = jnp.zeros((wide - rows, teacher.shape[1]), bf16)
        turned = jnp.concatenate([teacher[...], zeros], axis=0).T
        out[rel] = turned.reshape(out.shape[1:])


def turn(tq, tk):
    rows, columns = tq.shape
    wide = round_up(rows, 128)
    heads = columns // WT
    return pl.pallas_call(
        turn_kernel,
        grid=(heads // PACK,),
        out_shape=jax.ShapeDtypeStruct((2, heads, WT, wide), bf16),
        in_specs=[pl.BlockSpec((rows, PACK * WT), lambda i: (0, i))] * 2,
        out_specs=pl.BlockSpec((2, PACK, WT, wide), lambda i: (0, i, 0, 0)),
        compiler_params=pltpu.CompilerParams(vmem_limit_bytes=56 * MIB),
        cost_estimate=pl.CostEstimate(flops=0, bytes_accessed=5_000_000, transcendentals=0),
        name="turn_teacher",
    )(tq, tk)


def read_pair(pairs, place):
    code = pairs[place]
    return code & 255, (code >> 8) & 255, code >> 16


def fill(block, slab, segments, keys, weights):
    width, wide = slab.shape
    rows = keys.shape[1]
    row = lax.broadcasted_iota(jnp.int32, (EXTRA, wide), 0)
    lane = lax.broadcasted_iota(jnp.int32, (EXTRA, wide), 1)
    hot = jnp.where(row == segments[pl.ds(block, 1)], 1.0, 0.0)
    key_extra = jnp.where((row >= DOCS) & (row < DOCS + 3), 1.0, hot)
    query_extra = jnp.where((row < DOCS) & (lane < rows), (hot - 1.0) * HIDDEN, 0.0)
    zeros = jnp.zeros((DEPTH - EXTRA - width, wide), bf16)
    weights[block] = jnp.concatenate([slab, query_extra.astype(bf16), zeros], axis=0)
    keys[block] = jnp.concatenate([slab, key_extra.astype(bf16), zeros], axis=0).T[:rows]
    values = slab.astype(f32)
    return jnp.sum(values * values, axis=0, keepdims=True)


def subtract_maxima(width, blocks, count, pairs, keys, weights, causal, sums):
    rows, wide = causal.shape[1:]

    def raise_maxima(place, carry):
        query, key, diagonal = read_pair(pairs, place + LAG)
        scores = jnp.dot(keys[key], weights[query], preferred_element_type=f32)
        scores = scores + causal[diagonal]
        top = jnp.max(scores.reshape(rows // 8, 8, wide), axis=0)
        sums[query] = jnp.where(diagonal == 1, top, jnp.maximum(top, sums[query]))
        return carry

    lax.fori_loop(0, count, raise_maxima, 0)
    row = lax.broadcasted_iota(jnp.int32, (EXTRA, wide), 0)

    def set_maxima(block, carry):
        rest = jnp.max(sums[block], axis=0, keepdims=True)
        extra = weights[block, width : width + EXTRA].astype(f32)
        for part in range(3):
            piece = rest.astype(bf16).astype(f32)
            rest = rest - piece
            extra = jnp.where(row == DOCS + part, -piece, extra)
        weights[block, width : width + EXTRA] = extra.astype(bf16)
        return carry

    lax.fori_loop(0, blocks, set_maxima, 0)


def fill_causal(causal):
    shape = causal.shape[1:]
    key_at = lax.broadcasted_iota(jnp.int32, shape, 0)
    query_at = lax.broadcasted_iota(jnp.int32, shape, 1)
    causal[0] = jnp.zeros(shape, f32)
    causal[1] = jnp.where(key_at <= query_at, 0.0, -HIDDEN)


def halves(rows):
    return (0, 128), (128, rows)


def weigh(place, blocks, pairs, keys, weights, scale, causal, ring, slot, sums):
    query, key, diagonal = read_pair(pairs, place + LAG)
    rows, wide = causal.shape[1:]
    key_block = jnp.minimum(key, blocks - 1)
    operand = weights[jnp.minimum(query, blocks - 1)]
    part = jnp.where(diagonal == 1, 0.0, sums[query])
    for low, high in halves(rows):
        scores = jnp.dot(keys[key_block, low:high], operand, preferred_element_type=f32)
        made = jnp.exp(scores * scale + causal[diagonal, low:high])
        ring[slot, low:high] = made
        part += jnp.sum(made.reshape((high - low) // 8, 8, wide), axis=0)
    sums[query] = part


def student_kernel(
    blocks, ends, segments, slabs, made, scales, features, pairs, count_out, keys, weights, rings, causal, sums, seen, opened, sem, sems
):
    rows, wide = causal.shape[1:]
    fill_causal(causal)

    def look(block, carry):
        seen[pl.ds(block, 1)] = slabs[block, :16, wide - 128 :].astype(f32)[:1].astype(jnp.int32)
        return carry

    lax.fori_loop(0, blocks, look, 0, unroll=8)
    fetch = pltpu.make_async_copy(seen, opened, sem)
    fetch.start()
    fetch.wait()
    mask_lane = rows % 128

    def list_pairs(block, total):
        for back in range(REACH):
            key = jnp.maximum(block - back, 0)
            code = block | (key << 8)
            if back == 0:
                pairs[total + LAG] = code | (1 << 16)
                total = total + 1
            else:
                pairs[total + LAG] = code
                is_open = (block >= back) & (opened[block, mask_lane + back - 1] == 1)
                is_open = is_open & (ends[0, block] == ends[1, key])
                total = total + is_open.astype(jnp.int32)
        return total

    lane = lax.broadcasted_iota(jnp.int32, (WS, wide), 1)

    def prepare(block, carry):
        peak, total = carry
        total = list_pairs(block, total)
        slab = jnp.where(lane < rows, slabs[block].astype(f32), 0.0).astype(bf16)
        features[block] = slab
        return jnp.maximum(peak, fill(block, slab, segments, keys, weights)), total

    peak, count = lax.fori_loop(0, blocks, prepare, (jnp.zeros((1, wide), f32), 0), unroll=4)
    count_out[0] = count
    for place in range(LAG):
        pairs[place] = blocks | (blocks << 8)
    for place in range(LAG + LISTED):
        pairs[count + LAG + place] = blocks | (blocks << 8)

    @pl.when(jnp.logical_not(jnp.max(peak) * SCALE_S <= SAFE))
    def _():
        subtract_maxima(WS, blocks, count, pairs, keys, weights, causal, sums)

    def send(place, step, slot):
        return pltpu.make_async_copy(rings[step].at[slot], made.at[place], sems.at[step, slot])

    def steps(turn, carry):
        slot = turn & (SLOTS - 1)

        @pl.when(turn >= SLOTS)
        def _():
            for step in range(LISTED):
                send(LISTED * turn + step, step, slot).wait()

        for step in range(LISTED):
            place = LISTED * turn + step
            weigh(place, blocks, pairs, keys, weights, SCALE_S, causal, rings[step], slot, sums)
        for step in range(LISTED):
            send(LISTED * turn + step, step, slot).start()
        return carry

    turns = (count + LISTED - 1) // LISTED
    lax.fori_loop(0, turns, steps, 0)

    def drain(turn, carry):
        for step in range(LISTED):
            send(LISTED * turn + step, step, turn & (SLOTS - 1)).wait()
        return carry

    lax.fori_loop(jnp.maximum(turns - SLOTS, 0), turns, drain, 0)

    def finish(block, carry):
        total = jnp.sum(sums[block], axis=0, keepdims=True) * math.sqrt(WS)
        scales[block] = jnp.broadcast_to(1.0 / total, (8, wide))
        return carry

    lax.fori_loop(0, blocks, finish, 0, unroll=8)


def student_weights(slabs, ends, segments, rows):
    blocks, _, wide = slabs.shape
    vmem = pl.BlockSpec(memory_space=pltpu.VMEM)
    smem = pl.BlockSpec(memory_space=pltpu.SMEM)
    ring = pltpu.VMEM((SLOTS, rows, wide), f32)
    return pl.pallas_call(
        functools.partial(student_kernel, blocks),
        out_shape=(
            jax.ShapeDtypeStruct((blocks * REACH, rows, wide), f32),
            jax.ShapeDtypeStruct((blocks, 8, wide), f32),
            jax.ShapeDtypeStruct((blocks, WS, wide), bf16),
            jax.ShapeDtypeStruct((LIST,), jnp.int32),
            jax.ShapeDtypeStruct((1,), jnp.int32),
        ),
        in_specs=[smem, vmem, vmem],
        out_specs=(pl.BlockSpec(memory_space=pl.ANY), vmem, vmem, smem, smem),
        scratch_shapes=[
            pltpu.VMEM((blocks, rows, DEPTH), bf16),
            pltpu.VMEM((blocks, DEPTH, wide), bf16),
            [ring] * LISTED,
            pltpu.VMEM((2, rows, wide), f32),
            pltpu.VMEM((blocks + 1, 8, wide), f32),
            pltpu.VMEM((blocks, 128), jnp.int32),
            pltpu.SMEM((blocks, 128), jnp.int32),
            pltpu.SemaphoreType.DMA,
            pltpu.SemaphoreType.DMA((LISTED, SLOTS)),
        ],
        compiler_params=pltpu.CompilerParams(vmem_limit_bytes=48 * MIB),
        cost_estimate=pl.CostEstimate(
            flops=10_000_000_000, bytes_accessed=80_000_000, transcendentals=20_000_000
        ),
        name="student_weights",
    )(ends, segments, slabs)


def gradient_kernel(
    blocks, count_in, pairs, segments, slabs, made, scales, features, out, keys, weights, rings, fetched, causal, sums, grad, sems
):
    rows, wide = causal.shape[1:]
    count = count_in[0]
    fill_causal(causal)

    def fetch(turn, step):
        pair = jnp.clip(UNROLL * turn + step - LAG, 0, made.shape[0] - 1)
        slot = turn & (SLOTS - 1)
        return pltpu.make_async_copy(made.at[pair], fetched[step].at[slot], sems.at[step, slot])

    for turn in range(AHEAD):
        for step in range(UNROLL):
            fetch(turn, step).start()

    def prepare(block, peak):
        grad[block] = jnp.zeros((WS, wide), f32)
        return jnp.maximum(peak, fill(block, slabs[block], segments, keys, weights))

    peak = lax.fori_loop(0, blocks, prepare, jnp.zeros((1, wide), f32), unroll=4)

    @pl.when(jnp.logical_not(jnp.max(peak) * SCALE_T <= SAFE))
    def _():
        subtract_maxima(WT, blocks, count, pairs, keys, weights, causal, sums)

    def readable(block):
        return jnp.minimum(block, blocks - 1)

    def inverses(place):
        query, _, _ = read_pair(pairs, place)
        total = jnp.sum(sums[query], axis=0, keepdims=True) * math.sqrt(WS)
        return 1.0 / total, scales[readable(query), :1]

    def couple(place, teacher, student, scale):
        query, key, _ = read_pair(pairs, place)
        query_side = features[readable(query)]
        to_queries = jnp.zeros((WS, wide), f32)
        for low, high in halves(rows):
            coupling = student[low:high] * scale[1] - teacher[low:high] * scale[0]
            coupling = coupling.astype(bf16)
            key_side = features[readable(key), :, low:high]
            grad[key, :, low:high] += lax.dot_general(
                query_side, coupling, (((1,), (1,)), ((), ())), preferred_element_type=f32
            )
            to_queries += jnp.dot(key_side, coupling, preferred_element_type=f32)
        grad[query] += to_queries

    def half(turn, parity):
        slot = turn & (SLOTS - 1)
        for step in range(UNROLL):
            fetch(turn, step).wait()
        for step in range(UNROLL):
            fetch(turn + AHEAD, step).start()
        scale = [inverses(UNROLL * turn + step) for step in range(UNROLL)]
        now = turn // 2 & 1
        before = (turn - LAG // UNROLL) // 2 & 1
        for step in range(UNROLL):
            place = UNROLL * turn + step
            old = rings[1 - parity][step].at[before]
            couple(place, old, fetched[step].at[slot], scale[step])
            ring = rings[parity][step]
            weigh(place, blocks, pairs, keys, weights, SCALE_T, causal, ring, now, sums)

    def steps(turn, carry):
        for parity in range(2):
            pl.when(turn & 1 == parity)(functools.partial(half, turn, parity))
        return carry

    turns = (count + LAG + UNROLL - 1) // UNROLL
    lax.fori_loop(0, turns, steps, 0)
    for turn in range(AHEAD):
        for step in range(UNROLL):
            fetch(turns + turn, step).wait()

    def finish(block, carry):
        out[block] = grad[block].astype(bf16)
        return carry

    lax.fori_loop(0, blocks, finish, 0, unroll=8)


def relation_gradient(slabs, segments, made, scales, features, pairs, count):
    blocks, _, wide = slabs.shape
    rows = made.shape[1]
    vmem = pl.BlockSpec(memory_space=pltpu.VMEM)
    smem = pl.BlockSpec(memory_space=pltpu.SMEM)
    ring = pltpu.VMEM((SLOTS, rows, wide), f32)
    return pl.pallas_call(
        functools.partial(gradient_kernel, blocks),
        out_shape=jax.ShapeDtypeStruct((blocks, WS, wide), bf16),
        in_specs=[smem, smem, vmem, vmem, pl.BlockSpec(memory_space=pl.ANY), vmem, vmem],
        out_specs=vmem,
        scratch_shapes=[
            pltpu.VMEM((blocks, rows, DEPTH), bf16),
            pltpu.VMEM((blocks, DEPTH, wide), bf16),
            [[pltpu.VMEM((2, rows, wide), f32)] * UNROLL] * 2,
            [ring] * UNROLL,
            pltpu.VMEM((2, rows, wide), f32),
            pltpu.VMEM((blocks + 1, 8, wide), f32),
            pltpu.VMEM((blocks + 1, WS, wide), f32),
            pltpu.SemaphoreType.DMA((UNROLL, SLOTS)),
        ],
        compiler_params=pltpu.CompilerParams(vmem_limit_bytes=48 * MIB),
        cost_estimate=pl.CostEstimate(
            flops=20_000_000_000, bytes_accessed=80_000_000, transcendentals=20_000_000
        ),
        name="relation_gradient",
    )(count, pairs, segments, slabs, made, scales, features)


def head_gradient(student, teacher, segment_ids, rows):
    blocks, _, wide = student.shape
    ends = jnp.stack([segment_ids[::rows], segment_ids[rows - 1 :: rows]])
    segments = jnp.pad(
        segment_ids.reshape(blocks, rows), ((0, 0), (0, wide - rows)), constant_values=-1
    )
    made, scales, features, pairs, count = student_weights(student, ends, segments, rows)
    return relation_gradient(teacher, segments, made, scales, features, pairs, count)


def unproject_kernel(part, grads, wq, wk, out):
    half = grads.shape[0] // 2
    rows, width = out.shape
    columns = pl.ds(pl.multiple_of(part[0] * width, 256), width)
    total = jnp.zeros((width, grads.shape[2]), f32)
    for rel, weight in enumerate((wq, wk)):
        turned = grads[rel * half : (rel + 1) * half].reshape(half * WS, grads.shape[2])
        total += jnp.dot(weight[columns], turned, preferred_element_type=f32)
    out[...] = total.T[:rows].astype(out.dtype)


def unproject(part, grads, wq, wk, rows, dtype):
    width = wq.shape[0] // 2
    vmem = pl.BlockSpec(memory_space=pltpu.VMEM)
    return pl.pallas_call(
        unproject_kernel,
        in_specs=[pl.BlockSpec(memory_space=pltpu.SMEM), vmem, vmem, vmem],
        out_specs=vmem,
        out_shape=jax.ShapeDtypeStruct((rows, width), dtype),
        compiler_params=pltpu.CompilerParams(vmem_limit_bytes=32 * MIB),
        cost_estimate=pl.CostEstimate(
            flops=4 * rows * width * wq.shape[1], bytes_accessed=6_000_000, transcendentals=0
        ),
        name="unproject",
    )(part[None], grads, wq, wk)


def shards(teacher_query, teacher_key, student_hidden, w_query, w_key, segment_ids, block_mask):
    rows = student_hidden.shape[0]
    student = project(student_hidden, w_query, w_key, block_mask)
    teacher = turn(teacher_query, teacher_key)
    student = lax.all_to_all(student.reshape(-1, *student.shape[2:]), "ctx", 0, 0, tiled=True)
    teacher = lax.all_to_all(teacher.reshape(-1, *teacher.shape[2:]), "ctx", 0, 0, tiled=True)
    turned = head_gradient(student, teacher, segment_ids, rows)
    back = lax.all_to_all(turned, "ctx", 0, 0, tiled=True)
    side = lax.axis_index("head")
    away = unproject(1 - side, back, w_query, w_key, rows, bf16)
    away = lax.ppermute(away, "head", [(0, 1), (1, 0)])
    own = unproject(side, back, w_query, w_key, rows, f32)
    return (own + away).astype(bf16)


def solution(mesh):
    placed = (
        P("ctx", "head"),
        P("ctx", "head"),
        P("ctx", None),
        P(None, "head"),
        P(None, "head"),
        P(),
        P("ctx", None),
    )
    return jax.shard_map(
        shards, mesh=mesh, in_specs=placed, out_specs=P("ctx", "head"), check_vma=False
    )
```

```python
import functools
import math

import jax
import jax.numpy as jnp
from jax import lax
from jax.experimental import pallas as pl
from jax.experimental.pallas import tpu as pltpu
from jax.sharding import PartitionSpec as P

DT = 5120
DS = 2048
HEADS = 64
REACH = 8
WT = DT // HEADS
WS = DS // HEADS
DEPTH = 128
EXTRA = 16
DOCS = 4
PACK = 8
LISTED = 8
UNROLL = 4
LAG = 3 * UNROLL
SLOTS = 4
AHEAD = 2
LIST = 640
HIDDEN = 1e30
SCALE_T = 1.0 / math.sqrt(WT)
SCALE_S = 1.0 / math.sqrt(WS)
SAFE = 60.0
MIB = 1024 * 1024
f32 = jnp.float32
bf16 = jnp.bfloat16


def round_up(value, unit):
    return (value + unit - 1) // unit * unit


def project_kernel(mask, hidden, wq, wk, out):
    rows, wide = hidden.shape[0], out.shape[-1]
    row = lax.broadcasted_iota(jnp.int32, (wide - rows, PACK * WS), 0)
    extra = jnp.zeros(row.shape, f32)
    for back in range(REACH - 1):
        extra = jnp.where(row == back, mask[0, back].astype(f32), extra)
    extra = extra.astype(bf16)
    for rel, weight in enumerate((wq, wk)):
        student = jnp.dot(hidden[...], weight[...], preferred_element_type=f32).astype(bf16)
        turned = jnp.concatenate([student, extra], axis=0).T
        out[rel] = turned.reshape(out.shape[1:])


def project(hidden, wq, wk, mask):
    rows = hidden.shape[0]
    wide = round_up(rows, 128)
    heads = wq.shape[1] // WS
    return pl.pallas_call(
        project_kernel,
        grid=(heads // PACK,),
        out_shape=jax.ShapeDtypeStruct((2, heads, WS, wide), bf16),
        in_specs=[
            pl.BlockSpec(memory_space=pltpu.SMEM),
            pl.BlockSpec((rows, DS), lambda i: (0, 0)),
            pl.BlockSpec((DS, PACK * WS), lambda i: (0, i)),
            pl.BlockSpec((DS, PACK * WS), lambda i: (0, i)),
        ],
        out_specs=pl.BlockSpec((2, PACK, WS, wide), lambda i: (0, i, 0, 0)),
        compiler_params=pltpu.CompilerParams(vmem_limit_bytes=56 * MIB),
        cost_estimate=pl.CostEstimate(
            flops=4 * rows * DS * heads * WS, bytes_accessed=10_000_000, transcendentals=0
        ),
        name="project_student",
    )(mask, hidden, wq, wk)


def turn_kernel(tq, tk, out):
    rows = tq.shape[0]
    wide = out.shape[-1]
    for rel, teacher in enumerate((tq, tk)):
        zeros = jnp.zeros((wide - rows, teacher.shape[1]), bf16)
        turned = jnp.concatenate([teacher[...], zeros], axis=0).T
        out[rel] = turned.reshape(out.shape[1:])


def turn(tq, tk):
    rows, columns = tq.shape
    wide = round_up(rows, 128)
    heads = columns // WT
    return pl.pallas_call(
        turn_kernel,
        grid=(heads // PACK,),
        out_shape=jax.ShapeDtypeStruct((2, heads, WT, wide), bf16),
        in_specs=[pl.BlockSpec((rows, PACK * WT), lambda i: (0, i))] * 2,
        out_specs=pl.BlockSpec((2, PACK, WT, wide), lambda i: (0, i, 0, 0)),
        compiler_params=pltpu.CompilerParams(vmem_limit_bytes=56 * MIB),
        cost_estimate=pl.CostEstimate(flops=0, bytes_accessed=5_000_000, transcendentals=0),
        name="turn_teacher",
    )(tq, tk)


def read_pair(pairs, place):
    code = pairs[place]
    return code & 255, (code >> 8) & 255, code >> 16


def fill(block, slab, segments, keys, weights):
    width, wide = slab.shape
    rows = keys.shape[1]
    row = lax.broadcasted_iota(jnp.int32, (EXTRA, wide), 0)
    lane = lax.broadcasted_iota(jnp.int32, (EXTRA, wide), 1)
    hot = jnp.where(row == segments[pl.ds(block, 1)], 1.0, 0.0)
    key_extra = jnp.where((row >= DOCS) & (row < DOCS + 3), 1.0, hot)
    query_extra = jnp.where((row < DOCS) & (lane < rows), (hot - 1.0) * HIDDEN, 0.0)
    zeros = jnp.zeros((DEPTH - EXTRA - width, wide), bf16)
    weights[block] = jnp.concatenate([slab, query_extra.astype(bf16), zeros], axis=0)
    keys[block] = jnp.concatenate([slab, key_extra.astype(bf16), zeros], axis=0).T[:rows]
    values = slab.astype(f32)
    return jnp.sum(values * values, axis=0, keepdims=True)


def subtract_maxima(width, blocks, count, pairs, keys, weights, causal, sums):
    rows, wide = causal.shape[1:]

    def raise_maxima(place, carry):
        query, key, diagonal = read_pair(pairs, place + LAG)
        scores = jnp.dot(keys[key], weights[query], preferred_element_type=f32)
        scores = scores + causal[diagonal]
        top = jnp.max(scores.reshape(rows // 8, 8, wide), axis=0)
        sums[query] = jnp.where(diagonal == 1, top, jnp.maximum(top, sums[query]))
        return carry

    lax.fori_loop(0, count, raise_maxima, 0)
    row = lax.broadcasted_iota(jnp.int32, (EXTRA, wide), 0)

    def set_maxima(block, carry):
        rest = jnp.max(sums[block], axis=0, keepdims=True)
        extra = weights[block, width : width + EXTRA].astype(f32)
        for part in range(3):
            piece = rest.astype(bf16).astype(f32)
            rest = rest - piece
            extra = jnp.where(row == DOCS + part, -piece, extra)
        weights[block, width : width + EXTRA] = extra.astype(bf16)
        return carry

    lax.fori_loop(0, blocks, set_maxima, 0)


def fill_causal(causal):
    shape = causal.shape[1:]
    key_at = lax.broadcasted_iota(jnp.int32, shape, 0)
    query_at = lax.broadcasted_iota(jnp.int32, shape, 1)
    causal[0] = jnp.zeros(shape, f32)
    causal[1] = jnp.where(key_at <= query_at, 0.0, -HIDDEN)


def halves(rows):
    return (0, 128), (128, rows)


def weigh(place, blocks, pairs, keys, weights, scale, causal, target, sums):
    query, key, diagonal = read_pair(pairs, place + LAG)
    rows, wide = causal.shape[1:]
    key_block = jnp.minimum(key, blocks - 1)
    operand = weights[jnp.minimum(query, blocks - 1)]
    part = jnp.where(diagonal == 1, 0.0, sums[query])
    for low, high in halves(rows):
        scores = jnp.dot(keys[key_block, low:high], operand, preferred_element_type=f32)
        made = jnp.exp(scores * scale + causal[diagonal, low:high])
        target[low:high] = made
        part += jnp.sum(made.reshape((high - low) // 8, 8, wide), axis=0)
    sums[query] = part


def student_kernel(
    blocks, ends, segments, slabs_in, made, scales, features_out, pairs, count_out, slabs, features, keys, weights, ring, causal, sums, seen, opened, sem, sems
):
    rows, wide = causal.shape[1:]
    arrive = pltpu.make_async_copy(slabs_in, slabs, sem)
    arrive.start()
    fill_causal(causal)
    arrive.wait()

    def look(block, carry):
        seen[pl.ds(block, 1)] = slabs[block, :16, wide - 128 :].astype(f32)[:1].astype(jnp.int32)
        return carry

    lax.fori_loop(0, blocks, look, 0, unroll=8)
    fetch = pltpu.make_async_copy(seen, opened, sem)
    fetch.start()
    fetch.wait()
    mask_lane = rows % 128

    def list_pairs(block, total):
        for back in range(REACH):
            key = jnp.maximum(block - back, 0)
            code = block | (key << 8)
            if back == 0:
                pairs[total + LAG] = code | (1 << 16)
                total = total + 1
            else:
                pairs[total + LAG] = code
                is_open = (block >= back) & (opened[block, mask_lane + back - 1] == 1)
                is_open = is_open & (ends[0, block] == ends[1, key])
                total = total + is_open.astype(jnp.int32)
        return total

    lane = lax.broadcasted_iota(jnp.int32, (WS, wide), 1)

    def prepare(block, carry):
        peak, total = carry
        total = list_pairs(block, total)
        slab = jnp.where(lane < rows, slabs[block].astype(f32), 0.0).astype(bf16)
        features[block] = slab
        return jnp.maximum(peak, fill(block, slab, segments, keys, weights)), total

    peak, count = lax.fori_loop(0, blocks, prepare, (jnp.zeros((1, wide), f32), 0), unroll=4)
    count_out[0] = count
    for place in range(LAG):
        pairs[place] = blocks | (blocks << 8)
    for place in range(LAG + LISTED):
        pairs[count + LAG + place] = blocks | (blocks << 8)

    @pl.when(jnp.logical_not(jnp.max(peak) * SCALE_S <= SAFE))
    def _():
        subtract_maxima(WS, blocks, count, pairs, keys, weights, causal, sums)

    leave = pltpu.make_async_copy(features, features_out, sem)
    leave.start()

    def send(turn):
        slot = turn & (SLOTS - 1)
        group = made.at[pl.ds(turn * LISTED, LISTED)]
        return pltpu.make_async_copy(ring.at[slot], group, sems.at[slot])

    def steps(turn, carry):
        slot = turn & (SLOTS - 1)

        @pl.when(turn >= SLOTS)
        def _():
            send(turn - SLOTS).wait()

        for step in range(LISTED):
            place = LISTED * turn + step
            target = ring.at[slot, step]
            weigh(place, blocks, pairs, keys, weights, SCALE_S, causal, target, sums)
        send(turn).start()
        return carry

    turns = (count + LISTED - 1) // LISTED
    lax.fori_loop(0, turns, steps, 0)

    def drain(turn, carry):
        send(turn).wait()
        return carry

    lax.fori_loop(jnp.maximum(turns - SLOTS, 0), turns, drain, 0)
    leave.wait()

    def finish(block, carry):
        total = jnp.sum(sums[block], axis=0, keepdims=True) * math.sqrt(WS)
        scales[block] = jnp.broadcast_to(1.0 / total, (8, wide))
        return carry

    lax.fori_loop(0, blocks, finish, 0, unroll=8)


def student_weights(slabs, ends, segments, rows):
    blocks, _, wide = slabs.shape
    vmem = pl.BlockSpec(memory_space=pltpu.VMEM)
    smem = pl.BlockSpec(memory_space=pltpu.SMEM)
    hbm = pl.BlockSpec(memory_space=pl.ANY)
    slab = pltpu.VMEM((blocks, WS, wide), bf16)
    return pl.pallas_call(
        functools.partial(student_kernel, blocks),
        out_shape=(
            jax.ShapeDtypeStruct((blocks * REACH, rows, wide), f32),
            jax.ShapeDtypeStruct((blocks, 8, wide), f32),
            jax.ShapeDtypeStruct((blocks, WS, wide), bf16),
            jax.ShapeDtypeStruct((LIST,), jnp.int32),
            jax.ShapeDtypeStruct((1,), jnp.int32),
        ),
        in_specs=[smem, vmem, hbm],
        out_specs=(hbm, vmem, hbm, smem, smem),
        scratch_shapes=[
            slab,
            slab,
            pltpu.VMEM((blocks, rows, DEPTH), bf16),
            pltpu.VMEM((blocks, DEPTH, wide), bf16),
            pltpu.VMEM((SLOTS, LISTED, rows, wide), f32),
            pltpu.VMEM((2, rows, wide), f32),
            pltpu.VMEM((blocks + 1, 8, wide), f32),
            pltpu.VMEM((blocks, 128), jnp.int32),
            pltpu.SMEM((blocks, 128), jnp.int32),
            pltpu.SemaphoreType.DMA,
            pltpu.SemaphoreType.DMA((SLOTS,)),
        ],
        compiler_params=pltpu.CompilerParams(vmem_limit_bytes=48 * MIB),
        cost_estimate=pl.CostEstimate(
            flops=10_000_000_000, bytes_accessed=80_000_000, transcendentals=20_000_000
        ),
        name="student_weights",
    )(ends, segments, slabs)


def gradient_kernel(
    blocks, count_in, pairs, segments, slabs, made, scales, features_in, out, features, result, keys, weights, rings, fetched, causal, sums, grad, sems, sem, out_sems
):
    rows, wide = causal.shape[1:]
    count = count_in[0]
    arrive = pltpu.make_async_copy(features_in, features, sem)
    arrive.start()
    fill_causal(causal)

    def fetch(turn):
        group = jnp.clip(turn - LAG // UNROLL, 0, made.shape[0] // UNROLL - 1)
        slot = turn & (SLOTS - 1)
        group = made.at[pl.ds(group * UNROLL, UNROLL)]
        return pltpu.make_async_copy(group, fetched.at[slot], sems.at[slot])

    for turn in range(AHEAD):
        fetch(turn).start()

    def prepare(block, peak):
        grad[block] = jnp.zeros((WS, wide), f32)
        return jnp.maximum(peak, fill(block, slabs[block], segments, keys, weights))

    peak = lax.fori_loop(0, blocks, prepare, jnp.zeros((1, wide), f32), unroll=4)

    @pl.when(jnp.logical_not(jnp.max(peak) * SCALE_T <= SAFE))
    def _():
        subtract_maxima(WT, blocks, count, pairs, keys, weights, causal, sums)

    def readable(block):
        return jnp.minimum(block, blocks - 1)

    def inverses(place):
        query, _, _ = read_pair(pairs, place)
        total = jnp.sum(sums[query], axis=0, keepdims=True) * math.sqrt(WS)
        return 1.0 / total, scales[readable(query), :1]

    def couple(place, teacher, student, scale):
        query, key, _ = read_pair(pairs, place)
        query_side = features[readable(query)]
        to_queries = jnp.zeros((WS, wide), f32)
        for low, high in halves(rows):
            coupling = student[low:high] * scale[1] - teacher[low:high] * scale[0]
            coupling = coupling.astype(bf16)
            key_side = features[readable(key), :, low:high]
            grad[key, :, low:high] += lax.dot_general(
                query_side, coupling, (((1,), (1,)), ((), ())), preferred_element_type=f32
            )
            to_queries += jnp.dot(key_side, coupling, preferred_element_type=f32)
        grad[query] += to_queries

    def half(turn, parity):
        slot = turn & (SLOTS - 1)
        fetch(turn).wait()
        fetch(turn + AHEAD).start()
        scale = [inverses(UNROLL * turn + step) for step in range(UNROLL)]
        now = turn // 2 & 1
        before = (turn - LAG // UNROLL) // 2 & 1
        for step in range(UNROLL):
            place = UNROLL * turn + step
            old = rings[1 - parity].at[before, step]
            couple(place, old, fetched.at[slot, step], scale[step])
            target = rings[parity].at[now, step]
            weigh(place, blocks, pairs, keys, weights, SCALE_T, causal, target, sums)

    def steps(turn, carry):
        for parity in range(2):
            pl.when(turn & 1 == parity)(functools.partial(half, turn, parity))
        return carry

    turns = (count + LAG + UNROLL - 1) // UNROLL
    arrive.wait()
    lax.fori_loop(0, turns, steps, 0)
    for turn in range(AHEAD):
        fetch(turns + turn).wait()

    pieces = out_sems.shape[0]
    size = blocks // pieces

    def finish(block, carry):
        result[block] = grad[block].astype(bf16)
        return carry

    copies = []
    for piece in range(pieces):
        lax.fori_loop(piece * size, (piece + 1) * size, finish, 0, unroll=8)
        part = pl.ds(piece * size, size)
        copies.append(pltpu.make_async_copy(result.at[part], out.at[part], out_sems.at[piece]))
        copies[-1].start()
    for copy in copies:
        copy.wait()


def relation_gradient(slabs, segments, made, scales, features, pairs, count):
    blocks, _, wide = slabs.shape
    rows = made.shape[1]
    vmem = pl.BlockSpec(memory_space=pltpu.VMEM)
    smem = pl.BlockSpec(memory_space=pltpu.SMEM)
    hbm = pl.BlockSpec(memory_space=pl.ANY)
    slab = pltpu.VMEM((blocks, WS, wide), bf16)
    return pl.pallas_call(
        functools.partial(gradient_kernel, blocks),
        out_shape=jax.ShapeDtypeStruct((blocks, WS, wide), bf16),
        in_specs=[smem, smem, vmem, vmem, hbm, vmem, hbm],
        out_specs=hbm,
        scratch_shapes=[
            slab,
            slab,
            pltpu.VMEM((blocks, rows, DEPTH), bf16),
            pltpu.VMEM((blocks, DEPTH, wide), bf16),
            [pltpu.VMEM((2, UNROLL, rows, wide), f32)] * 2,
            pltpu.VMEM((SLOTS, UNROLL, rows, wide), f32),
            pltpu.VMEM((2, rows, wide), f32),
            pltpu.VMEM((blocks + 1, 8, wide), f32),
            pltpu.VMEM((blocks + 1, WS, wide), f32),
            pltpu.SemaphoreType.DMA((SLOTS,)),
            pltpu.SemaphoreType.DMA,
            pltpu.SemaphoreType.DMA((4,)),
        ],
        compiler_params=pltpu.CompilerParams(vmem_limit_bytes=48 * MIB),
        cost_estimate=pl.CostEstimate(
            flops=20_000_000_000, bytes_accessed=80_000_000, transcendentals=20_000_000
        ),
        name="relation_gradient",
    )(count, pairs, segments, slabs, made, scales, features)


def head_gradient(student, teacher, segment_ids, rows):
    blocks, _, wide = student.shape
    ends = jnp.stack([segment_ids[::rows], segment_ids[rows - 1 :: rows]])
    segments = jnp.pad(
        segment_ids.reshape(blocks, rows), ((0, 0), (0, wide - rows)), constant_values=-1
    )
    made, scales, features, pairs, count = student_weights(student, ends, segments, rows)
    return relation_gradient(teacher, segments, made, scales, features, pairs, count)


def unproject_kernel(part, grads, wq, wk, out):
    half = grads.shape[0] // 2
    rows, width = out.shape
    columns = pl.ds(pl.multiple_of(part[0] * width, 256), width)
    total = jnp.zeros((width, grads.shape[2]), f32)
    for rel, weight in enumerate((wq, wk)):
        turned = grads[rel * half : (rel + 1) * half].reshape(half * WS, grads.shape[2])
        total += jnp.dot(weight[columns], turned, preferred_element_type=f32)
    out[...] = total.T[:rows].astype(out.dtype)


def unproject(part, grads, wq, wk, rows, dtype):
    width = wq.shape[0] // 2
    vmem = pl.BlockSpec(memory_space=pltpu.VMEM)
    return pl.pallas_call(
        unproject_kernel,
        in_specs=[pl.BlockSpec(memory_space=pltpu.SMEM), vmem, vmem, vmem],
        out_specs=vmem,
        out_shape=jax.ShapeDtypeStruct((rows, width), dtype),
        compiler_params=pltpu.CompilerParams(vmem_limit_bytes=32 * MIB),
        cost_estimate=pl.CostEstimate(
            flops=4 * rows * width * wq.shape[1], bytes_accessed=6_000_000, transcendentals=0
        ),
        name="unproject",
    )(part[None], grads, wq, wk)


def shards(teacher_query, teacher_key, student_hidden, w_query, w_key, segment_ids, block_mask):
    rows = student_hidden.shape[0]
    student = project(student_hidden, w_query, w_key, block_mask)
    teacher = turn(teacher_query, teacher_key)
    student = lax.all_to_all(student.reshape(-1, *student.shape[2:]), "ctx", 0, 0, tiled=True)
    teacher = lax.all_to_all(teacher.reshape(-1, *teacher.shape[2:]), "ctx", 0, 0, tiled=True)
    turned = head_gradient(student, teacher, segment_ids, rows)
    back = lax.all_to_all(turned, "ctx", 0, 0, tiled=True)
    side = lax.axis_index("head")
    away = unproject(1 - side, back, w_query, w_key, rows, bf16)
    away = lax.ppermute(away, "head", [(0, 1), (1, 0)])
    own = unproject(side, back, w_query, w_key, rows, f32)
    return (own + away).astype(bf16)


def solution(mesh):
    placed = (
        P("ctx", "head"),
        P("ctx", "head"),
        P("ctx", None),
        P(None, "head"),
        P(None, "head"),
        P(),
        P("ctx", None),
    )
    return jax.shard_map(
        shards, mesh=mesh, in_specs=placed, out_specs=P("ctx", "head"), check_vma=False
    )
```

```python
import functools
import math

import jax
import jax.numpy as jnp
from jax import lax
from jax.experimental import pallas as pl
from jax.experimental.pallas import tpu as pltpu
from jax.sharding import PartitionSpec as P

DT = 5120
DS = 2048
HEADS = 64
REACH = 8
WT = DT // HEADS
WS = DS // HEADS
DEPTH = 128
EXTRA = 16
DOCS = 4
PACK = 8
LISTED = 8
UNROLL = 4
LAG = 3 * UNROLL
SLOTS = 4
AHEAD = 2
LIST = 640
HIDDEN = 1e30
SCALE_T = 1.0 / math.sqrt(WT)
SCALE_S = 1.0 / math.sqrt(WS)
SAFE = 60.0
MIB = 1024 * 1024
f32 = jnp.float32
bf16 = jnp.bfloat16


def round_up(value, unit):
    return (value + unit - 1) // unit * unit


def project_kernel(mask, hidden, wq, wk, out):
    rows, wide = hidden.shape[0], out.shape[-1]
    row = lax.broadcasted_iota(jnp.int32, (wide - rows, PACK * WS), 0)
    extra = jnp.zeros(row.shape, f32)
    for back in range(REACH - 1):
        extra = jnp.where(row == back, mask[0, back].astype(f32), extra)
    extra = extra.astype(bf16)
    for rel, weight in enumerate((wq, wk)):
        student = jnp.dot(hidden[...], weight[...], preferred_element_type=f32).astype(bf16)
        turned = jnp.concatenate([student, extra], axis=0).T
        out[rel] = turned.reshape(out.shape[1:])


def project(hidden, wq, wk, mask):
    rows = hidden.shape[0]
    wide = round_up(rows, 128)
    heads = wq.shape[1] // WS
    return pl.pallas_call(
        project_kernel,
        grid=(heads // PACK,),
        out_shape=jax.ShapeDtypeStruct((2, heads, WS, wide), bf16),
        in_specs=[
            pl.BlockSpec(memory_space=pltpu.SMEM),
            pl.BlockSpec((rows, DS), lambda i: (0, 0)),
            pl.BlockSpec((DS, PACK * WS), lambda i: (0, i)),
            pl.BlockSpec((DS, PACK * WS), lambda i: (0, i)),
        ],
        out_specs=pl.BlockSpec((2, PACK, WS, wide), lambda i: (0, i, 0, 0)),
        compiler_params=pltpu.CompilerParams(vmem_limit_bytes=56 * MIB),
        cost_estimate=pl.CostEstimate(
            flops=4 * rows * DS * heads * WS, bytes_accessed=10_000_000, transcendentals=0
        ),
        name="project_student",
    )(mask, hidden, wq, wk)


def turn_kernel(tq, tk, out):
    rows = tq.shape[0]
    wide = out.shape[-1]
    for rel, teacher in enumerate((tq, tk)):
        zeros = jnp.zeros((wide - rows, teacher.shape[1]), bf16)
        turned = jnp.concatenate([teacher[...], zeros], axis=0).T
        out[rel] = turned.reshape(out.shape[1:])


def turn(tq, tk):
    rows, columns = tq.shape
    wide = round_up(rows, 128)
    heads = columns // WT
    return pl.pallas_call(
        turn_kernel,
        grid=(heads // PACK,),
        out_shape=jax.ShapeDtypeStruct((2, heads, WT, wide), bf16),
        in_specs=[pl.BlockSpec((rows, PACK * WT), lambda i: (0, i))] * 2,
        out_specs=pl.BlockSpec((2, PACK, WT, wide), lambda i: (0, i, 0, 0)),
        compiler_params=pltpu.CompilerParams(vmem_limit_bytes=56 * MIB),
        cost_estimate=pl.CostEstimate(flops=0, bytes_accessed=5_000_000, transcendentals=0),
        name="turn_teacher",
    )(tq, tk)


def read_pair(pairs, place):
    code = pairs[place]
    return code & 255, (code >> 8) & 255, code >> 16


def fill(block, slab, segments, keys, weights):
    width, wide = slab.shape
    rows = keys.shape[1]
    row = lax.broadcasted_iota(jnp.int32, (EXTRA, wide), 0)
    lane = lax.broadcasted_iota(jnp.int32, (EXTRA, wide), 1)
    hot = jnp.where(row == segments[pl.ds(block, 1)], 1.0, 0.0)
    key_extra = jnp.where((row >= DOCS) & (row < DOCS + 3), 1.0, hot)
    query_extra = jnp.where((row < DOCS) & (lane < rows), (hot - 1.0) * HIDDEN, 0.0)
    zeros = jnp.zeros((DEPTH - EXTRA - width, wide), bf16)
    weights[block] = jnp.concatenate([slab, query_extra.astype(bf16), zeros], axis=0)
    keys[block] = jnp.concatenate([slab, key_extra.astype(bf16), zeros], axis=0).T[:rows]
    values = slab.astype(f32)
    return jnp.sum(values * values, axis=0, keepdims=True)


def subtract_maxima(width, blocks, count, pairs, keys, weights, causal, sums):
    rows, wide = causal.shape[1:]

    def raise_maxima(place, carry):
        query, key, diagonal = read_pair(pairs, place + LAG)
        scores = jnp.dot(keys[key], weights[query], preferred_element_type=f32)
        scores = scores + causal[diagonal]
        top = jnp.max(scores.reshape(rows // 8, 8, wide), axis=0)
        sums[query] = jnp.where(diagonal == 1, top, jnp.maximum(top, sums[query]))
        return carry

    lax.fori_loop(0, count, raise_maxima, 0)
    row = lax.broadcasted_iota(jnp.int32, (EXTRA, wide), 0)

    def set_maxima(block, carry):
        rest = jnp.max(sums[block], axis=0, keepdims=True)
        extra = weights[block, width : width + EXTRA].astype(f32)
        for part in range(3):
            piece = rest.astype(bf16).astype(f32)
            rest = rest - piece
            extra = jnp.where(row == DOCS + part, -piece, extra)
        weights[block, width : width + EXTRA] = extra.astype(bf16)
        return carry

    lax.fori_loop(0, blocks, set_maxima, 0)


def fill_causal(causal):
    shape = causal.shape[1:]
    key_at = lax.broadcasted_iota(jnp.int32, shape, 0)
    query_at = lax.broadcasted_iota(jnp.int32, shape, 1)
    causal[0] = jnp.zeros(shape, f32)
    causal[1] = jnp.where(key_at <= query_at, 0.0, -HIDDEN)


def halves(rows):
    return (0, 128), (128, rows)


def weigh(place, blocks, pairs, keys, weights, scale, causal, target, sums):
    query, key, diagonal = read_pair(pairs, place + LAG)
    rows, wide = causal.shape[1:]
    key_block = jnp.minimum(key, blocks - 1)
    operand = weights[jnp.minimum(query, blocks - 1)]
    part = jnp.where(diagonal == 1, 0.0, sums[query])
    for low, high in halves(rows):
        scores = jnp.dot(keys[key_block, low:high], operand, preferred_element_type=f32)
        made = jnp.exp(scores * scale + causal[diagonal, low:high])
        target[low:high] = made
        part += jnp.sum(made.reshape((high - low) // 8, 8, wide), axis=0)
    sums[query] = part


def student_kernel(
    blocks, ends, segments, slabs_in, made, scales, features_out, pairs, count_out, slabs, features, keys, weights, ring, causal, sums, seen, opened, sem, sems
):
    rows, wide = causal.shape[1:]
    arrive = pltpu.make_async_copy(slabs_in, slabs, sem)
    arrive.start()
    fill_causal(causal)
    arrive.wait()

    def look(block, carry):
        seen[pl.ds(block, 1)] = slabs[block, :16, wide - 128 :].astype(f32)[:1].astype(jnp.int32)
        return carry

    lax.fori_loop(0, blocks, look, 0, unroll=8)
    fetch = pltpu.make_async_copy(seen, opened, sem)
    fetch.start()
    fetch.wait()
    mask_lane = rows % 128

    def list_pairs(block, total):
        for back in range(REACH):
            key = jnp.maximum(block - back, 0)
            code = block | (key << 8)
            if back == 0:
                pairs[total + LAG] = code | (1 << 16)
                total = total + 1
            else:
                pairs[total + LAG] = code
                is_open = (block >= back) & (opened[block, mask_lane + back - 1] == 1)
                is_open = is_open & (ends[0, block] == ends[1, key])
                total = total + is_open.astype(jnp.int32)
        return total

    lane = lax.broadcasted_iota(jnp.int32, (WS, wide), 1)

    def prepare(block, carry):
        peak, total = carry
        total = list_pairs(block, total)
        slab = jnp.where(lane < rows, slabs[block].astype(f32), 0.0).astype(bf16)
        features[block] = slab
        return jnp.maximum(peak, fill(block, slab, segments, keys, weights)), total

    peak, count = lax.fori_loop(0, blocks, prepare, (jnp.zeros((1, wide), f32), 0), unroll=4)
    count_out[0] = count
    for place in range(LAG):
        pairs[place] = blocks | (blocks << 8)
    for place in range(LAG + LISTED):
        pairs[count + LAG + place] = blocks | (blocks << 8)

    @pl.when(jnp.logical_not(jnp.max(peak) * SCALE_S <= SAFE))
    def _():
        subtract_maxima(WS, blocks, count, pairs, keys, weights, causal, sums)

    leave = pltpu.make_async_copy(features, features_out, sem)
    leave.start()

    def send(turn):
        slot = turn & (SLOTS - 1)
        group = made.at[pl.ds(turn * LISTED, LISTED)]
        return pltpu.make_async_copy(ring.at[slot], group, sems.at[slot])

    def steps(turn, carry):
        slot = turn & (SLOTS - 1)

        @pl.when(turn >= SLOTS)
        def _():
            send(turn - SLOTS).wait()

        for step in range(LISTED):
            place = LISTED * turn + step
            target = ring.at[slot, step]
            weigh(place, blocks, pairs, keys, weights, SCALE_S, causal, target, sums)
        send(turn).start()
        return carry

    turns = (count + LISTED - 1) // LISTED
    lax.fori_loop(0, turns, steps, 0)

    def drain(turn, carry):
        send(turn).wait()
        return carry

    lax.fori_loop(jnp.maximum(turns - SLOTS, 0), turns, drain, 0)
    leave.wait()

    def finish(block, carry):
        total = jnp.sum(sums[block], axis=0, keepdims=True) * math.sqrt(WS)
        scales[block] = jnp.broadcast_to(1.0 / total, (8, wide))
        return carry

    lax.fori_loop(0, blocks, finish, 0, unroll=8)


def student_weights(slabs, ends, segments, rows):
    blocks, _, wide = slabs.shape
    vmem = pl.BlockSpec(memory_space=pltpu.VMEM)
    smem = pl.BlockSpec(memory_space=pltpu.SMEM)
    hbm = pl.BlockSpec(memory_space=pl.ANY)
    slab = pltpu.VMEM((blocks, WS, wide), bf16)
    return pl.pallas_call(
        functools.partial(student_kernel, blocks),
        out_shape=(
            jax.ShapeDtypeStruct((blocks * REACH, rows, wide), f32),
            jax.ShapeDtypeStruct((blocks, 8, wide), f32),
            jax.ShapeDtypeStruct((blocks, WS, wide), bf16),
            jax.ShapeDtypeStruct((LIST,), jnp.int32),
            jax.ShapeDtypeStruct((1,), jnp.int32),
        ),
        in_specs=[smem, vmem, hbm],
        out_specs=(hbm, vmem, hbm, smem, smem),
        scratch_shapes=[
            slab,
            slab,
            pltpu.VMEM((blocks, rows, DEPTH), bf16),
            pltpu.VMEM((blocks, DEPTH, wide), bf16),
            pltpu.VMEM((SLOTS, LISTED, rows, wide), f32),
            pltpu.VMEM((2, rows, wide), f32),
            pltpu.VMEM((blocks + 1, 8, wide), f32),
            pltpu.VMEM((blocks, 128), jnp.int32),
            pltpu.SMEM((blocks, 128), jnp.int32),
            pltpu.SemaphoreType.DMA,
            pltpu.SemaphoreType.DMA((SLOTS,)),
        ],
        compiler_params=pltpu.CompilerParams(vmem_limit_bytes=56 * MIB),
        cost_estimate=pl.CostEstimate(
            flops=10_000_000_000, bytes_accessed=80_000_000, transcendentals=20_000_000
        ),
        name="student_weights",
    )(ends, segments, slabs)


def gradient_kernel(
    blocks, count_in, pairs, segments, slabs_in, made, scales, features_in, out, slabs, features, result, keys, weights, rings, fetched, causal, sums, grad, sems, sem, piece_sems
):
    rows, wide = causal.shape[1:]
    count = count_in[0]
    pieces = piece_sems.shape[0]
    size = blocks // pieces

    def copy_piece(source, target, piece):
        part = pl.ds(piece * size, size)
        return pltpu.make_async_copy(source.at[part], target.at[part], piece_sems.at[piece])

    for piece in range(pieces):
        copy_piece(slabs_in, slabs, piece).start()
    arrive = pltpu.make_async_copy(features_in, features, sem)
    arrive.start()
    fill_causal(causal)

    def fetch(turn):
        group = jnp.clip(turn - LAG // UNROLL, 0, made.shape[0] // UNROLL - 1)
        slot = turn & (SLOTS - 1)
        group = made.at[pl.ds(group * UNROLL, UNROLL)]
        return pltpu.make_async_copy(group, fetched.at[slot], sems.at[slot])

    for turn in range(AHEAD):
        fetch(turn).start()

    def prepare(block, peak):
        grad[block] = jnp.zeros((WS, wide), f32)
        return jnp.maximum(peak, fill(block, slabs[block], segments, keys, weights))

    peak = jnp.zeros((1, wide), f32)
    for piece in range(pieces):
        copy_piece(slabs_in, slabs, piece).wait()
        peak = lax.fori_loop(piece * size, (piece + 1) * size, prepare, peak, unroll=4)

    @pl.when(jnp.logical_not(jnp.max(peak) * SCALE_T <= SAFE))
    def _():
        subtract_maxima(WT, blocks, count, pairs, keys, weights, causal, sums)

    def readable(block):
        return jnp.minimum(block, blocks - 1)

    def inverses(place):
        query, _, _ = read_pair(pairs, place)
        total = jnp.sum(sums[query], axis=0, keepdims=True) * math.sqrt(WS)
        return 1.0 / total, scales[readable(query), :1]

    def couple(place, teacher, student, scale):
        query, key, _ = read_pair(pairs, place)
        query_side = features[readable(query)]
        to_queries = jnp.zeros((WS, wide), f32)
        for low, high in halves(rows):
            coupling = student[low:high] * scale[1] - teacher[low:high] * scale[0]
            coupling = coupling.astype(bf16)
            key_side = features[readable(key), :, low:high]
            grad[key, :, low:high] += lax.dot_general(
                query_side, coupling, (((1,), (1,)), ((), ())), preferred_element_type=f32
            )
            to_queries += jnp.dot(key_side, coupling, preferred_element_type=f32)
        grad[query] += to_queries

    def half(turn, parity):
        slot = turn & (SLOTS - 1)
        fetch(turn).wait()
        fetch(turn + AHEAD).start()
        scale = [inverses(UNROLL * turn + step) for step in range(UNROLL)]
        now = turn // 2 & 1
        before = (turn - LAG // UNROLL) // 2 & 1
        for step in range(UNROLL):
            place = UNROLL * turn + step
            old = rings[1 - parity].at[before, step]
            couple(place, old, fetched.at[slot, step], scale[step])
            target = rings[parity].at[now, step]
            weigh(place, blocks, pairs, keys, weights, SCALE_T, causal, target, sums)

    def steps(turn, carry):
        for parity in range(2):
            pl.when(turn & 1 == parity)(functools.partial(half, turn, parity))
        return carry

    turns = (count + LAG + UNROLL - 1) // UNROLL
    arrive.wait()
    lax.fori_loop(0, turns, steps, 0)
    for turn in range(AHEAD):
        fetch(turns + turn).wait()

    def finish(block, carry):
        result[block] = grad[block].astype(bf16)
        return carry

    for piece in range(pieces):
        lax.fori_loop(piece * size, (piece + 1) * size, finish, 0, unroll=8)
        copy_piece(result, out, piece).start()
    for piece in range(pieces):
        copy_piece(result, out, piece).wait()


def relation_gradient(slabs, segments, made, scales, features, pairs, count):
    blocks, _, wide = slabs.shape
    rows = made.shape[1]
    vmem = pl.BlockSpec(memory_space=pltpu.VMEM)
    smem = pl.BlockSpec(memory_space=pltpu.SMEM)
    hbm = pl.BlockSpec(memory_space=pl.ANY)
    slab = pltpu.VMEM((blocks, WS, wide), bf16)
    return pl.pallas_call(
        functools.partial(gradient_kernel, blocks),
        out_shape=jax.ShapeDtypeStruct((blocks, WS, wide), bf16),
        in_specs=[smem, smem, vmem, hbm, hbm, vmem, hbm],
        out_specs=hbm,
        scratch_shapes=[
            pltpu.VMEM(slabs.shape, bf16),
            slab,
            slab,
            pltpu.VMEM((blocks, rows, DEPTH), bf16),
            pltpu.VMEM((blocks, DEPTH, wide), bf16),
            [pltpu.VMEM((2, UNROLL, rows, wide), f32)] * 2,
            pltpu.VMEM((SLOTS, UNROLL, rows, wide), f32),
            pltpu.VMEM((2, rows, wide), f32),
            pltpu.VMEM((blocks + 1, 8, wide), f32),
            pltpu.VMEM((blocks + 1, WS, wide), f32),
            pltpu.SemaphoreType.DMA((SLOTS,)),
            pltpu.SemaphoreType.DMA,
            pltpu.SemaphoreType.DMA((4,)),
        ],
        compiler_params=pltpu.CompilerParams(vmem_limit_bytes=56 * MIB),
        cost_estimate=pl.CostEstimate(
            flops=20_000_000_000, bytes_accessed=80_000_000, transcendentals=20_000_000
        ),
        name="relation_gradient",
    )(count, pairs, segments, slabs, made, scales, features)


def head_gradient(student, teacher, segment_ids, rows):
    blocks, _, wide = student.shape
    ends = jnp.stack([segment_ids[::rows], segment_ids[rows - 1 :: rows]])
    segments = jnp.pad(
        segment_ids.reshape(blocks, rows), ((0, 0), (0, wide - rows)), constant_values=-1
    )
    made, scales, features, pairs, count = student_weights(student, ends, segments, rows)
    return relation_gradient(teacher, segments, made, scales, features, pairs, count)


def unproject_kernel(grads, wq, wk, out):
    half = grads.shape[0] // 2
    rows, width = out.shape
    total = jnp.zeros((width, grads.shape[2]), f32)
    for rel, weight in enumerate((wq, wk)):
        turned = grads[rel * half : (rel + 1) * half].reshape(half * WS, grads.shape[2])
        total += jnp.dot(weight[...], turned, preferred_element_type=f32)
    out[...] = total.T[:rows].astype(out.dtype)


def unproject(grads, wq, wk, rows, dtype):
    width = wq.shape[0]
    vmem = pl.BlockSpec(memory_space=pltpu.VMEM)
    return pl.pallas_call(
        unproject_kernel,
        in_specs=[vmem, vmem, vmem],
        out_specs=vmem,
        out_shape=jax.ShapeDtypeStruct((rows, width), dtype),
        compiler_params=pltpu.CompilerParams(vmem_limit_bytes=32 * MIB),
        cost_estimate=pl.CostEstimate(
            flops=4 * rows * width * wq.shape[1], bytes_accessed=6_000_000, transcendentals=0
        ),
        name="unproject",
    )(grads, wq, wk)


def shards(teacher_query, teacher_key, student_hidden, w_query, w_key, segment_ids, block_mask):
    rows = student_hidden.shape[0]
    student = project(student_hidden, w_query, w_key, block_mask)
    teacher = turn(teacher_query, teacher_key)
    student = lax.all_to_all(student.reshape(-1, *student.shape[2:]), "ctx", 0, 0, tiled=True)
    teacher = lax.all_to_all(teacher.reshape(-1, *teacher.shape[2:]), "ctx", 0, 0, tiled=True)
    turned = head_gradient(student, teacher, segment_ids, rows)
    side = lax.axis_index("head")
    width = w_query.shape[0] // 2
    turned, side = lax.optimization_barrier((turned, side))
    cut = [
        [lax.dynamic_slice_in_dim(weight, part * width, width, 0) for weight in (w_query, w_key)]
        for part in (1 - side, side)
    ]
    cut = lax.optimization_barrier(cut)
    back = lax.all_to_all(turned, "ctx", 0, 0, tiled=True)
    away = unproject(back, *cut[0], rows, bf16)
    away = lax.ppermute(away, "head", [(0, 1), (1, 0)])
    own = unproject(back, *cut[1], rows, f32)
    return (own + away).astype(bf16)


def solution(mesh):
    placed = (
        P("ctx", "head"),
        P("ctx", "head"),
        P("ctx", None),
        P(None, "head"),
        P(None, "head"),
        P(),
        P("ctx", None),
    )
    return jax.shard_map(
        shards, mesh=mesh, in_specs=placed, out_specs=P("ctx", "head"), check_vma=False
    )
```

```python
import functools
import math

import jax
import jax.numpy as jnp
from jax import lax
from jax.experimental import pallas as pl
from jax.experimental.pallas import tpu as pltpu
from jax.sharding import PartitionSpec as P

DT = 5120
DS = 2048
HEADS = 64
REACH = 8
WT = DT // HEADS
WS = DS // HEADS
DEPTH = 128
EXTRA = 16
DOCS = 4
PACK = 8
LISTED = 16
UNROLL = 6
LAG = 3 * UNROLL
SLOTS = 4
AHEAD = 2
LIST = 640
HIDDEN = 1e30
SCALE_T = 1.0 / math.sqrt(WT)
SCALE_S = 1.0 / math.sqrt(WS)
SAFE = 60.0
MIB = 1024 * 1024
f32 = jnp.float32
bf16 = jnp.bfloat16


def round_up(value, unit):
    return (value + unit - 1) // unit * unit


def project_kernel(mask, hidden, wq, wk, out):
    rows, wide = hidden.shape[0], out.shape[-1]
    row = lax.broadcasted_iota(jnp.int32, (wide - rows, PACK * WS), 0)
    extra = jnp.zeros(row.shape, f32)
    for back in range(REACH - 1):
        extra = jnp.where(row == back, mask[0, back].astype(f32), extra)
    extra = extra.astype(bf16)
    for rel, weight in enumerate((wq, wk)):
        student = jnp.dot(hidden[...], weight[...], preferred_element_type=f32).astype(bf16)
        turned = jnp.concatenate([student, extra], axis=0).T
        out[rel] = turned.reshape(out.shape[1:])


def project(hidden, wq, wk, mask):
    rows = hidden.shape[0]
    wide = round_up(rows, 128)
    heads = wq.shape[1] // WS
    return pl.pallas_call(
        project_kernel,
        grid=(heads // PACK,),
        out_shape=jax.ShapeDtypeStruct((2, heads, WS, wide), bf16),
        in_specs=[
            pl.BlockSpec(memory_space=pltpu.SMEM),
            pl.BlockSpec((rows, DS), lambda i: (0, 0)),
            pl.BlockSpec((DS, PACK * WS), lambda i: (0, i)),
            pl.BlockSpec((DS, PACK * WS), lambda i: (0, i)),
        ],
        out_specs=pl.BlockSpec((2, PACK, WS, wide), lambda i: (0, i, 0, 0)),
        compiler_params=pltpu.CompilerParams(vmem_limit_bytes=56 * MIB),
        cost_estimate=pl.CostEstimate(
            flops=4 * rows * DS * heads * WS, bytes_accessed=10_000_000, transcendentals=0
        ),
        name="project_student",
    )(mask, hidden, wq, wk)


def turn_kernel(tq, tk, out):
    rows = tq.shape[0]
    wide = out.shape[-1]
    for rel, teacher in enumerate((tq, tk)):
        zeros = jnp.zeros((wide - rows, teacher.shape[1]), bf16)
        turned = jnp.concatenate([teacher[...], zeros], axis=0).T
        out[rel] = turned.reshape(out.shape[1:])


def turn(tq, tk):
    rows, columns = tq.shape
    wide = round_up(rows, 128)
    heads = columns // WT
    return pl.pallas_call(
        turn_kernel,
        grid=(heads // PACK,),
        out_shape=jax.ShapeDtypeStruct((2, heads, WT, wide), bf16),
        in_specs=[pl.BlockSpec((rows, PACK * WT), lambda i: (0, i))] * 2,
        out_specs=pl.BlockSpec((2, PACK, WT, wide), lambda i: (0, i, 0, 0)),
        compiler_params=pltpu.CompilerParams(vmem_limit_bytes=56 * MIB),
        cost_estimate=pl.CostEstimate(flops=0, bytes_accessed=5_000_000, transcendentals=0),
        name="turn_teacher",
    )(tq, tk)


def read_pair(pairs, place):
    code = pairs[place]
    return code & 255, (code >> 8) & 255, code >> 16


def fill(block, slab, segments, keys, weights):
    width, wide = slab.shape
    rows = keys.shape[1]
    row = lax.broadcasted_iota(jnp.int32, (EXTRA, wide), 0)
    lane = lax.broadcasted_iota(jnp.int32, (EXTRA, wide), 1)
    hot = jnp.where(row == segments[pl.ds(block, 1)], 1.0, 0.0)
    key_extra = jnp.where((row >= DOCS) & (row < DOCS + 3), 1.0, hot)
    query_extra = jnp.where((row < DOCS) & (lane < rows), (hot - 1.0) * HIDDEN, 0.0)
    zeros = jnp.zeros((DEPTH - EXTRA - width, wide), bf16)
    weights[block] = jnp.concatenate([slab, query_extra.astype(bf16), zeros], axis=0)
    keys[block] = jnp.concatenate([slab, key_extra.astype(bf16), zeros], axis=0).T[:rows]
    values = slab.astype(f32)
    return jnp.sum(values * values, axis=0, keepdims=True)


def subtract_maxima(width, blocks, count, pairs, keys, weights, causal, sums):
    rows, wide = causal.shape[1:]

    def raise_maxima(place, carry):
        query, key, diagonal = read_pair(pairs, place + LAG)
        scores = jnp.dot(keys[key], weights[query], preferred_element_type=f32)
        scores = scores + causal[diagonal]
        top = jnp.max(scores.reshape(rows // 8, 8, wide), axis=0)
        sums[query] = jnp.where(diagonal == 1, top, jnp.maximum(top, sums[query]))
        return carry

    lax.fori_loop(0, count, raise_maxima, 0)
    row = lax.broadcasted_iota(jnp.int32, (EXTRA, wide), 0)

    def set_maxima(block, carry):
        rest = jnp.max(sums[block], axis=0, keepdims=True)
        extra = weights[block, width : width + EXTRA].astype(f32)
        for part in range(3):
            piece = rest.astype(bf16).astype(f32)
            rest = rest - piece
            extra = jnp.where(row == DOCS + part, -piece, extra)
        weights[block, width : width + EXTRA] = extra.astype(bf16)
        return carry

    lax.fori_loop(0, blocks, set_maxima, 0)


def fill_causal(causal):
    shape = causal.shape[1:]
    key_at = lax.broadcasted_iota(jnp.int32, shape, 0)
    query_at = lax.broadcasted_iota(jnp.int32, shape, 1)
    causal[0] = jnp.zeros(shape, f32)
    causal[1] = jnp.where(key_at <= query_at, 0.0, -HIDDEN)


def halves(rows):
    return (0, 128), (128, rows)


def weigh(place, blocks, pairs, keys, weights, scale, causal, target, sums):
    query, key, diagonal = read_pair(pairs, place + LAG)
    rows, wide = causal.shape[1:]
    key_block = jnp.minimum(key, blocks - 1)
    operand = weights[jnp.minimum(query, blocks - 1)]
    part = jnp.where(diagonal == 1, 0.0, sums[query])
    for low, high in halves(rows):
        scores = jnp.dot(keys[key_block, low:high], operand, preferred_element_type=f32)
        made = jnp.exp(scores * scale + causal[diagonal, low:high])
        target[low:high] = made
        part += jnp.sum(made.reshape((high - low) // 8, 8, wide), axis=0)
    sums[query] = part


def student_kernel(
    blocks, ends, segments, slabs_in, made, scales, features_out, pairs, count_out, slabs, features, keys, weights, ring, causal, sums, seen, opened, sem, sems
):
    rows, wide = causal.shape[1:]
    arrive = pltpu.make_async_copy(slabs_in, slabs, sem)
    arrive.start()
    fill_causal(causal)
    arrive.wait()

    def look(block, carry):
        seen[pl.ds(block, 1)] = slabs[block, :16, wide - 128 :].astype(f32)[:1].astype(jnp.int32)
        return carry

    lax.fori_loop(0, blocks, look, 0, unroll=8)
    fetch = pltpu.make_async_copy(seen, opened, sem)
    fetch.start()
    fetch.wait()
    mask_lane = rows % 128

    def list_pairs(block, total):
        for back in range(REACH):
            key = jnp.maximum(block - back, 0)
            code = block | (key << 8)
            if back == 0:
                pairs[total + LAG] = code | (1 << 16)
                total = total + 1
            else:
                pairs[total + LAG] = code
                is_open = (block >= back) & (opened[block, mask_lane + back - 1] == 1)
                is_open = is_open & (ends[0, block] == ends[1, key])
                total = total + is_open.astype(jnp.int32)
        return total

    lane = lax.broadcasted_iota(jnp.int32, (WS, wide), 1)

    def prepare(block, carry):
        peak, total = carry
        total = list_pairs(block, total)
        slab = jnp.where(lane < rows, slabs[block].astype(f32), 0.0).astype(bf16)
        features[block] = slab
        return jnp.maximum(peak, fill(block, slab, segments, keys, weights)), total

    peak, count = lax.fori_loop(0, blocks, prepare, (jnp.zeros((1, wide), f32), 0), unroll=4)
    count_out[0] = count
    for place in range(LAG):
        pairs[place] = blocks | (blocks << 8)
    for place in range(LAG + LISTED):
        pairs[count + LAG + place] = blocks | (blocks << 8)

    @pl.when(jnp.logical_not(jnp.max(peak) * SCALE_S <= SAFE))
    def _():
        subtract_maxima(WS, blocks, count, pairs, keys, weights, causal, sums)

    leave = pltpu.make_async_copy(features, features_out, sem)
    leave.start()

    def send(turn):
        slot = turn & (SLOTS - 1)
        group = made.at[pl.ds(turn * LISTED, LISTED)]
        return pltpu.make_async_copy(ring.at[slot], group, sems.at[slot])

    def steps(turn, carry):
        slot = turn & (SLOTS - 1)

        @pl.when(turn >= SLOTS)
        def _():
            send(turn - SLOTS).wait()

        for step in range(LISTED):
            place = LISTED * turn + step
            target = ring.at[slot, step]
            weigh(place, blocks, pairs, keys, weights, SCALE_S, causal, target, sums)
        send(turn).start()
        return carry

    turns = (count + LISTED - 1) // LISTED
    lax.fori_loop(0, turns, steps, 0)

    def drain(turn, carry):
        send(turn).wait()
        return carry

    lax.fori_loop(jnp.maximum(turns - SLOTS, 0), turns, drain, 0)
    leave.wait()

    def finish(block, carry):
        total = jnp.sum(sums[block], axis=0, keepdims=True) * math.sqrt(WS)
        scales[block] = jnp.broadcast_to(1.0 / total, (8, wide))
        return carry

    lax.fori_loop(0, blocks, finish, 0, unroll=8)


def student_weights(slabs, ends, segments, rows):
    blocks, _, wide = slabs.shape
    vmem = pl.BlockSpec(memory_space=pltpu.VMEM)
    smem = pl.BlockSpec(memory_space=pltpu.SMEM)
    hbm = pl.BlockSpec(memory_space=pl.ANY)
    slab = pltpu.VMEM((blocks, WS, wide), bf16)
    return pl.pallas_call(
        functools.partial(student_kernel, blocks),
        out_shape=(
            jax.ShapeDtypeStruct((blocks * REACH, rows, wide), f32),
            jax.ShapeDtypeStruct((blocks, 8, wide), f32),
            jax.ShapeDtypeStruct((blocks, WS, wide), bf16),
            jax.ShapeDtypeStruct((LIST,), jnp.int32),
            jax.ShapeDtypeStruct((1,), jnp.int32),
        ),
        in_specs=[smem, vmem, hbm],
        out_specs=(hbm, vmem, hbm, smem, smem),
        scratch_shapes=[
            slab,
            slab,
            pltpu.VMEM((blocks, rows, DEPTH), bf16),
            pltpu.VMEM((blocks, DEPTH, wide), bf16),
            pltpu.VMEM((SLOTS, LISTED, rows, wide), f32),
            pltpu.VMEM((2, rows, wide), f32),
            pltpu.VMEM((blocks + 1, 8, wide), f32),
            pltpu.VMEM((blocks, 128), jnp.int32),
            pltpu.SMEM((blocks, 128), jnp.int32),
            pltpu.SemaphoreType.DMA,
            pltpu.SemaphoreType.DMA((SLOTS,)),
        ],
        compiler_params=pltpu.CompilerParams(vmem_limit_bytes=48 * MIB),
        cost_estimate=pl.CostEstimate(
            flops=10_000_000_000, bytes_accessed=80_000_000, transcendentals=20_000_000
        ),
        name="student_weights",
    )(ends, segments, slabs)


def gradient_kernel(
    blocks, count_in, pairs, segments, slabs, made, scales, features_in, out, features, result, keys, weights, rings, fetched, causal, sums, grad, sems, sem, out_sems
):
    rows, wide = causal.shape[1:]
    count = count_in[0]
    arrive = pltpu.make_async_copy(features_in, features, sem)
    arrive.start()
    fill_causal(causal)

    def fetch(turn):
        group = jnp.clip(turn - LAG // UNROLL, 0, made.shape[0] // UNROLL - 1)
        slot = turn & (SLOTS - 1)
        group = made.at[pl.ds(group * UNROLL, UNROLL)]
        return pltpu.make_async_copy(group, fetched.at[slot], sems.at[slot])

    for turn in range(AHEAD):
        fetch(turn).start()

    def prepare(block, peak):
        grad[block] = jnp.zeros((WS, wide), f32)
        return jnp.maximum(peak, fill(block, slabs[block], segments, keys, weights))

    peak = lax.fori_loop(0, blocks, prepare, jnp.zeros((1, wide), f32), unroll=4)

    @pl.when(jnp.logical_not(jnp.max(peak) * SCALE_T <= SAFE))
    def _():
        subtract_maxima(WT, blocks, count, pairs, keys, weights, causal, sums)

    def readable(block):
        return jnp.minimum(block, blocks - 1)

    def inverses(place):
        query, _, _ = read_pair(pairs, place)
        total = jnp.sum(sums[query], axis=0, keepdims=True) * math.sqrt(WS)
        return 1.0 / total, scales[readable(query), :1]

    def couple(place, teacher, student, scale):
        query, key, _ = read_pair(pairs, place)
        query_side = features[readable(query)]
        to_queries = jnp.zeros((WS, wide), f32)
        for low, high in halves(rows):
            coupling = student[low:high] * scale[1] - teacher[low:high] * scale[0]
            coupling = coupling.astype(bf16)
            key_side = features[readable(key), :, low:high]
            grad[key, :, low:high] += lax.dot_general(
                query_side, coupling, (((1,), (1,)), ((), ())), preferred_element_type=f32
            )
            to_queries += jnp.dot(key_side, coupling, preferred_element_type=f32)
        grad[query] += to_queries

    def half(turn, parity):
        slot = turn & (SLOTS - 1)
        fetch(turn).wait()
        fetch(turn + AHEAD).start()
        scale = [inverses(UNROLL * turn + step) for step in range(UNROLL)]
        now = turn // 2 & 1
        before = (turn - LAG // UNROLL) // 2 & 1
        for step in range(UNROLL):
            place = UNROLL * turn + step
            old = rings[1 - parity].at[before, step]
            couple(place, old, fetched.at[slot, step], scale[step])
            target = rings[parity].at[now, step]
            weigh(place, blocks, pairs, keys, weights, SCALE_T, causal, target, sums)

    def steps(turn, carry):
        for parity in range(2):
            pl.when(turn & 1 == parity)(functools.partial(half, turn, parity))
        return carry

    turns = (count + LAG + UNROLL - 1) // UNROLL
    arrive.wait()
    lax.fori_loop(0, turns, steps, 0)
    for turn in range(AHEAD):
        fetch(turns + turn).wait()

    pieces = out_sems.shape[0]
    size = blocks // pieces

    def finish(block, carry):
        result[block] = grad[block].astype(bf16)
        return carry

    copies = []
    for piece in range(pieces):
        lax.fori_loop(piece * size, (piece + 1) * size, finish, 0, unroll=8)
        part = pl.ds(piece * size, size)
        copies.append(pltpu.make_async_copy(result.at[part], out.at[part], out_sems.at[piece]))
        copies[-1].start()
    for copy in copies:
        copy.wait()


def relation_gradient(slabs, segments, made, scales, features, pairs, count):
    blocks, _, wide = slabs.shape
    rows = made.shape[1]
    vmem = pl.BlockSpec(memory_space=pltpu.VMEM)
    smem = pl.BlockSpec(memory_space=pltpu.SMEM)
    hbm = pl.BlockSpec(memory_space=pl.ANY)
    slab = pltpu.VMEM((blocks, WS, wide), bf16)
    return pl.pallas_call(
        functools.partial(gradient_kernel, blocks),
        out_shape=jax.ShapeDtypeStruct((blocks, WS, wide), bf16),
        in_specs=[smem, smem, vmem, vmem, hbm, vmem, hbm],
        out_specs=hbm,
        scratch_shapes=[
            slab,
            slab,
            pltpu.VMEM((blocks, rows, DEPTH), bf16),
            pltpu.VMEM((blocks, DEPTH, wide), bf16),
            [pltpu.VMEM((2, UNROLL, rows, wide), f32)] * 2,
            pltpu.VMEM((SLOTS, UNROLL, rows, wide), f32),
            pltpu.VMEM((2, rows, wide), f32),
            pltpu.VMEM((blocks + 1, 8, wide), f32),
            pltpu.VMEM((blocks + 1, WS, wide), f32),
            pltpu.SemaphoreType.DMA((SLOTS,)),
            pltpu.SemaphoreType.DMA,
            pltpu.SemaphoreType.DMA((4,)),
        ],
        compiler_params=pltpu.CompilerParams(vmem_limit_bytes=48 * MIB),
        cost_estimate=pl.CostEstimate(
            flops=20_000_000_000, bytes_accessed=80_000_000, transcendentals=20_000_000
        ),
        name="relation_gradient",
    )(count, pairs, segments, slabs, made, scales, features)


def head_gradient(student, teacher, segment_ids, rows):
    blocks, _, wide = student.shape
    ends = jnp.stack([segment_ids[::rows], segment_ids[rows - 1 :: rows]])
    segments = jnp.pad(
        segment_ids.reshape(blocks, rows), ((0, 0), (0, wide - rows)), constant_values=-1
    )
    made, scales, features, pairs, count = student_weights(student, ends, segments, rows)
    return relation_gradient(teacher, segments, made, scales, features, pairs, count)


def unproject_kernel(grads, wq, wk, out):
    half = grads.shape[0] // 2
    rows, width = out.shape
    total = jnp.zeros((width, grads.shape[2]), f32)
    for rel, weight in enumerate((wq, wk)):
        turned = grads[rel * half : (rel + 1) * half].reshape(half * WS, grads.shape[2])
        total += jnp.dot(weight[...], turned, preferred_element_type=f32)
    out[...] = total.T[:rows].astype(out.dtype)


def unproject(grads, wq, wk, rows, dtype):
    width = wq.shape[0]
    vmem = pl.BlockSpec(memory_space=pltpu.VMEM)
    return pl.pallas_call(
        unproject_kernel,
        in_specs=[vmem, vmem, vmem],
        out_specs=vmem,
        out_shape=jax.ShapeDtypeStruct((rows, width), dtype),
        compiler_params=pltpu.CompilerParams(vmem_limit_bytes=32 * MIB),
        cost_estimate=pl.CostEstimate(
            flops=4 * rows * width * wq.shape[1], bytes_accessed=6_000_000, transcendentals=0
        ),
        name="unproject",
    )(grads, wq, wk)


def shards(teacher_query, teacher_key, student_hidden, w_query, w_key, segment_ids, block_mask):
    rows = student_hidden.shape[0]
    student = project(student_hidden, w_query, w_key, block_mask)
    teacher = turn(teacher_query, teacher_key)
    student = lax.all_to_all(student.reshape(-1, *student.shape[2:]), "ctx", 0, 0, tiled=True)
    teacher = lax.all_to_all(teacher.reshape(-1, *teacher.shape[2:]), "ctx", 0, 0, tiled=True)
    turned = head_gradient(student, teacher, segment_ids, rows)
    side = lax.axis_index("head")
    width = w_query.shape[0] // 2
    turned, side = lax.optimization_barrier((turned, side))
    cut = [
        [lax.dynamic_slice_in_dim(weight, part * width, width, 0) for weight in (w_query, w_key)]
        for part in (1 - side, side)
    ]
    cut = lax.optimization_barrier(cut)
    back = lax.all_to_all(turned, "ctx", 0, 0, tiled=True)
    away = unproject(back, *cut[0], rows, bf16)
    away = lax.ppermute(away, "head", [(0, 1), (1, 0)])
    own = unproject(back, *cut[1], rows, f32)
    return (own + away).astype(bf16)


def solution(mesh):
    placed = (
        P("ctx", "head"),
        P("ctx", "head"),
        P("ctx", None),
        P(None, "head"),
        P(None, "head"),
        P(),
        P("ctx", None),
    )
    return jax.shard_map(
        shards, mesh=mesh, in_specs=placed, out_specs=P("ctx", "head"), check_vma=False
    )
```

```python
import functools
import math

import jax
import jax.numpy as jnp
from jax import lax
from jax.experimental import pallas as pl
from jax.experimental.pallas import tpu as pltpu
from jax.sharding import PartitionSpec as P

DT = 5120
DS = 2048
HEADS = 64
REACH = 8
WT = DT // HEADS
WS = DS // HEADS
DEPTH = 128
EXTRA = 16
DOCS = 4
PACK = 8
LISTED = 8
UNROLL = 10
LAG = 3 * UNROLL
SLOTS = 4
AHEAD = 2
LIST = 640
HIDDEN = 1e30
SCALE_T = 1.0 / math.sqrt(WT)
SCALE_S = 1.0 / math.sqrt(WS)
SAFE = 60.0
MIB = 1024 * 1024
f32 = jnp.float32
bf16 = jnp.bfloat16


def round_up(value, unit):
    return (value + unit - 1) // unit * unit


def project_kernel(mask, hidden, wq, wk, out):
    rows, wide = hidden.shape[0], out.shape[-1]
    row = lax.broadcasted_iota(jnp.int32, (wide - rows, PACK * WS), 0)
    extra = jnp.zeros(row.shape, f32)
    for back in range(REACH - 1):
        extra = jnp.where(row == back, mask[0, back].astype(f32), extra)
    extra = extra.astype(bf16)
    for rel, weight in enumerate((wq, wk)):
        student = jnp.dot(hidden[...], weight[...], preferred_element_type=f32).astype(bf16)
        turned = jnp.concatenate([student, extra], axis=0).T
        out[rel] = turned.reshape(out.shape[1:])


def project(hidden, wq, wk, mask):
    rows = hidden.shape[0]
    wide = round_up(rows, 128)
    heads = wq.shape[1] // WS
    return pl.pallas_call(
        project_kernel,
        grid=(heads // PACK,),
        out_shape=jax.ShapeDtypeStruct((2, heads, WS, wide), bf16),
        in_specs=[
            pl.BlockSpec(memory_space=pltpu.SMEM),
            pl.BlockSpec((rows, DS), lambda i: (0, 0)),
            pl.BlockSpec((DS, PACK * WS), lambda i: (0, i)),
            pl.BlockSpec((DS, PACK * WS), lambda i: (0, i)),
        ],
        out_specs=pl.BlockSpec((2, PACK, WS, wide), lambda i: (0, i, 0, 0)),
        compiler_params=pltpu.CompilerParams(vmem_limit_bytes=56 * MIB),
        cost_estimate=pl.CostEstimate(
            flops=4 * rows * DS * heads * WS, bytes_accessed=10_000_000, transcendentals=0
        ),
        name="project_student",
    )(mask, hidden, wq, wk)


def turn_kernel(tq, tk, out):
    rows = tq.shape[0]
    wide = out.shape[-1]
    for rel, teacher in enumerate((tq, tk)):
        zeros = jnp.zeros((wide - rows, teacher.shape[1]), bf16)
        turned = jnp.concatenate([teacher[...], zeros], axis=0).T
        out[rel] = turned.reshape(out.shape[1:])


def turn(tq, tk):
    rows, columns = tq.shape
    wide = round_up(rows, 128)
    heads = columns // WT
    return pl.pallas_call(
        turn_kernel,
        grid=(heads // PACK,),
        out_shape=jax.ShapeDtypeStruct((2, heads, WT, wide), bf16),
        in_specs=[pl.BlockSpec((rows, PACK * WT), lambda i: (0, i))] * 2,
        out_specs=pl.BlockSpec((2, PACK, WT, wide), lambda i: (0, i, 0, 0)),
        compiler_params=pltpu.CompilerParams(vmem_limit_bytes=56 * MIB),
        cost_estimate=pl.CostEstimate(flops=0, bytes_accessed=5_000_000, transcendentals=0),
        name="turn_teacher",
    )(tq, tk)


def read_pair(pairs, place):
    code = pairs[place]
    return code & 255, (code >> 8) & 255, code >> 16


def fill(block, slab, segments, keys, weights):
    width, wide = slab.shape
    rows = keys.shape[1]
    row = lax.broadcasted_iota(jnp.int32, (EXTRA, wide), 0)
    lane = lax.broadcasted_iota(jnp.int32, (EXTRA, wide), 1)
    hot = jnp.where(row == segments[pl.ds(block, 1)], 1.0, 0.0)
    key_extra = jnp.where((row >= DOCS) & (row < DOCS + 3), 1.0, hot)
    query_extra = jnp.where((row < DOCS) & (lane < rows), (hot - 1.0) * HIDDEN, 0.0)
    zeros = jnp.zeros((DEPTH - EXTRA - width, wide), bf16)
    weights[block] = jnp.concatenate([slab, query_extra.astype(bf16), zeros], axis=0)
    keys[block] = jnp.concatenate([slab, key_extra.astype(bf16), zeros], axis=0).T[:rows]
    values = slab.astype(f32)
    return jnp.sum(values * values, axis=0, keepdims=True)


def subtract_maxima(width, blocks, count, pairs, keys, weights, causal, sums):
    rows, wide = causal.shape[1:]

    def raise_maxima(place, carry):
        query, key, diagonal = read_pair(pairs, place + LAG)
        scores = jnp.dot(keys[key], weights[query], preferred_element_type=f32)
        scores = scores + causal[diagonal]
        top = jnp.max(scores.reshape(rows // 8, 8, wide), axis=0)
        sums[query] = jnp.where(diagonal == 1, top, jnp.maximum(top, sums[query]))
        return carry

    lax.fori_loop(0, count, raise_maxima, 0)
    row = lax.broadcasted_iota(jnp.int32, (EXTRA, wide), 0)

    def set_maxima(block, carry):
        rest = jnp.max(sums[block], axis=0, keepdims=True)
        extra = weights[block, width : width + EXTRA].astype(f32)
        for part in range(3):
            piece = rest.astype(bf16).astype(f32)
            rest = rest - piece
            extra = jnp.where(row == DOCS + part, -piece, extra)
        weights[block, width : width + EXTRA] = extra.astype(bf16)
        return carry

    lax.fori_loop(0, blocks, set_maxima, 0)


def fill_causal(causal):
    shape = causal.shape[1:]
    key_at = lax.broadcasted_iota(jnp.int32, shape, 0)
    query_at = lax.broadcasted_iota(jnp.int32, shape, 1)
    causal[0] = jnp.zeros(shape, f32)
    causal[1] = jnp.where(key_at <= query_at, 0.0, -HIDDEN)


def halves(rows):
    return (0, 128), (128, rows)


def weigh(place, blocks, pairs, keys, weights, scale, causal, target, sums):
    query, key, diagonal = read_pair(pairs, place + LAG)
    rows, wide = causal.shape[1:]
    key_block = jnp.minimum(key, blocks - 1)
    operand = weights[jnp.minimum(query, blocks - 1)]
    part = jnp.where(diagonal == 1, 0.0, sums[query])
    for low, high in halves(rows):
        scores = jnp.dot(keys[key_block, low:high], operand, preferred_element_type=f32)
        made = jnp.exp(scores * scale + causal[diagonal, low:high])
        target[low:high] = made
        part += jnp.sum(made.reshape((high - low) // 8, 8, wide), axis=0)
    sums[query] = part


def student_kernel(
    blocks, ends, segments, slabs_in, made, scales, features_out, pairs, count_out, slabs, features, keys, weights, ring, causal, sums, seen, opened, sem, sems
):
    rows, wide = causal.shape[1:]
    arrive = pltpu.make_async_copy(slabs_in, slabs, sem)
    arrive.start()
    fill_causal(causal)
    arrive.wait()

    def look(block, carry):
        seen[pl.ds(block, 1)] = slabs[block, :16, wide - 128 :].astype(f32)[:1].astype(jnp.int32)
        return carry

    lax.fori_loop(0, blocks, look, 0, unroll=8)
    fetch = pltpu.make_async_copy(seen, opened, sem)
    fetch.start()
    fetch.wait()
    mask_lane = rows % 128

    def list_pairs(block, total):
        for back in range(REACH):
            key = jnp.maximum(block - back, 0)
            code = block | (key << 8)
            if back == 0:
                pairs[total + LAG] = code | (1 << 16)
                total = total + 1
            else:
                pairs[total + LAG] = code
                is_open = (block >= back) & (opened[block, mask_lane + back - 1] == 1)
                is_open = is_open & (ends[0, block] == ends[1, key])
                total = total + is_open.astype(jnp.int32)
        return total

    lane = lax.broadcasted_iota(jnp.int32, (WS, wide), 1)

    def prepare(block, carry):
        peak, total = carry
        total = list_pairs(block, total)
        slab = jnp.where(lane < rows, slabs[block].astype(f32), 0.0).astype(bf16)
        features[block] = slab
        return jnp.maximum(peak, fill(block, slab, segments, keys, weights)), total

    peak, count = lax.fori_loop(0, blocks, prepare, (jnp.zeros((1, wide), f32), 0), unroll=4)
    count_out[0] = count
    for place in range(LAG):
        pairs[place] = blocks | (blocks << 8)
    for place in range(LAG + UNROLL + LISTED):
        pairs[count + LAG + place] = blocks | (blocks << 8)

    @pl.when(jnp.logical_not(jnp.max(peak) * SCALE_S <= SAFE))
    def _():
        subtract_maxima(WS, blocks, count, pairs, keys, weights, causal, sums)

    leave = pltpu.make_async_copy(features, features_out, sem)
    leave.start()

    def send(turn):
        slot = turn & (SLOTS - 1)
        group = made.at[pl.ds(turn * LISTED, LISTED)]
        return pltpu.make_async_copy(ring.at[slot], group, sems.at[slot])

    def steps(turn, carry):
        slot = turn & (SLOTS - 1)

        @pl.when(turn >= SLOTS)
        def _():
            send(turn - SLOTS).wait()

        for step in range(LISTED):
            place = LISTED * turn + step
            target = ring.at[slot, step]
            weigh(place, blocks, pairs, keys, weights, SCALE_S, causal, target, sums)
        send(turn).start()
        return carry

    turns = (count + LISTED - 1) // LISTED
    lax.fori_loop(0, turns, steps, 0)

    def drain(turn, carry):
        send(turn).wait()
        return carry

    lax.fori_loop(jnp.maximum(turns - SLOTS, 0), turns, drain, 0)
    leave.wait()

    def finish(block, carry):
        total = jnp.sum(sums[block], axis=0, keepdims=True) * math.sqrt(WS)
        scales[block] = jnp.broadcast_to(1.0 / total, (8, wide))
        return carry

    lax.fori_loop(0, blocks, finish, 0, unroll=8)


def student_weights(slabs, ends, segments, rows):
    blocks, _, wide = slabs.shape
    vmem = pl.BlockSpec(memory_space=pltpu.VMEM)
    smem = pl.BlockSpec(memory_space=pltpu.SMEM)
    hbm = pl.BlockSpec(memory_space=pl.ANY)
    slab = pltpu.VMEM((blocks, WS, wide), bf16)
    return pl.pallas_call(
        functools.partial(student_kernel, blocks),
        out_shape=(
            jax.ShapeDtypeStruct((blocks * REACH, rows, wide), f32),
            jax.ShapeDtypeStruct((blocks, 8, wide), f32),
            jax.ShapeDtypeStruct((blocks, WS, wide), bf16),
            jax.ShapeDtypeStruct((LIST,), jnp.int32),
            jax.ShapeDtypeStruct((1,), jnp.int32),
        ),
        in_specs=[smem, vmem, hbm],
        out_specs=(hbm, vmem, hbm, smem, smem),
        scratch_shapes=[
            slab,
            slab,
            pltpu.VMEM((blocks, rows, DEPTH), bf16),
            pltpu.VMEM((blocks, DEPTH, wide), bf16),
            pltpu.VMEM((SLOTS, LISTED, rows, wide), f32),
            pltpu.VMEM((2, rows, wide), f32),
            pltpu.VMEM((blocks + 1, 8, wide), f32),
            pltpu.VMEM((blocks, 128), jnp.int32),
            pltpu.SMEM((blocks, 128), jnp.int32),
            pltpu.SemaphoreType.DMA,
            pltpu.SemaphoreType.DMA((SLOTS,)),
        ],
        compiler_params=pltpu.CompilerParams(vmem_limit_bytes=48 * MIB),
        cost_estimate=pl.CostEstimate(
            flops=10_000_000_000, bytes_accessed=80_000_000, transcendentals=20_000_000
        ),
        name="student_weights",
    )(ends, segments, slabs)


def gradient_kernel(
    blocks, count_in, pairs, segments, slabs, made, scales, features_in, out, features, result, keys, weights, rings, fetched, causal, sums, grad, sems, sem, out_sems
):
    rows, wide = causal.shape[1:]
    count = count_in[0]
    arrive = pltpu.make_async_copy(features_in, features, sem)
    arrive.start()
    fill_causal(causal)

    def fetch(turn):
        group = jnp.clip(turn - LAG // UNROLL, 0, made.shape[0] // UNROLL - 1)
        slot = turn & (SLOTS - 1)
        group = made.at[pl.ds(group * UNROLL, UNROLL)]
        return pltpu.make_async_copy(group, fetched.at[slot], sems.at[slot])

    for turn in range(AHEAD):
        fetch(turn).start()

    def prepare(block, peak):
        grad[block] = jnp.zeros((WS, wide), f32)
        return jnp.maximum(peak, fill(block, slabs[block], segments, keys, weights))

    peak = lax.fori_loop(0, blocks, prepare, jnp.zeros((1, wide), f32), unroll=4)

    @pl.when(jnp.logical_not(jnp.max(peak) * SCALE_T <= SAFE))
    def _():
        subtract_maxima(WT, blocks, count, pairs, keys, weights, causal, sums)

    def readable(block):
        return jnp.minimum(block, blocks - 1)

    def inverses(place):
        query, _, _ = read_pair(pairs, place)
        total = jnp.sum(sums[query], axis=0, keepdims=True) * math.sqrt(WS)
        return 1.0 / total, scales[readable(query), :1]

    def couple(place, teacher, student, scale):
        query, key, _ = read_pair(pairs, place)
        query_side = features[readable(query)]
        to_queries = jnp.zeros((WS, wide), f32)
        for low, high in halves(rows):
            coupling = student[low:high] * scale[1] - teacher[low:high] * scale[0]
            coupling = coupling.astype(bf16)
            key_side = features[readable(key), :, low:high]
            grad[key, :, low:high] += lax.dot_general(
                query_side, coupling, (((1,), (1,)), ((), ())), preferred_element_type=f32
            )
            to_queries += jnp.dot(key_side, coupling, preferred_element_type=f32)
        grad[query] += to_queries

    def half(turn, parity):
        slot = turn & (SLOTS - 1)
        fetch(turn).wait()
        fetch(turn + AHEAD).start()
        scale = [inverses(UNROLL * turn + step) for step in range(UNROLL)]
        now = turn // 2 & 1
        before = (turn - LAG // UNROLL) // 2 & 1
        for step in range(UNROLL):
            place = UNROLL * turn + step
            old = rings[1 - parity].at[before, step]
            couple(place, old, fetched.at[slot, step], scale[step])
            target = rings[parity].at[now, step]
            weigh(place, blocks, pairs, keys, weights, SCALE_T, causal, target, sums)

    def steps(turn, carry):
        for parity in range(2):
            pl.when(turn & 1 == parity)(functools.partial(half, turn, parity))
        return carry

    turns = (count + LAG + UNROLL - 1) // UNROLL
    arrive.wait()
    lax.fori_loop(0, turns, steps, 0)
    for turn in range(AHEAD):
        fetch(turns + turn).wait()

    pieces = out_sems.shape[0]
    size = blocks // pieces

    def finish(block, carry):
        result[block] = grad[block].astype(bf16)
        return carry

    copies = []
    for piece in range(pieces):
        lax.fori_loop(piece * size, (piece + 1) * size, finish, 0, unroll=8)
        part = pl.ds(piece * size, size)
        copies.append(pltpu.make_async_copy(result.at[part], out.at[part], out_sems.at[piece]))
        copies[-1].start()
    for copy in copies:
        copy.wait()


def relation_gradient(slabs, segments, made, scales, features, pairs, count):
    blocks, _, wide = slabs.shape
    rows = made.shape[1]
    vmem = pl.BlockSpec(memory_space=pltpu.VMEM)
    smem = pl.BlockSpec(memory_space=pltpu.SMEM)
    hbm = pl.BlockSpec(memory_space=pl.ANY)
    slab = pltpu.VMEM((blocks, WS, wide), bf16)
    return pl.pallas_call(
        functools.partial(gradient_kernel, blocks),
        out_shape=jax.ShapeDtypeStruct((blocks, WS, wide), bf16),
        in_specs=[smem, smem, vmem, vmem, hbm, vmem, hbm],
        out_specs=hbm,
        scratch_shapes=[
            slab,
            slab,
            pltpu.VMEM((blocks, rows, DEPTH), bf16),
            pltpu.VMEM((blocks, DEPTH, wide), bf16),
            [pltpu.VMEM((2, UNROLL, rows, wide), f32)] * 2,
            pltpu.VMEM((SLOTS, UNROLL, rows, wide), f32),
            pltpu.VMEM((2, rows, wide), f32),
            pltpu.VMEM((blocks + 1, 8, wide), f32),
            pltpu.VMEM((blocks + 1, WS, wide), f32),
            pltpu.SemaphoreType.DMA((SLOTS,)),
            pltpu.SemaphoreType.DMA,
            pltpu.SemaphoreType.DMA((4,)),
        ],
        compiler_params=pltpu.CompilerParams(vmem_limit_bytes=48 * MIB),
        cost_estimate=pl.CostEstimate(
            flops=20_000_000_000, bytes_accessed=80_000_000, transcendentals=20_000_000
        ),
        name="relation_gradient",
    )(count, pairs, segments, slabs, made, scales, features)


def head_gradient(student, teacher, segment_ids, rows):
    blocks, _, wide = student.shape
    ends = jnp.stack([segment_ids[::rows], segment_ids[rows - 1 :: rows]])
    segments = jnp.pad(
        segment_ids.reshape(blocks, rows), ((0, 0), (0, wide - rows)), constant_values=-1
    )
    made, scales, features, pairs, count = student_weights(student, ends, segments, rows)
    return relation_gradient(teacher, segments, made, scales, features, pairs, count)


def unproject_kernel(grads, wq, wk, out):
    half = grads.shape[0] // 2
    rows, width = out.shape
    total = jnp.zeros((width, grads.shape[2]), f32)
    for rel, weight in enumerate((wq, wk)):
        turned = grads[rel * half : (rel + 1) * half].reshape(half * WS, grads.shape[2])
        total += jnp.dot(weight[...], turned, preferred_element_type=f32)
    out[...] = total.T[:rows].astype(out.dtype)


def unproject(grads, wq, wk, rows, dtype):
    width = wq.shape[0]
    vmem = pl.BlockSpec(memory_space=pltpu.VMEM)
    return pl.pallas_call(
        unproject_kernel,
        in_specs=[vmem, vmem, vmem],
        out_specs=vmem,
        out_shape=jax.ShapeDtypeStruct((rows, width), dtype),
        compiler_params=pltpu.CompilerParams(vmem_limit_bytes=32 * MIB),
        cost_estimate=pl.CostEstimate(
            flops=4 * rows * width * wq.shape[1], bytes_accessed=6_000_000, transcendentals=0
        ),
        name="unproject",
    )(grads, wq, wk)


def shards(teacher_query, teacher_key, student_hidden, w_query, w_key, segment_ids, block_mask):
    rows = student_hidden.shape[0]
    student = project(student_hidden, w_query, w_key, block_mask)
    teacher = turn(teacher_query, teacher_key)
    student = lax.all_to_all(student.reshape(-1, *student.shape[2:]), "ctx", 0, 0, tiled=True)
    teacher = lax.all_to_all(teacher.reshape(-1, *teacher.shape[2:]), "ctx", 0, 0, tiled=True)
    turned = head_gradient(student, teacher, segment_ids, rows)
    side = lax.axis_index("head")
    width = w_query.shape[0] // 2
    turned, side = lax.optimization_barrier((turned, side))
    cut = [
        [lax.dynamic_slice_in_dim(weight, part * width, width, 0) for weight in (w_query, w_key)]
        for part in (1 - side, side)
    ]
    cut = lax.optimization_barrier(cut)
    back = lax.all_to_all(turned, "ctx", 0, 0, tiled=True)
    away = unproject(back, *cut[0], rows, bf16)
    away = lax.ppermute(away, "head", [(0, 1), (1, 0)])
    own = unproject(back, *cut[1], rows, f32)
    return (own + away).astype(bf16)


def solution(mesh):
    placed = (
        P("ctx", "head"),
        P("ctx", "head"),
        P("ctx", None),
        P(None, "head"),
        P(None, "head"),
        P(),
        P("ctx", None),
    )
    return jax.shard_map(
        shards, mesh=mesh, in_specs=placed, out_specs=P("ctx", "head"), check_vma=False
    )
```

```python
import functools
import math

import jax
import jax.numpy as jnp
from jax import lax
from jax.experimental import pallas as pl
from jax.experimental.pallas import tpu as pltpu
from jax.sharding import PartitionSpec as P

DT = 5120
DS = 2048
HEADS = 64
REACH = 8
WT = DT // HEADS
WS = DS // HEADS
DEPTH = 128
EXTRA = 16
DOCS = 4
PACK = 8
LISTED = 8
UNROLL = 16
LAG = 3 * UNROLL
SLOTS = 4
AHEAD = 2
LIST = 640
HIDDEN = 1e30
SCALE_T = 1.0 / math.sqrt(WT)
SCALE_S = 1.0 / math.sqrt(WS)
SAFE = 60.0
MIB = 1024 * 1024
f32 = jnp.float32
bf16 = jnp.bfloat16


def round_up(value, unit):
    return (value + unit - 1) // unit * unit


def project_kernel(mask, hidden, wq, wk, out):
    rows, wide = hidden.shape[0], out.shape[-1]
    row = lax.broadcasted_iota(jnp.int32, (wide - rows, PACK * WS), 0)
    extra = jnp.zeros(row.shape, f32)
    for back in range(REACH - 1):
        extra = jnp.where(row == back, mask[0, back].astype(f32), extra)
    extra = extra.astype(bf16)
    for rel, weight in enumerate((wq, wk)):
        student = jnp.dot(hidden[...], weight[...], preferred_element_type=f32).astype(bf16)
        turned = jnp.concatenate([student, extra], axis=0).T
        out[rel] = turned.reshape(out.shape[1:])


def project(hidden, wq, wk, mask):
    rows = hidden.shape[0]
    wide = round_up(rows, 128)
    heads = wq.shape[1] // WS
    return pl.pallas_call(
        project_kernel,
        grid=(heads // PACK,),
        out_shape=jax.ShapeDtypeStruct((2, heads, WS, wide), bf16),
        in_specs=[
            pl.BlockSpec(memory_space=pltpu.SMEM),
            pl.BlockSpec((rows, DS), lambda i: (0, 0)),
            pl.BlockSpec((DS, PACK * WS), lambda i: (0, i)),
            pl.BlockSpec((DS, PACK * WS), lambda i: (0, i)),
        ],
        out_specs=pl.BlockSpec((2, PACK, WS, wide), lambda i: (0, i, 0, 0)),
        compiler_params=pltpu.CompilerParams(vmem_limit_bytes=56 * MIB),
        cost_estimate=pl.CostEstimate(
            flops=4 * rows * DS * heads * WS, bytes_accessed=10_000_000, transcendentals=0
        ),
        name="project_student",
    )(mask, hidden, wq, wk)


def turn_kernel(tq, tk, out):
    rows = tq.shape[0]
    wide = out.shape[-1]
    for rel, teacher in enumerate((tq, tk)):
        zeros = jnp.zeros((wide - rows, teacher.shape[1]), bf16)
        turned = jnp.concatenate([teacher[...], zeros], axis=0).T
        out[rel] = turned.reshape(out.shape[1:])


def turn(tq, tk):
    rows, columns = tq.shape
    wide = round_up(rows, 128)
    heads = columns // WT
    return pl.pallas_call(
        turn_kernel,
        grid=(heads // PACK,),
        out_shape=jax.ShapeDtypeStruct((2, heads, WT, wide), bf16),
        in_specs=[pl.BlockSpec((rows, PACK * WT), lambda i: (0, i))] * 2,
        out_specs=pl.BlockSpec((2, PACK, WT, wide), lambda i: (0, i, 0, 0)),
        compiler_params=pltpu.CompilerParams(vmem_limit_bytes=56 * MIB),
        cost_estimate=pl.CostEstimate(flops=0, bytes_accessed=5_000_000, transcendentals=0),
        name="turn_teacher",
    )(tq, tk)


def read_pair(pairs, place):
    code = pairs[place]
    return code & 255, (code >> 8) & 255, code >> 16


def fill(block, slab, segments, keys, weights):
    width, wide = slab.shape
    rows = keys.shape[1]
    row = lax.broadcasted_iota(jnp.int32, (EXTRA, wide), 0)
    lane = lax.broadcasted_iota(jnp.int32, (EXTRA, wide), 1)
    hot = jnp.where(row == segments[pl.ds(block, 1)], 1.0, 0.0)
    key_extra = jnp.where((row >= DOCS) & (row < DOCS + 3), 1.0, hot)
    query_extra = jnp.where((row < DOCS) & (lane < rows), (hot - 1.0) * HIDDEN, 0.0)
    zeros = jnp.zeros((DEPTH - EXTRA - width, wide), bf16)
    weights[block] = jnp.concatenate([slab, query_extra.astype(bf16), zeros], axis=0)
    keys[block] = jnp.concatenate([slab, key_extra.astype(bf16), zeros], axis=0).T[:rows]
    values = slab.astype(f32)
    return jnp.sum(values * values, axis=0, keepdims=True)


def subtract_maxima(width, blocks, count, pairs, keys, weights, causal, sums):
    rows, wide = causal.shape[1:]

    def raise_maxima(place, carry):
        query, key, diagonal = read_pair(pairs, place + LAG)
        scores = jnp.dot(keys[key], weights[query], preferred_element_type=f32)
        scores = scores + causal[diagonal]
        top = jnp.max(scores.reshape(rows // 8, 8, wide), axis=0)
        sums[query] = jnp.where(diagonal == 1, top, jnp.maximum(top, sums[query]))
        return carry

    lax.fori_loop(0, count, raise_maxima, 0)
    row = lax.broadcasted_iota(jnp.int32, (EXTRA, wide), 0)

    def set_maxima(block, carry):
        rest = jnp.max(sums[block], axis=0, keepdims=True)
        extra = weights[block, width : width + EXTRA].astype(f32)
        for part in range(3):
            piece = rest.astype(bf16).astype(f32)
            rest = rest - piece
            extra = jnp.where(row == DOCS + part, -piece, extra)
        weights[block, width : width + EXTRA] = extra.astype(bf16)
        return carry

    lax.fori_loop(0, blocks, set_maxima, 0)


def fill_causal(causal):
    shape = causal.shape[1:]
    key_at = lax.broadcasted_iota(jnp.int32, shape, 0)
    query_at = lax.broadcasted_iota(jnp.int32, shape, 1)
    causal[0] = jnp.zeros(shape, f32)
    causal[1] = jnp.where(key_at <= query_at, 0.0, -HIDDEN)


def halves(rows):
    return (0, 128), (128, rows)


def weigh(place, blocks, pairs, keys, weights, scale, causal, target, sums):
    query, key, diagonal = read_pair(pairs, place + LAG)
    rows, wide = causal.shape[1:]
    key_block = jnp.minimum(key, blocks - 1)
    operand = weights[jnp.minimum(query, blocks - 1)]
    part = jnp.where(diagonal == 1, 0.0, sums[query])
    for low, high in halves(rows):
        scores = jnp.dot(keys[key_block, low:high], operand, preferred_element_type=f32)
        made = jnp.exp(scores * scale + causal[diagonal, low:high])
        target[low:high] = made
        part += jnp.sum(made.reshape((high - low) // 8, 8, wide), axis=0)
    sums[query] = part


def student_kernel(
    blocks, ends, segments, slabs_in, made, scales, features_out, pairs, count_out, slabs, features, keys, weights, ring, causal, sums, seen, opened, sem, sems
):
    rows, wide = causal.shape[1:]
    arrive = pltpu.make_async_copy(slabs_in, slabs, sem)
    arrive.start()
    fill_causal(causal)
    arrive.wait()

    def look(block, carry):
        seen[pl.ds(block, 1)] = slabs[block, :16, wide - 128 :].astype(f32)[:1].astype(jnp.int32)
        return carry

    lax.fori_loop(0, blocks, look, 0, unroll=8)
    fetch = pltpu.make_async_copy(seen, opened, sem)
    fetch.start()
    fetch.wait()
    mask_lane = rows % 128

    def list_pairs(block, total):
        for back in range(REACH):
            key = jnp.maximum(block - back, 0)
            code = block | (key << 8)
            if back == 0:
                pairs[total + LAG] = code | (1 << 16)
                total = total + 1
            else:
                pairs[total + LAG] = code
                is_open = (block >= back) & (opened[block, mask_lane + back - 1] == 1)
                is_open = is_open & (ends[0, block] == ends[1, key])
                total = total + is_open.astype(jnp.int32)
        return total

    lane = lax.broadcasted_iota(jnp.int32, (WS, wide), 1)

    def prepare(block, carry):
        peak, total = carry
        total = list_pairs(block, total)
        slab = jnp.where(lane < rows, slabs[block].astype(f32), 0.0).astype(bf16)
        features[block] = slab
        return jnp.maximum(peak, fill(block, slab, segments, keys, weights)), total

    peak, count = lax.fori_loop(0, blocks, prepare, (jnp.zeros((1, wide), f32), 0), unroll=4)
    count_out[0] = count
    for place in range(LAG):
        pairs[place] = blocks | (blocks << 8)
    for place in range(LAG + UNROLL + LISTED):
        pairs[count + LAG + place] = blocks | (blocks << 8)

    @pl.when(jnp.logical_not(jnp.max(peak) * SCALE_S <= SAFE))
    def _():
        subtract_maxima(WS, blocks, count, pairs, keys, weights, causal, sums)

    leave = pltpu.make_async_copy(features, features_out, sem)
    leave.start()

    def send(turn):
        slot = turn & (SLOTS - 1)
        group = made.at[pl.ds(turn * LISTED, LISTED)]
        return pltpu.make_async_copy(ring.at[slot], group, sems.at[slot])

    def steps(turn, carry):
        slot = turn & (SLOTS - 1)

        @pl.when(turn >= SLOTS)
        def _():
            send(turn - SLOTS).wait()

        for step in range(LISTED):
            place = LISTED * turn + step
            target = ring.at[slot, step]
            weigh(place, blocks, pairs, keys, weights, SCALE_S, causal, target, sums)
        send(turn).start()
        return carry

    turns = (count + LISTED - 1) // LISTED
    lax.fori_loop(0, turns, steps, 0)

    def drain(turn, carry):
        send(turn).wait()
        return carry

    lax.fori_loop(jnp.maximum(turns - SLOTS, 0), turns, drain, 0)
    leave.wait()

    def finish(block, carry):
        total = jnp.sum(sums[block], axis=0, keepdims=True) * math.sqrt(WS)
        scales[block] = jnp.broadcast_to(1.0 / total, (8, wide))
        return carry

    lax.fori_loop(0, blocks, finish, 0, unroll=8)


def student_weights(slabs, ends, segments, rows):
    blocks, _, wide = slabs.shape
    vmem = pl.BlockSpec(memory_space=pltpu.VMEM)
    smem = pl.BlockSpec(memory_space=pltpu.SMEM)
    hbm = pl.BlockSpec(memory_space=pl.ANY)
    slab = pltpu.VMEM((blocks, WS, wide), bf16)
    return pl.pallas_call(
        functools.partial(student_kernel, blocks),
        out_shape=(
            jax.ShapeDtypeStruct((blocks * REACH, rows, wide), f32),
            jax.ShapeDtypeStruct((blocks, 8, wide), f32),
            jax.ShapeDtypeStruct((blocks, WS, wide), bf16),
            jax.ShapeDtypeStruct((LIST,), jnp.int32),
            jax.ShapeDtypeStruct((1,), jnp.int32),
        ),
        in_specs=[smem, vmem, hbm],
        out_specs=(hbm, vmem, hbm, smem, smem),
        scratch_shapes=[
            slab,
            slab,
            pltpu.VMEM((blocks, rows, DEPTH), bf16),
            pltpu.VMEM((blocks, DEPTH, wide), bf16),
            pltpu.VMEM((SLOTS, LISTED, rows, wide), f32),
            pltpu.VMEM((2, rows, wide), f32),
            pltpu.VMEM((blocks + 1, 8, wide), f32),
            pltpu.VMEM((blocks, 128), jnp.int32),
            pltpu.SMEM((blocks, 128), jnp.int32),
            pltpu.SemaphoreType.DMA,
            pltpu.SemaphoreType.DMA((SLOTS,)),
        ],
        compiler_params=pltpu.CompilerParams(vmem_limit_bytes=48 * MIB),
        cost_estimate=pl.CostEstimate(
            flops=10_000_000_000, bytes_accessed=80_000_000, transcendentals=20_000_000
        ),
        name="student_weights",
    )(ends, segments, slabs)


def gradient_kernel(
    blocks, count_in, pairs, segments, slabs, made, scales, features_in, out, features, result, keys, weights, rings, fetched, causal, sums, grad, key_grad, sems, sem, out_sems
):
    rows, wide = causal.shape[1:]
    count = count_in[0]
    arrive = pltpu.make_async_copy(features_in, features, sem)
    arrive.start()
    fill_causal(causal)

    def fetch(turn):
        group = jnp.clip(turn - LAG // UNROLL, 0, made.shape[0] // UNROLL - 1)
        slot = lax.rem(turn, AHEAD + 1)
        group = made.at[pl.ds(group * UNROLL, UNROLL)]
        return pltpu.make_async_copy(group, fetched.at[slot], sems.at[slot])

    for turn in range(AHEAD):
        fetch(turn).start()

    def prepare(block, peak):
        grad[block] = jnp.zeros((WS, wide), f32)
        key_grad[block] = jnp.zeros((WS, wide), f32)
        return jnp.maximum(peak, fill(block, slabs[block], segments, keys, weights))

    peak = lax.fori_loop(0, blocks, prepare, jnp.zeros((1, wide), f32), unroll=4)

    @pl.when(jnp.logical_not(jnp.max(peak) * SCALE_T <= SAFE))
    def _():
        subtract_maxima(WT, blocks, count, pairs, keys, weights, causal, sums)

    def readable(block):
        return jnp.minimum(block, blocks - 1)

    def inverses(place):
        query, _, _ = read_pair(pairs, place)
        total = jnp.sum(sums[query], axis=0, keepdims=True) * math.sqrt(WS)
        return 1.0 / total, scales[readable(query), :1]

    def couple(place, teacher, student, scale):
        query, key, _ = read_pair(pairs, place)
        query_side = features[readable(query)]
        to_queries = jnp.zeros((WS, wide), f32)
        for low, high in halves(rows):
            coupling = student[low:high] * scale[1] - teacher[low:high] * scale[0]
            coupling = coupling.astype(bf16)
            key_side = features[readable(key), :, low:high]
            key_grad[key, :, low:high] += lax.dot_general(
                query_side, coupling, (((1,), (1,)), ((), ())), preferred_element_type=f32
            )
            to_queries += jnp.dot(key_side, coupling, preferred_element_type=f32)
        grad[query] += to_queries

    def half(turn, parity):
        slot = lax.rem(turn, AHEAD + 1)
        fetch(turn).wait()
        fetch(turn + AHEAD).start()
        scale = [inverses(UNROLL * turn + step) for step in range(UNROLL)]
        now = turn // 2 & 1
        before = (turn - LAG // UNROLL) // 2 & 1
        for step in range(UNROLL):
            place = UNROLL * turn + step
            old = rings[1 - parity].at[before, step]
            couple(place, old, fetched.at[slot, step], scale[step])
            target = rings[parity].at[now, step]
            weigh(place, blocks, pairs, keys, weights, SCALE_T, causal, target, sums)

    def steps(turn, carry):
        for parity in range(2):
            pl.when(turn & 1 == parity)(functools.partial(half, turn, parity))
        return carry

    turns = (count + LAG + UNROLL - 1) // UNROLL
    arrive.wait()
    lax.fori_loop(0, turns, steps, 0)
    for turn in range(AHEAD):
        fetch(turns + turn).wait()

    pieces = out_sems.shape[0]
    size = blocks // pieces

    def finish(block, carry):
        result[block] = (grad[block] + key_grad[block]).astype(bf16)
        return carry

    copies = []
    for piece in range(pieces):
        lax.fori_loop(piece * size, (piece + 1) * size, finish, 0, unroll=8)
        part = pl.ds(piece * size, size)
        copies.append(pltpu.make_async_copy(result.at[part], out.at[part], out_sems.at[piece]))
        copies[-1].start()
    for copy in copies:
        copy.wait()


def relation_gradient(slabs, segments, made, scales, features, pairs, count):
    blocks, _, wide = slabs.shape
    rows = made.shape[1]
    vmem = pl.BlockSpec(memory_space=pltpu.VMEM)
    smem = pl.BlockSpec(memory_space=pltpu.SMEM)
    hbm = pl.BlockSpec(memory_space=pl.ANY)
    slab = pltpu.VMEM((blocks, WS, wide), bf16)
    return pl.pallas_call(
        functools.partial(gradient_kernel, blocks),
        out_shape=jax.ShapeDtypeStruct((blocks, WS, wide), bf16),
        in_specs=[smem, smem, vmem, vmem, hbm, vmem, hbm],
        out_specs=hbm,
        scratch_shapes=[
            slab,
            slab,
            pltpu.VMEM((blocks, rows, DEPTH), bf16),
            pltpu.VMEM((blocks, DEPTH, wide), bf16),
            [pltpu.VMEM((2, UNROLL, rows, wide), f32)] * 2,
            pltpu.VMEM((AHEAD + 1, UNROLL, rows, wide), f32),
            pltpu.VMEM((2, rows, wide), f32),
            pltpu.VMEM((blocks + 1, 8, wide), f32),
            pltpu.VMEM((blocks + 1, WS, wide), f32),
            pltpu.VMEM((blocks + 1, WS, wide), f32),
            pltpu.SemaphoreType.DMA((AHEAD + 1,)),
            pltpu.SemaphoreType.DMA,
            pltpu.SemaphoreType.DMA((4,)),
        ],
        compiler_params=pltpu.CompilerParams(vmem_limit_bytes=48 * MIB),
        cost_estimate=pl.CostEstimate(
            flops=20_000_000_000, bytes_accessed=80_000_000, transcendentals=20_000_000
        ),
        name="relation_gradient",
    )(count, pairs, segments, slabs, made, scales, features)


def head_gradient(student, teacher, segment_ids, rows):
    blocks, _, wide = student.shape
    ends = jnp.stack([segment_ids[::rows], segment_ids[rows - 1 :: rows]])
    segments = jnp.pad(
        segment_ids.reshape(blocks, rows), ((0, 0), (0, wide - rows)), constant_values=-1
    )
    made, scales, features, pairs, count = student_weights(student, ends, segments, rows)
    return relation_gradient(teacher, segments, made, scales, features, pairs, count)


def unproject_kernel(grads, wq, wk, out):
    half = grads.shape[0] // 2
    rows, width = out.shape
    total = jnp.zeros((width, grads.shape[2]), f32)
    for rel, weight in enumerate((wq, wk)):
        turned = grads[rel * half : (rel + 1) * half].reshape(half * WS, grads.shape[2])
        total += jnp.dot(weight[...], turned, preferred_element_type=f32)
    out[...] = total.T[:rows].astype(out.dtype)


def unproject(grads, wq, wk, rows, dtype):
    width = wq.shape[0]
    vmem = pl.BlockSpec(memory_space=pltpu.VMEM)
    return pl.pallas_call(
        unproject_kernel,
        in_specs=[vmem, vmem, vmem],
        out_specs=vmem,
        out_shape=jax.ShapeDtypeStruct((rows, width), dtype),
        compiler_params=pltpu.CompilerParams(vmem_limit_bytes=32 * MIB),
        cost_estimate=pl.CostEstimate(
            flops=4 * rows * width * wq.shape[1], bytes_accessed=6_000_000, transcendentals=0
        ),
        name="unproject",
    )(grads, wq, wk)


def shards(teacher_query, teacher_key, student_hidden, w_query, w_key, segment_ids, block_mask):
    rows = student_hidden.shape[0]
    student = project(student_hidden, w_query, w_key, block_mask)
    teacher = turn(teacher_query, teacher_key)
    student = lax.all_to_all(student.reshape(-1, *student.shape[2:]), "ctx", 0, 0, tiled=True)
    teacher = lax.all_to_all(teacher.reshape(-1, *teacher.shape[2:]), "ctx", 0, 0, tiled=True)
    turned = head_gradient(student, teacher, segment_ids, rows)
    side = lax.axis_index("head")
    width = w_query.shape[0] // 2
    turned, side = lax.optimization_barrier((turned, side))
    cut = [
        [lax.dynamic_slice_in_dim(weight, part * width, width, 0) for weight in (w_query, w_key)]
        for part in (1 - side, side)
    ]
    cut = lax.optimization_barrier(cut)
    back = lax.all_to_all(turned, "ctx", 0, 0, tiled=True)
    away = unproject(back, *cut[0], rows, bf16)
    away = lax.ppermute(away, "head", [(0, 1), (1, 0)])
    own = unproject(back, *cut[1], rows, f32)
    return (own + away).astype(bf16)


def solution(mesh):
    placed = (
        P("ctx", "head"),
        P("ctx", "head"),
        P("ctx", None),
        P(None, "head"),
        P(None, "head"),
        P(),
        P("ctx", None),
    )
    return jax.shard_map(
        shards, mesh=mesh, in_specs=placed, out_specs=P("ctx", "head"), check_vma=False
    )
```

```python
import functools
import math

import jax
import jax.numpy as jnp
from jax import lax
from jax.experimental import pallas as pl
from jax.experimental.pallas import tpu as pltpu
from jax.sharding import PartitionSpec as P

DT = 5120
DS = 2048
HEADS = 64
REACH = 8
WT = DT // HEADS
WS = DS // HEADS
DEPTH = 128
EXTRA = 16
DOCS = 4
PACK = 8
LISTED = 8
UNROLL = 16
LAG = 3 * UNROLL
SLOTS = 4
AHEAD = 2
LIST = 640
HIDDEN = 1e30
SCALE_T = 1.0 / math.sqrt(WT)
SCALE_S = 1.0 / math.sqrt(WS)
SAFE = 60.0
MIB = 1024 * 1024
f32 = jnp.float32
bf16 = jnp.bfloat16


def round_up(value, unit):
    return (value + unit - 1) // unit * unit


def project_kernel(mask, hidden, wq, wk, out):
    rows, wide = hidden.shape[0], out.shape[-1]
    row = lax.broadcasted_iota(jnp.int32, (wide - rows, PACK * WS), 0)
    extra = jnp.zeros(row.shape, f32)
    for back in range(REACH - 1):
        extra = jnp.where(row == back, mask[0, back].astype(f32), extra)
    extra = extra.astype(bf16)
    for rel, weight in enumerate((wq, wk)):
        student = jnp.dot(hidden[...], weight[...], preferred_element_type=f32).astype(bf16)
        turned = jnp.concatenate([student, extra], axis=0).T
        out[rel] = turned.reshape(out.shape[1:])


def project(hidden, wq, wk, mask):
    rows = hidden.shape[0]
    wide = round_up(rows, 128)
    heads = wq.shape[1] // WS
    return pl.pallas_call(
        project_kernel,
        grid=(heads // PACK,),
        out_shape=jax.ShapeDtypeStruct((2, heads, WS, wide), bf16),
        in_specs=[
            pl.BlockSpec(memory_space=pltpu.SMEM),
            pl.BlockSpec((rows, DS), lambda i: (0, 0)),
            pl.BlockSpec((DS, PACK * WS), lambda i: (0, i)),
            pl.BlockSpec((DS, PACK * WS), lambda i: (0, i)),
        ],
        out_specs=pl.BlockSpec((2, PACK, WS, wide), lambda i: (0, i, 0, 0)),
        compiler_params=pltpu.CompilerParams(vmem_limit_bytes=56 * MIB),
        cost_estimate=pl.CostEstimate(
            flops=4 * rows * DS * heads * WS, bytes_accessed=10_000_000, transcendentals=0
        ),
        name="project_student",
    )(mask, hidden, wq, wk)


def turn_kernel(tq, tk, out):
    rows = tq.shape[0]
    wide = out.shape[-1]
    for rel, teacher in enumerate((tq, tk)):
        zeros = jnp.zeros((wide - rows, teacher.shape[1]), bf16)
        turned = jnp.concatenate([teacher[...], zeros], axis=0).T
        out[rel] = turned.reshape(out.shape[1:])


def turn(tq, tk):
    rows, columns = tq.shape
    wide = round_up(rows, 128)
    heads = columns // WT
    return pl.pallas_call(
        turn_kernel,
        grid=(heads // PACK,),
        out_shape=jax.ShapeDtypeStruct((2, heads, WT, wide), bf16),
        in_specs=[pl.BlockSpec((rows, PACK * WT), lambda i: (0, i))] * 2,
        out_specs=pl.BlockSpec((2, PACK, WT, wide), lambda i: (0, i, 0, 0)),
        compiler_params=pltpu.CompilerParams(vmem_limit_bytes=56 * MIB),
        cost_estimate=pl.CostEstimate(flops=0, bytes_accessed=5_000_000, transcendentals=0),
        name="turn_teacher",
    )(tq, tk)


def read_pair(pairs, place):
    code = pairs[place]
    return code & 255, (code >> 8) & 255, code >> 16


def fill(block, slab, segments, keys, weights):
    width, wide = slab.shape
    rows = keys.shape[1]
    row = lax.broadcasted_iota(jnp.int32, (EXTRA, wide), 0)
    lane = lax.broadcasted_iota(jnp.int32, (EXTRA, wide), 1)
    hot = jnp.where(row == segments[pl.ds(block, 1)], 1.0, 0.0)
    key_extra = jnp.where((row >= DOCS) & (row < DOCS + 3), 1.0, hot)
    query_extra = jnp.where((row < DOCS) & (lane < rows), (hot - 1.0) * HIDDEN, 0.0)
    zeros = jnp.zeros((DEPTH - EXTRA - width, wide), bf16)
    weights[block] = jnp.concatenate([slab, query_extra.astype(bf16), zeros], axis=0)
    keys[block] = jnp.concatenate([slab, key_extra.astype(bf16), zeros], axis=0).T[:rows]
    values = slab.astype(f32)
    return jnp.sum(values * values, axis=0, keepdims=True)


def subtract_maxima(width, blocks, count, pairs, keys, weights, causal, sums):
    rows, wide = causal.shape[1:]

    def raise_maxima(place, carry):
        query, key, diagonal = read_pair(pairs, place + LAG)
        scores = jnp.dot(keys[key], weights[query], preferred_element_type=f32)
        scores = scores + causal[diagonal]
        top = jnp.max(scores.reshape(rows // 8, 8, wide), axis=0)
        sums[query] = jnp.where(diagonal == 1, top, jnp.maximum(top, sums[query]))
        return carry

    lax.fori_loop(0, count, raise_maxima, 0)
    row = lax.broadcasted_iota(jnp.int32, (EXTRA, wide), 0)

    def set_maxima(block, carry):
        rest = jnp.max(sums[block], axis=0, keepdims=True)
        extra = weights[block, width : width + EXTRA].astype(f32)
        for part in range(3):
            piece = rest.astype(bf16).astype(f32)
            rest = rest - piece
            extra = jnp.where(row == DOCS + part, -piece, extra)
        weights[block, width : width + EXTRA] = extra.astype(bf16)
        return carry

    lax.fori_loop(0, blocks, set_maxima, 0)


def fill_causal(causal):
    shape = causal.shape[1:]
    key_at = lax.broadcasted_iota(jnp.int32, shape, 0)
    query_at = lax.broadcasted_iota(jnp.int32, shape, 1)
    causal[0] = jnp.zeros(shape, f32)
    causal[1] = jnp.where(key_at <= query_at, 0.0, -HIDDEN)


def halves(rows):
    return (0, 128), (128, rows)


def weigh(place, blocks, pairs, keys, weights, scale, causal, target, sums):
    query, key, diagonal = read_pair(pairs, place + LAG)
    rows, wide = causal.shape[1:]
    key_block = jnp.minimum(key, blocks - 1)
    operand = weights[jnp.minimum(query, blocks - 1)]
    part = jnp.where(diagonal == 1, 0.0, sums[query])
    for low, high in halves(rows):
        scores = jnp.dot(keys[key_block, low:high], operand, preferred_element_type=f32)
        made = jnp.exp(scores * scale + causal[diagonal, low:high])
        target[low:high] = made
        part += jnp.sum(made.reshape((high - low) // 8, 8, wide), axis=0)
    sums[query] = part


def student_kernel(
    blocks, ends, segments, slabs_in, made, scales, features_out, pairs, count_out, slabs, features, keys, weights, ring, causal, sums, seen, opened, sem, sems
):
    rows, wide = causal.shape[1:]
    arrive = pltpu.make_async_copy(slabs_in, slabs, sem)
    arrive.start()
    fill_causal(causal)
    arrive.wait()

    def look(block, carry):
        seen[pl.ds(block, 1)] = slabs[block, :16, wide - 128 :].astype(f32)[:1].astype(jnp.int32)
        return carry

    lax.fori_loop(0, blocks, look, 0, unroll=8)
    fetch = pltpu.make_async_copy(seen, opened, sem)
    fetch.start()
    fetch.wait()
    mask_lane = rows % 128

    def list_pairs(block, total):
        for back in range(REACH):
            key = jnp.maximum(block - back, 0)
            code = block | (key << 8)
            if back == 0:
                pairs[total + LAG] = code | (1 << 16)
                total = total + 1
            else:
                pairs[total + LAG] = code
                is_open = (block >= back) & (opened[block, mask_lane + back - 1] == 1)
                is_open = is_open & (ends[0, block] == ends[1, key])
                total = total + is_open.astype(jnp.int32)
        return total

    lane = lax.broadcasted_iota(jnp.int32, (WS, wide), 1)

    def prepare(block, carry):
        peak, total = carry
        total = list_pairs(block, total)
        slab = jnp.where(lane < rows, slabs[block].astype(f32), 0.0).astype(bf16)
        features[block] = slab
        return jnp.maximum(peak, fill(block, slab, segments, keys, weights)), total

    peak, count = lax.fori_loop(0, blocks, prepare, (jnp.zeros((1, wide), f32), 0), unroll=4)
    count_out[0] = count
    for place in range(LAG):
        pairs[place] = blocks | (blocks << 8)
    for place in range(LAG + UNROLL + LISTED):
        pairs[count + LAG + place] = blocks | (blocks << 8)

    @pl.when(jnp.logical_not(jnp.max(peak) * SCALE_S <= SAFE))
    def _():
        subtract_maxima(WS, blocks, count, pairs, keys, weights, causal, sums)

    leave = pltpu.make_async_copy(features, features_out, sem)
    leave.start()

    def send(turn):
        slot = turn & (SLOTS - 1)
        group = made.at[pl.ds(turn * LISTED, LISTED)]
        return pltpu.make_async_copy(ring.at[slot], group, sems.at[slot])

    def steps(turn, carry):
        slot = turn & (SLOTS - 1)

        @pl.when(turn >= SLOTS)
        def _():
            send(turn - SLOTS).wait()

        for step in range(LISTED):
            place = LISTED * turn + step
            target = ring.at[slot, step]
            weigh(place, blocks, pairs, keys, weights, SCALE_S, causal, target, sums)
        send(turn).start()
        return carry

    turns = (count + LISTED - 1) // LISTED
    lax.fori_loop(0, turns, steps, 0)

    def drain(turn, carry):
        send(turn).wait()
        return carry

    lax.fori_loop(jnp.maximum(turns - SLOTS, 0), turns, drain, 0)
    leave.wait()

    def finish(block, carry):
        total = jnp.sum(sums[block], axis=0, keepdims=True) * math.sqrt(WS)
        scales[block] = jnp.broadcast_to(1.0 / total, (8, wide))
        return carry

    lax.fori_loop(0, blocks, finish, 0, unroll=8)


def student_weights(slabs, ends, segments, rows):
    blocks, _, wide = slabs.shape
    vmem = pl.BlockSpec(memory_space=pltpu.VMEM)
    smem = pl.BlockSpec(memory_space=pltpu.SMEM)
    hbm = pl.BlockSpec(memory_space=pl.ANY)
    slab = pltpu.VMEM((blocks, WS, wide), bf16)
    return pl.pallas_call(
        functools.partial(student_kernel, blocks),
        out_shape=(
            jax.ShapeDtypeStruct((blocks * REACH, rows, wide), f32),
            jax.ShapeDtypeStruct((blocks, 8, wide), f32),
            jax.ShapeDtypeStruct((blocks, WS, wide), bf16),
            jax.ShapeDtypeStruct((LIST,), jnp.int32),
            jax.ShapeDtypeStruct((1,), jnp.int32),
        ),
        in_specs=[smem, vmem, hbm],
        out_specs=(hbm, vmem, hbm, smem, smem),
        scratch_shapes=[
            slab,
            slab,
            pltpu.VMEM((blocks, rows, DEPTH), bf16),
            pltpu.VMEM((blocks, DEPTH, wide), bf16),
            pltpu.VMEM((SLOTS, LISTED, rows, wide), f32),
            pltpu.VMEM((2, rows, wide), f32),
            pltpu.VMEM((blocks + 1, 8, wide), f32),
            pltpu.VMEM((blocks, 128), jnp.int32),
            pltpu.SMEM((blocks, 128), jnp.int32),
            pltpu.SemaphoreType.DMA,
            pltpu.SemaphoreType.DMA((SLOTS,)),
        ],
        compiler_params=pltpu.CompilerParams(vmem_limit_bytes=48 * MIB),
        cost_estimate=pl.CostEstimate(
            flops=10_000_000_000, bytes_accessed=80_000_000, transcendentals=20_000_000
        ),
        name="student_weights",
    )(ends, segments, slabs)


def gradient_kernel(
    blocks, count_in, pairs, segments, slabs, made, scales, features_in, out, features, result, keys, weights, rings, fetched, causal, sums, grad, key_grad, sems, sem, out_sems
):
    rows, wide = causal.shape[1:]
    count = count_in[0]
    arrive = pltpu.make_async_copy(features_in, features, sem)
    arrive.start()
    fill_causal(causal)

    def fetch(turn):
        group = jnp.clip(turn - LAG // UNROLL, 0, made.shape[0] // UNROLL - 1)
        slot = lax.rem(turn, AHEAD + 1)
        group = made.at[pl.ds(group * UNROLL, UNROLL)]
        return pltpu.make_async_copy(group, fetched.at[slot], sems.at[slot])

    for turn in range(AHEAD):
        fetch(turn).start()

    def prepare(block, peak):
        grad[block] = jnp.zeros((WS, wide), f32)
        key_grad[block] = jnp.zeros((WS, wide), f32)
        return jnp.maximum(peak, fill(block, slabs[block], segments, keys, weights))

    peak = lax.fori_loop(0, blocks, prepare, jnp.zeros((1, wide), f32), unroll=8)

    @pl.when(jnp.logical_not(jnp.max(peak) * SCALE_T <= SAFE))
    def _():
        subtract_maxima(WT, blocks, count, pairs, keys, weights, causal, sums)

    def readable(block):
        return jnp.minimum(block, blocks - 1)

    def inverses(place):
        query, _, _ = read_pair(pairs, place)
        total = jnp.sum(sums[query], axis=0, keepdims=True) * math.sqrt(WS)
        return 1.0 / total, scales[readable(query), :1]

    def couple(place, teacher, student, scale):
        query, key, _ = read_pair(pairs, place)
        query_side = features[readable(query)]
        to_queries = jnp.zeros((WS, wide), f32)
        for low, high in halves(rows):
            coupling = student[low:high] * scale[1] - teacher[low:high] * scale[0]
            coupling = coupling.astype(bf16)
            key_side = features[readable(key), :, low:high]
            key_grad[key, :, low:high] += lax.dot_general(
                query_side, coupling, (((1,), (1,)), ((), ())), preferred_element_type=f32
            )
            to_queries += jnp.dot(key_side, coupling, preferred_element_type=f32)
        grad[query] += to_queries

    def half(turn, parity):
        slot = lax.rem(turn, AHEAD + 1)
        fetch(turn).wait()
        fetch(turn + AHEAD).start()
        scale = [inverses(UNROLL * turn + step) for step in range(UNROLL)]
        now = turn // 2 & 1
        before = (turn - LAG // UNROLL) // 2 & 1
        for step in range(UNROLL):
            place = UNROLL * turn + step
            old = rings[1 - parity].at[before, step]
            couple(place, old, fetched.at[slot, step], scale[step])
            target = rings[parity].at[now, step]
            weigh(place, blocks, pairs, keys, weights, SCALE_T, causal, target, sums)

    def steps(turn, carry):
        for parity in range(2):
            pl.when(turn & 1 == parity)(functools.partial(half, turn, parity))
        return carry

    turns = (count + LAG + UNROLL - 1) // UNROLL
    arrive.wait()
    lax.fori_loop(0, turns, steps, 0)
    for turn in range(AHEAD):
        fetch(turns + turn).wait()

    pieces = out_sems.shape[0]
    size = blocks // pieces

    def finish(block, carry):
        result[block] = (grad[block] + key_grad[block]).astype(bf16)
        return carry

    copies = []
    for piece in range(pieces):
        lax.fori_loop(piece * size, (piece + 1) * size, finish, 0, unroll=8)
        part = pl.ds(piece * size, size)
        copies.append(pltpu.make_async_copy(result.at[part], out.at[part], out_sems.at[piece]))
        copies[-1].start()
    for copy in copies:
        copy.wait()


def relation_gradient(slabs, segments, made, scales, features, pairs, count):
    blocks, _, wide = slabs.shape
    rows = made.shape[1]
    vmem = pl.BlockSpec(memory_space=pltpu.VMEM)
    smem = pl.BlockSpec(memory_space=pltpu.SMEM)
    hbm = pl.BlockSpec(memory_space=pl.ANY)
    slab = pltpu.VMEM((blocks, WS, wide), bf16)
    return pl.pallas_call(
        functools.partial(gradient_kernel, blocks),
        out_shape=jax.ShapeDtypeStruct((blocks, WS, wide), bf16),
        in_specs=[smem, smem, vmem, vmem, hbm, vmem, hbm],
        out_specs=hbm,
        scratch_shapes=[
            slab,
            slab,
            pltpu.VMEM((blocks, rows, DEPTH), bf16),
            pltpu.VMEM((blocks, DEPTH, wide), bf16),
            [pltpu.VMEM((2, UNROLL, rows, wide), f32)] * 2,
            pltpu.VMEM((AHEAD + 1, UNROLL, rows, wide), f32),
            pltpu.VMEM((2, rows, wide), f32),
            pltpu.VMEM((blocks + 1, 8, wide), f32),
            pltpu.VMEM((blocks + 1, WS, wide), f32),
            pltpu.VMEM((blocks + 1, WS, wide), f32),
            pltpu.SemaphoreType.DMA((AHEAD + 1,)),
            pltpu.SemaphoreType.DMA,
            pltpu.SemaphoreType.DMA((4,)),
        ],
        compiler_params=pltpu.CompilerParams(vmem_limit_bytes=48 * MIB),
        cost_estimate=pl.CostEstimate(
            flops=20_000_000_000, bytes_accessed=80_000_000, transcendentals=20_000_000
        ),
        name="relation_gradient",
    )(count, pairs, segments, slabs, made, scales, features)


def head_gradient(student, teacher, segment_ids, rows):
    blocks, _, wide = student.shape
    ends = jnp.stack([segment_ids[::rows], segment_ids[rows - 1 :: rows]])
    segments = jnp.pad(
        segment_ids.reshape(blocks, rows), ((0, 0), (0, wide - rows)), constant_values=-1
    )
    made, scales, features, pairs, count = student_weights(student, ends, segments, rows)
    return relation_gradient(teacher, segments, made, scales, features, pairs, count)


def unproject_kernel(grads, wq, wk, out):
    half = grads.shape[0] // 2
    rows, width = out.shape
    total = jnp.zeros((width, grads.shape[2]), f32)
    for rel, weight in enumerate((wq, wk)):
        turned = grads[rel * half : (rel + 1) * half].reshape(half * WS, grads.shape[2])
        total += jnp.dot(weight[...], turned, preferred_element_type=f32)
    out[...] = total.T[:rows].astype(out.dtype)


def unproject(grads, wq, wk, rows, dtype):
    width = wq.shape[0]
    vmem = pl.BlockSpec(memory_space=pltpu.VMEM)
    return pl.pallas_call(
        unproject_kernel,
        in_specs=[vmem, vmem, vmem],
        out_specs=vmem,
        out_shape=jax.ShapeDtypeStruct((rows, width), dtype),
        compiler_params=pltpu.CompilerParams(vmem_limit_bytes=12 * MIB),
        cost_estimate=pl.CostEstimate(
            flops=4 * rows * width * wq.shape[1], bytes_accessed=6_000_000, transcendentals=0
        ),
        name="unproject",
    )(grads, wq, wk)


def shards(teacher_query, teacher_key, student_hidden, w_query, w_key, segment_ids, block_mask):
    rows = student_hidden.shape[0]
    student = project(student_hidden, w_query, w_key, block_mask)
    teacher = turn(teacher_query, teacher_key)
    student = lax.all_to_all(student.reshape(-1, *student.shape[2:]), "ctx", 0, 0, tiled=True)
    teacher = lax.all_to_all(teacher.reshape(-1, *teacher.shape[2:]), "ctx", 0, 0, tiled=True)
    turned = head_gradient(student, teacher, segment_ids, rows)
    side = lax.axis_index("head")
    width = w_query.shape[0] // 2
    turned, side = lax.optimization_barrier((turned, side))
    cut = [
        [lax.dynamic_slice_in_dim(weight, part * width, width, 0) for weight in (w_query, w_key)]
        for part in (1 - side, side)
    ]
    cut = lax.optimization_barrier(cut)
    back = lax.all_to_all(turned, "ctx", 0, 0, tiled=True)
    away = unproject(back, *cut[0], rows, bf16)
    away = lax.ppermute(away, "head", [(0, 1), (1, 0)])
    own = unproject(back, *cut[1], rows, f32)
    return (own + away).astype(bf16)


def solution(mesh):
    placed = (
        P("ctx", "head"),
        P("ctx", "head"),
        P("ctx", None),
        P(None, "head"),
        P(None, "head"),
        P(),
        P("ctx", None),
    )
    return jax.shard_map(
        shards, mesh=mesh, in_specs=placed, out_specs=P("ctx", "head"), check_vma=False
    )
```

```python
import functools
import math

import jax
import jax.numpy as jnp
from jax import lax
from jax.experimental import pallas as pl
from jax.experimental.pallas import tpu as pltpu
from jax.sharding import PartitionSpec as P

DT = 5120
DS = 2048
HEADS = 64
REACH = 8
WT = DT // HEADS
WS = DS // HEADS
DEPTH = 128
EXTRA = 16
DOCS = 4
PACK = 8
LISTED = 8
UNROLL = 16
LAG = 3 * UNROLL
SLOTS = 4
AHEAD = 2
LIST = 640
HIDDEN = 1e30
SCALE_T = 1.0 / math.sqrt(WT)
SCALE_S = 1.0 / math.sqrt(WS)
SAFE = 60.0
MIB = 1024 * 1024
f32 = jnp.float32
bf16 = jnp.bfloat16


def round_up(value, unit):
    return (value + unit - 1) // unit * unit


def project_kernel(mask, hidden, wq, wk, out):
    rows, wide = hidden.shape[0], out.shape[-1]
    row = lax.broadcasted_iota(jnp.int32, (wide - rows, PACK * WS), 0)
    extra = jnp.zeros(row.shape, f32)
    for back in range(REACH - 1):
        extra = jnp.where(row == back, mask[0, back].astype(f32), extra)
    extra = extra.astype(bf16)
    for rel, weight in enumerate((wq, wk)):
        student = jnp.dot(hidden[...], weight[...], preferred_element_type=f32).astype(bf16)
        turned = jnp.concatenate([student, extra], axis=0).T
        out[rel] = turned.reshape(out.shape[1:])


def project(hidden, wq, wk, mask):
    rows = hidden.shape[0]
    wide = round_up(rows, 128)
    heads = wq.shape[1] // WS
    return pl.pallas_call(
        project_kernel,
        grid=(heads // PACK,),
        out_shape=jax.ShapeDtypeStruct((2, heads, WS, wide), bf16),
        in_specs=[
            pl.BlockSpec(memory_space=pltpu.SMEM),
            pl.BlockSpec((rows, DS), lambda i: (0, 0)),
            pl.BlockSpec((DS, PACK * WS), lambda i: (0, i)),
            pl.BlockSpec((DS, PACK * WS), lambda i: (0, i)),
        ],
        out_specs=pl.BlockSpec((2, PACK, WS, wide), lambda i: (0, i, 0, 0)),
        compiler_params=pltpu.CompilerParams(vmem_limit_bytes=56 * MIB),
        cost_estimate=pl.CostEstimate(
            flops=4 * rows * DS * heads * WS, bytes_accessed=10_000_000, transcendentals=0
        ),
        name="project_student",
    )(mask, hidden, wq, wk)


def turn_kernel(tq, tk, out):
    rows = tq.shape[0]
    wide = out.shape[-1]
    for rel, teacher in enumerate((tq, tk)):
        zeros = jnp.zeros((wide - rows, teacher.shape[1]), bf16)
        turned = jnp.concatenate([teacher[...], zeros], axis=0).T
        out[rel] = turned.reshape(out.shape[1:])


def turn(tq, tk):
    rows, columns = tq.shape
    wide = round_up(rows, 128)
    heads = columns // WT
    return pl.pallas_call(
        turn_kernel,
        grid=(heads // PACK,),
        out_shape=jax.ShapeDtypeStruct((2, heads, WT, wide), bf16),
        in_specs=[pl.BlockSpec((rows, PACK * WT), lambda i: (0, i))] * 2,
        out_specs=pl.BlockSpec((2, PACK, WT, wide), lambda i: (0, i, 0, 0)),
        compiler_params=pltpu.CompilerParams(vmem_limit_bytes=56 * MIB),
        cost_estimate=pl.CostEstimate(flops=0, bytes_accessed=5_000_000, transcendentals=0),
        name="turn_teacher",
    )(tq, tk)


def read_pair(pairs, place):
    code = pairs[place]
    return code & 255, (code >> 8) & 255, code >> 16


def fill(block, slab, segments, keys, weights):
    width, wide = slab.shape
    rows = keys.shape[1]
    row = lax.broadcasted_iota(jnp.int32, (EXTRA, wide), 0)
    lane = lax.broadcasted_iota(jnp.int32, (EXTRA, wide), 1)
    hot = jnp.where(row == segments[pl.ds(block, 1)], 1.0, 0.0)
    key_extra = jnp.where((row >= DOCS) & (row < DOCS + 3), 1.0, hot)
    query_extra = jnp.where((row < DOCS) & (lane < rows), (hot - 1.0) * HIDDEN, 0.0)
    zeros = jnp.zeros((DEPTH - EXTRA - width, wide), bf16)
    weights[block] = jnp.concatenate([slab, query_extra.astype(bf16), zeros], axis=0)
    keys[block] = jnp.concatenate([slab, key_extra.astype(bf16), zeros], axis=0).T[:rows]
    values = slab.astype(f32)
    return jnp.sum(values * values, axis=0, keepdims=True)


def subtract_maxima(width, blocks, count, pairs, keys, weights, causal, sums):
    rows, wide = causal.shape[1:]

    def raise_maxima(place, carry):
        query, key, diagonal = read_pair(pairs, place + LAG)
        scores = jnp.dot(keys[key], weights[query], preferred_element_type=f32)
        scores = scores + causal[diagonal]
        top = jnp.max(scores.reshape(rows // 8, 8, wide), axis=0)
        sums[query] = jnp.where(diagonal == 1, top, jnp.maximum(top, sums[query]))
        return carry

    lax.fori_loop(0, count, raise_maxima, 0)
    row = lax.broadcasted_iota(jnp.int32, (EXTRA, wide), 0)

    def set_maxima(block, carry):
        rest = jnp.max(sums[block], axis=0, keepdims=True)
        extra = weights[block, width : width + EXTRA].astype(f32)
        for part in range(3):
            piece = rest.astype(bf16).astype(f32)
            rest = rest - piece
            extra = jnp.where(row == DOCS + part, -piece, extra)
        weights[block, width : width + EXTRA] = extra.astype(bf16)
        return carry

    lax.fori_loop(0, blocks, set_maxima, 0)


def fill_causal(causal):
    shape = causal.shape[1:]
    key_at = lax.broadcasted_iota(jnp.int32, shape, 0)
    query_at = lax.broadcasted_iota(jnp.int32, shape, 1)
    causal[0] = jnp.zeros(shape, f32)
    causal[1] = jnp.where(key_at <= query_at, 0.0, -HIDDEN)


def halves(rows):
    return (0, 128), (128, rows)


def weigh(place, blocks, pairs, keys, weights, scale, causal, target, sums):
    query, key, diagonal = read_pair(pairs, place + LAG)
    rows, wide = causal.shape[1:]
    key_block = jnp.minimum(key, blocks - 1)
    operand = weights[jnp.minimum(query, blocks - 1)]
    part = jnp.where(diagonal == 1, 0.0, sums[query])
    for low, high in ((0, rows),):
        scores = jnp.dot(keys[key_block, low:high], operand, preferred_element_type=f32)
        made = jnp.exp(scores * scale + causal[diagonal, low:high])
        target[low:high] = made
        part += jnp.sum(made.reshape((high - low) // 8, 8, wide), axis=0)
    sums[query] = part


def student_kernel(
    blocks, ends, segments, slabs_in, made, scales, features_out, pairs, count_out, slabs, features, keys, weights, ring, causal, sums, seen, opened, sem, sems
):
    rows, wide = causal.shape[1:]
    arrive = pltpu.make_async_copy(slabs_in, slabs, sem)
    arrive.start()
    fill_causal(causal)
    arrive.wait()

    def look(block, carry):
        seen[pl.ds(block, 1)] = slabs[block, :16, wide - 128 :].astype(f32)[:1].astype(jnp.int32)
        return carry

    lax.fori_loop(0, blocks, look, 0, unroll=8)
    fetch = pltpu.make_async_copy(seen, opened, sem)
    fetch.start()
    fetch.wait()
    mask_lane = rows % 128

    def list_pairs(block, total):
        for back in range(REACH):
            key = jnp.maximum(block - back, 0)
            code = block | (key << 8)
            if back == 0:
                pairs[total + LAG] = code | (1 << 16)
                total = total + 1
            else:
                pairs[total + LAG] = code
                is_open = (block >= back) & (opened[block, mask_lane + back - 1] == 1)
                is_open = is_open & (ends[0, block] == ends[1, key])
                total = total + is_open.astype(jnp.int32)
        return total

    lane = lax.broadcasted_iota(jnp.int32, (WS, wide), 1)

    def prepare(block, carry):
        peak, total = carry
        total = list_pairs(block, total)
        slab = jnp.where(lane < rows, slabs[block].astype(f32), 0.0).astype(bf16)
        features[block] = slab
        return jnp.maximum(peak, fill(block, slab, segments, keys, weights)), total

    peak, count = lax.fori_loop(0, blocks, prepare, (jnp.zeros((1, wide), f32), 0), unroll=4)
    count_out[0] = count
    for place in range(LAG):
        pairs[place] = blocks | (blocks << 8)
    for place in range(LAG + UNROLL + LISTED):
        pairs[count + LAG + place] = blocks | (blocks << 8)

    @pl.when(jnp.logical_not(jnp.max(peak) * SCALE_S <= SAFE))
    def _():
        subtract_maxima(WS, blocks, count, pairs, keys, weights, causal, sums)

    leave = pltpu.make_async_copy(features, features_out, sem)
    leave.start()

    def send(turn):
        slot = turn & (SLOTS - 1)
        group = made.at[pl.ds(turn * LISTED, LISTED)]
        return pltpu.make_async_copy(ring.at[slot], group, sems.at[slot])

    def steps(turn, carry):
        slot = turn & (SLOTS - 1)

        @pl.when(turn >= SLOTS)
        def _():
            send(turn - SLOTS).wait()

        for step in range(LISTED):
            place = LISTED * turn + step
            target = ring.at[slot, step]
            weigh(place, blocks, pairs, keys, weights, SCALE_S, causal, target, sums)
        send(turn).start()
        return carry

    turns = (count + LISTED - 1) // LISTED
    lax.fori_loop(0, turns, steps, 0)

    def drain(turn, carry):
        send(turn).wait()
        return carry

    lax.fori_loop(jnp.maximum(turns - SLOTS, 0), turns, drain, 0)
    leave.wait()

    def finish(block, carry):
        total = jnp.sum(sums[block], axis=0, keepdims=True) * math.sqrt(WS)
        scales[block] = jnp.broadcast_to(1.0 / total, (8, wide))
        return carry

    lax.fori_loop(0, blocks, finish, 0, unroll=8)


def student_weights(slabs, ends, segments, rows):
    blocks, _, wide = slabs.shape
    vmem = pl.BlockSpec(memory_space=pltpu.VMEM)
    smem = pl.BlockSpec(memory_space=pltpu.SMEM)
    hbm = pl.BlockSpec(memory_space=pl.ANY)
    slab = pltpu.VMEM((blocks, WS, wide), bf16)
    return pl.pallas_call(
        functools.partial(student_kernel, blocks),
        out_shape=(
            jax.ShapeDtypeStruct((blocks * REACH, rows, wide), f32),
            jax.ShapeDtypeStruct((blocks, 8, wide), f32),
            jax.ShapeDtypeStruct((blocks, WS, wide), bf16),
            jax.ShapeDtypeStruct((LIST,), jnp.int32),
            jax.ShapeDtypeStruct((1,), jnp.int32),
        ),
        in_specs=[smem, vmem, hbm],
        out_specs=(hbm, vmem, hbm, smem, smem),
        scratch_shapes=[
            slab,
            slab,
            pltpu.VMEM((blocks, rows, DEPTH), bf16),
            pltpu.VMEM((blocks, DEPTH, wide), bf16),
            pltpu.VMEM((SLOTS, LISTED, rows, wide), f32),
            pltpu.VMEM((2, rows, wide), f32),
            pltpu.VMEM((blocks + 1, 8, wide), f32),
            pltpu.VMEM((blocks, 128), jnp.int32),
            pltpu.SMEM((blocks, 128), jnp.int32),
            pltpu.SemaphoreType.DMA,
            pltpu.SemaphoreType.DMA((SLOTS,)),
        ],
        compiler_params=pltpu.CompilerParams(vmem_limit_bytes=48 * MIB),
        cost_estimate=pl.CostEstimate(
            flops=10_000_000_000, bytes_accessed=80_000_000, transcendentals=20_000_000
        ),
        name="student_weights",
    )(ends, segments, slabs)


def gradient_kernel(
    blocks, count_in, pairs, segments, slabs, made, scales, features_in, out, features, result, keys, weights, rings, fetched, causal, sums, grad, key_grad, sems, sem, out_sems
):
    rows, wide = causal.shape[1:]
    count = count_in[0]
    arrive = pltpu.make_async_copy(features_in, features, sem)
    arrive.start()
    fill_causal(causal)

    def fetch(turn):
        group = jnp.clip(turn - LAG // UNROLL, 0, made.shape[0] // UNROLL - 1)
        slot = lax.rem(turn, AHEAD + 1)
        group = made.at[pl.ds(group * UNROLL, UNROLL)]
        return pltpu.make_async_copy(group, fetched.at[slot], sems.at[slot])

    for turn in range(AHEAD):
        fetch(turn).start()

    def prepare(block, peak):
        grad[block] = jnp.zeros((WS, wide), f32)
        key_grad[block] = jnp.zeros((WS, wide), f32)
        return jnp.maximum(peak, fill(block, slabs[block], segments, keys, weights))

    peak = lax.fori_loop(0, blocks, prepare, jnp.zeros((1, wide), f32), unroll=4)

    @pl.when(jnp.logical_not(jnp.max(peak) * SCALE_T <= SAFE))
    def _():
        subtract_maxima(WT, blocks, count, pairs, keys, weights, causal, sums)

    def readable(block):
        return jnp.minimum(block, blocks - 1)

    def inverses(place):
        query, _, _ = read_pair(pairs, place)
        total = jnp.sum(sums[query], axis=0, keepdims=True) * math.sqrt(WS)
        return 1.0 / total, scales[readable(query), :1]

    def couple(place, teacher, student, scale):
        query, key, _ = read_pair(pairs, place)
        query_side = features[readable(query)]
        to_queries = jnp.zeros((WS, wide), f32)
        for low, high in halves(rows):
            coupling = student[low:high] * scale[1] - teacher[low:high] * scale[0]
            coupling = coupling.astype(bf16)
            key_side = features[readable(key), :, low:high]
            key_grad[key, :, low:high] += lax.dot_general(
                query_side, coupling, (((1,), (1,)), ((), ())), preferred_element_type=f32
            )
            to_queries += jnp.dot(key_side, coupling, preferred_element_type=f32)
        grad[query] += to_queries

    def half(turn, parity):
        slot = lax.rem(turn, AHEAD + 1)
        fetch(turn).wait()
        fetch(turn + AHEAD).start()
        scale = [inverses(UNROLL * turn + step) for step in range(UNROLL)]
        now = turn // 2 & 1
        before = (turn - LAG // UNROLL) // 2 & 1
        for step in range(UNROLL):
            place = UNROLL * turn + step
            old = rings[1 - parity].at[before, step]
            couple(place, old, fetched.at[slot, step], scale[step])
            target = rings[parity].at[now, step]
            weigh(place, blocks, pairs, keys, weights, SCALE_T, causal, target, sums)

    def steps(turn, carry):
        for parity in range(2):
            pl.when(turn & 1 == parity)(functools.partial(half, turn, parity))
        return carry

    turns = (count + LAG + UNROLL - 1) // UNROLL
    arrive.wait()
    lax.fori_loop(0, turns, steps, 0)
    for turn in range(AHEAD):
        fetch(turns + turn).wait()

    pieces = out_sems.shape[0]
    size = blocks // pieces

    def finish(block, carry):
        result[block] = (grad[block] + key_grad[block]).astype(bf16)
        return carry

    copies = []
    for piece in range(pieces):
        lax.fori_loop(piece * size, (piece + 1) * size, finish, 0, unroll=8)
        part = pl.ds(piece * size, size)
        copies.append(pltpu.make_async_copy(result.at[part], out.at[part], out_sems.at[piece]))
        copies[-1].start()
    for copy in copies:
        copy.wait()


def relation_gradient(slabs, segments, made, scales, features, pairs, count):
    blocks, _, wide = slabs.shape
    rows = made.shape[1]
    vmem = pl.BlockSpec(memory_space=pltpu.VMEM)
    smem = pl.BlockSpec(memory_space=pltpu.SMEM)
    hbm = pl.BlockSpec(memory_space=pl.ANY)
    slab = pltpu.VMEM((blocks, WS, wide), bf16)
    return pl.pallas_call(
        functools.partial(gradient_kernel, blocks),
        out_shape=jax.ShapeDtypeStruct((blocks, WS, wide), bf16),
        in_specs=[smem, smem, vmem, vmem, hbm, vmem, hbm],
        out_specs=hbm,
        scratch_shapes=[
            slab,
            slab,
            pltpu.VMEM((blocks, rows, DEPTH), bf16),
            pltpu.VMEM((blocks, DEPTH, wide), bf16),
            [pltpu.VMEM((2, UNROLL, rows, wide), f32)] * 2,
            pltpu.VMEM((AHEAD + 1, UNROLL, rows, wide), f32),
            pltpu.VMEM((2, rows, wide), f32),
            pltpu.VMEM((blocks + 1, 8, wide), f32),
            pltpu.VMEM((blocks + 1, WS, wide), f32),
            pltpu.VMEM((blocks + 1, WS, wide), f32),
            pltpu.SemaphoreType.DMA((AHEAD + 1,)),
            pltpu.SemaphoreType.DMA,
            pltpu.SemaphoreType.DMA((4,)),
        ],
        compiler_params=pltpu.CompilerParams(vmem_limit_bytes=48 * MIB),
        cost_estimate=pl.CostEstimate(
            flops=20_000_000_000, bytes_accessed=80_000_000, transcendentals=20_000_000
        ),
        name="relation_gradient",
    )(count, pairs, segments, slabs, made, scales, features)


def head_gradient(student, teacher, segment_ids, rows):
    blocks, _, wide = student.shape
    ends = jnp.stack([segment_ids[::rows], segment_ids[rows - 1 :: rows]])
    segments = jnp.pad(
        segment_ids.reshape(blocks, rows), ((0, 0), (0, wide - rows)), constant_values=-1
    )
    made, scales, features, pairs, count = student_weights(student, ends, segments, rows)
    return relation_gradient(teacher, segments, made, scales, features, pairs, count)


def unproject_kernel(grads, wq, wk, out):
    half = grads.shape[0] // 2
    rows, width = out.shape
    total = jnp.zeros((width, grads.shape[2]), f32)
    for rel, weight in enumerate((wq, wk)):
        turned = grads[rel * half : (rel + 1) * half].reshape(half * WS, grads.shape[2])
        total += jnp.dot(weight[...], turned, preferred_element_type=f32)
    out[...] = total.T[:rows].astype(out.dtype)


def unproject(grads, wq, wk, rows, dtype):
    width = wq.shape[0]
    vmem = pl.BlockSpec(memory_space=pltpu.VMEM)
    return pl.pallas_call(
        unproject_kernel,
        in_specs=[vmem, vmem, vmem],
        out_specs=vmem,
        out_shape=jax.ShapeDtypeStruct((rows, width), dtype),
        compiler_params=pltpu.CompilerParams(vmem_limit_bytes=32 * MIB),
        cost_estimate=pl.CostEstimate(
            flops=4 * rows * width * wq.shape[1], bytes_accessed=6_000_000, transcendentals=0
        ),
        name="unproject",
    )(grads, wq, wk)


def shards(teacher_query, teacher_key, student_hidden, w_query, w_key, segment_ids, block_mask):
    rows = student_hidden.shape[0]
    student = project(student_hidden, w_query, w_key, block_mask)
    teacher = turn(teacher_query, teacher_key)
    student = lax.all_to_all(student.reshape(-1, *student.shape[2:]), "ctx", 0, 0, tiled=True)
    teacher = lax.all_to_all(teacher.reshape(-1, *teacher.shape[2:]), "ctx", 0, 0, tiled=True)
    turned = head_gradient(student, teacher, segment_ids, rows)
    side = lax.axis_index("head")
    width = w_query.shape[0] // 2
    turned, side = lax.optimization_barrier((turned, side))
    cut = [
        [lax.dynamic_slice_in_dim(weight, part * width, width, 0) for weight in (w_query, w_key)]
        for part in (1 - side, side)
    ]
    cut = lax.optimization_barrier(cut)
    back = lax.all_to_all(turned, "ctx", 0, 0, tiled=True)
    away = unproject(back, *cut[0], rows, bf16)
    away = lax.ppermute(away, "head", [(0, 1), (1, 0)])
    own = unproject(back, *cut[1], rows, f32)
    return (own + away).astype(bf16)


def solution(mesh):
    placed = (
        P("ctx", "head"),
        P("ctx", "head"),
        P("ctx", None),
        P(None, "head"),
        P(None, "head"),
        P(),
        P("ctx", None),
    )
    return jax.shard_map(
        shards, mesh=mesh, in_specs=placed, out_specs=P("ctx", "head"), check_vma=False
    )
```
